256 devices in a mesh: ctx: 128 (over z, y_lo, x, core), tp: 2 (over y_hi).
Axes of the slice: x: 4, y: 4 (y_hi: 2, y_lo: 2; y = y_hi * 2 + y_lo), z: 8, core: 2. Of those that a mesh axis runs over, the one named last changes fastest.
Arguments:
- queries: bfloat16 [24576, 2048], P('ctx', 'tp'), may hold values from -9 to 9
- keys: bfloat16 [24576, 2048], P('ctx', 'tp'), may hold values from -9 to 9
- values: bfloat16 [24576, 2048], P('ctx', 'tp'), may hold values from -6 to 6
- stream_grad: bfloat16 [24576, 2048], P('ctx', 'tp'), may hold values from -6 to 6
- conv_input: bfloat16 [24576, 2048], P('ctx', 'tp'), may hold values from -6 to 6
- conv_weight: bfloat16 [31, 2048], P(None, 'tp'), may hold values from -1 to 1
- out_weight: bfloat16 [2048, 2048], P('tp'), may hold values from -0.125 to 0.125
Outputs:
- query_grad: bfloat16 [24576, 2048], P('ctx', 'tp')
- key_grad: bfloat16 [24576, 2048], P('ctx', 'tp')
- value_grad: bfloat16 [24576, 2048], P('ctx', 'tp')
- grad_stream: bfloat16 [24576, 2048], P('ctx', 'tp')
- kernel_grad: float32 [31, 2048], P(None, 'tp')
The draws below stay inside these ranges and needn't reach their ends.
All inputs are finite; a program needn't handle non-finite values.
Results may differ from the reference program's by a relative error of at most 0.012.
The reference program's roundings to bfloat16 on the way count: a program that leaves them out, or rounds other values in their place, can miss the bound.
Values may be sent and summed in bfloat16 or wider, within the bound.
No kernel may reach another device: no remote copies, remote signals or barrier semaphores. Data moves between devices by JAX's collectives and lax.ppermute only.
A program may use at most 64 MiB of HBM per device.

```python
import math
import jax
import jax.numpy as jnp
from jax import lax

D = 2048
HEADS = 16
HEAD = 128
KERNEL = 31
FRAMES_DEV = 192
FRAMES = 24576


def draw_queries(key, part):
    key = jax.random.fold_in(key, 1)
    result = jnp.clip(jax.random.normal(key, (FRAMES, D), jnp.float32), -6.0, 6.0)
    return result.astype(jnp.bfloat16)


def draw_keys(key, part):
    key = jax.random.fold_in(key, 2)
    result = jnp.clip(jax.random.normal(key, (FRAMES, D), jnp.float32), -6.0, 6.0)
    return result.astype(jnp.bfloat16)


def steps_of(rng, extent, shards, smallest, high):
    level, own = 1.0, jax.random.fold_in(rng, 6)
    for dim, blocks in shards:
        draws = jnp.exp(jax.random.uniform(jax.random.fold_in(own, dim), (blocks,), jnp.float32, smallest / len(shards), high / len(shards)))
        level = level * jnp.repeat(draws, extent[dim] // blocks).reshape([-1 if axis == dim else 1 for axis in range(len(extent))])
    return level


def gaussian(own_key, dims, spread, most, shards=(), kind=jnp.bfloat16):
    values = spread * jax.random.normal(own_key, dims, jnp.float32)
    if shards:
        values = values * steps_of(own_key, dims, shards, -0.22, 0.18)
    return jnp.clip(values, -most, most).astype(kind)


def setup_inputs(seed: int = 0) -> dict:
    seeds = jax.random.split(jax.random.key(seed), 8)
    return {
        "queries": draw_queries(jax.random.fold_in(seeds[7], 71), 0),
        "keys": draw_keys(jax.random.fold_in(seeds[7], 71), 0),
        "values": gaussian(seeds[2], (FRAMES, D), 1.0, 6.0, ((0, 128), (1, 2))),
        "stream_grad": gaussian(seeds[3], (FRAMES, D), 1.0, 6.0, ((0, 128), (1, 2))),
        "conv_input": gaussian(seeds[4], (FRAMES, D), 1.0, 6.0, ((0, 128), (1, 2))),
        "conv_weight": gaussian(seeds[5], (KERNEL, D), KERNEL ** -0.5, 1.0, ((1, 2),)),
        "out_weight": gaussian(seeds[6], (D, D), D ** -0.5, 0.125, ((0, 2),)),
    }


def head_grads(qh, kh, vh, doh, valid, scale):
    contract_last = (((1,), (1,)), ((), ()))
    contract_first = (((0,), (0,)), ((), ()))
    scores = lax.dot_general(qh, kh, contract_last, preferred_element_type=jnp.float32) * scale
    scores = jnp.where(valid, scores, -jnp.inf)
    top = lax.optimization_barrier(jnp.max(scores, axis=1, keepdims=True))
    expo = jnp.exp(scores - top)
    probs = expo / lax.optimization_barrier(jnp.sum(expo, axis=1, keepdims=True))
    probs_low = probs.astype(jnp.bfloat16)
    attn_out = jnp.dot(probs_low, vh, preferred_element_type=jnp.float32)
    delta = lax.optimization_barrier(jnp.sum(doh.astype(jnp.float32) * attn_out, axis=1, keepdims=True))
    prob_grad = lax.dot_general(doh, vh, contract_last, preferred_element_type=jnp.float32)
    score_grad = (probs * (prob_grad - delta)).astype(jnp.bfloat16)
    query_part = jnp.dot(score_grad, kh, preferred_element_type=jnp.float32) * scale
    key_part = lax.dot_general(score_grad, qh, contract_first, preferred_element_type=jnp.float32) * scale
    value_part = lax.dot_general(probs_low, doh, contract_first, preferred_element_type=jnp.float32)
    return (query_part, key_part, value_part)

def reference(queries, keys, values, stream_grad, conv_input, conv_weight, out_weight):
    reach = KERNEL // 2
    grad_f = stream_grad.astype(jnp.float32)
    input_f = conv_input.astype(jnp.float32)
    taps = conv_weight.astype(jnp.float32)
    grad_pad = jnp.pad(grad_f, ((reach, reach), (0, 0)))
    input_pad = jnp.pad(input_f, ((reach, reach), (0, 0)))
    conv_back = jnp.zeros_like(grad_f)
    tap_rows = []
    for tap in range(KERNEL):
        conv_back = conv_back + taps[tap] * grad_pad[2 * reach - tap:2 * reach - tap + FRAMES]
        tap_rows.append(lax.optimization_barrier(jnp.sum(grad_f * input_pad[tap:tap + FRAMES], axis=0)))
    kernel_grad = jnp.stack(tap_rows) / math.sqrt(FRAMES)
    grad_stream = (grad_f + conv_back).astype(jnp.bfloat16)
    out_grad = lax.dot_general(grad_stream, out_weight, (((1,), (1,)), ((), ())), preferred_element_type=jnp.float32).astype(jnp.bfloat16)
    block = FRAMES_DEV
    front = jnp.zeros((3 * block, D), jnp.bfloat16)
    keys_pad = jnp.concatenate([front, keys], axis=0)
    values_pad = jnp.concatenate([front, values], axis=0)
    rows = jnp.arange(block, dtype=jnp.int32)[:, None]
    cols = jnp.arange(4 * block, dtype=jnp.int32)[None, :]
    scale = 1.0 / math.sqrt(HEAD)

    def step(carry, index):
        key_acc, value_acc = carry
        start = (index * block).astype(jnp.int32)
        q_block = lax.dynamic_slice_in_dim(queries, start, block, 0)
        do_block = lax.dynamic_slice_in_dim(out_grad, start, block, 0)
        k_block = lax.dynamic_slice_in_dim(keys_pad, start, 4 * block, 0)
        v_block = lax.dynamic_slice_in_dim(values_pad, start, 4 * block, 0)
        valid = (cols <= 3 * block + rows) & (cols >= (3 - index) * block)
        query_parts, key_parts, value_parts = ([], [], [])
        for head in range(HEADS):
            lo, hi = (head * HEAD, (head + 1) * HEAD)
            qp, kp, vp = head_grads(q_block[:, lo:hi], k_block[:, lo:hi], v_block[:, lo:hi], do_block[:, lo:hi], valid, scale)
            query_parts.append(qp)
            key_parts.append(kp)
            value_parts.append(vp)
        key_term = jnp.concatenate(key_parts, axis=1).astype(jnp.bfloat16).astype(jnp.float32)
        value_term = jnp.concatenate(value_parts, axis=1).astype(jnp.bfloat16).astype(jnp.float32)
        key_acc = lax.dynamic_update_slice_in_dim(key_acc, lax.dynamic_slice_in_dim(key_acc, start, 4 * block, 0) + key_term, start, 0)
        value_acc = lax.dynamic_update_slice_in_dim(value_acc, lax.dynamic_slice_in_dim(value_acc, start, 4 * block, 0) + value_term, start, 0)
        return ((key_acc, value_acc), jnp.concatenate(query_parts, axis=1).astype(jnp.bfloat16))
    zeros = jnp.zeros((FRAMES + 3 * block, D), jnp.float32)
    (key_acc, value_acc), query_blocks = lax.scan(step, (zeros, zeros), jnp.arange(FRAMES // block, dtype=jnp.int32))
    query_grad = query_blocks.reshape(FRAMES, D)
    key_grad = key_acc[3 * block:].astype(jnp.bfloat16)
    value_grad = value_acc[3 * block:].astype(jnp.bfloat16)
    return (query_grad, key_grad, value_grad, grad_stream, kernel_grad)
```

```python
import math

import jax
import jax.numpy as jnp
from jax import lax
from jax.sharding import PartitionSpec as P

HEAD = 128


def with_halo(block, sides, width):
    for axis, dim in sides:
        count = lax.axis_size(axis)
        forward = [(i, i + 1) for i in range(count - 1)]
        backward = [(target, source) for source, target in forward]
        low = lax.ppermute(
            lax.slice_in_dim(block, block.shape[dim] - width, None, axis=dim), axis, forward
        )
        high = lax.ppermute(lax.slice_in_dim(block, 0, width, axis=dim), axis, backward)
        block = jnp.concatenate([low, block, high], axis=dim)
    return block


def shifted(shard, axis, by):
    count = lax.axis_size(axis)
    pairs = [(i, i + by) for i in range(count) if 0 <= i + by < count]
    return lax.ppermute(shard, axis, pairs)


def exchanged(part, by):
    count = lax.axis_size("ctx")
    return lax.ppermute(part, "ctx", [(i, i ^ by) for i in range(count)])


def summed(part):
    part = part + exchanged(part, 1)
    for low in (2, 8, 32):
        one, two, three = (exchanged(part, low * k) for k in (1, 2, 3))
        part = (part + one) + (two + three)
    return part


def head_grads(qh, kh, vh, doh, valid, scale):
    contract_last = (((1,), (1,)), ((), ()))
    contract_first = (((0,), (0,)), ((), ()))
    scores = lax.dot_general(qh, kh, contract_last, preferred_element_type=jnp.float32) * scale
    scores = jnp.where(valid, scores, -jnp.inf)
    top = jnp.max(scores, axis=1, keepdims=True)
    expo = jnp.exp(scores - top)
    probs = expo / jnp.sum(expo, axis=1, keepdims=True)
    probs_low = probs.astype(jnp.bfloat16)
    attn_out = jnp.dot(probs_low, vh, preferred_element_type=jnp.float32)
    delta = jnp.sum(doh.astype(jnp.float32) * attn_out, axis=1, keepdims=True)
    prob_grad = lax.dot_general(doh, vh, contract_last, preferred_element_type=jnp.float32)
    score_grad = (probs * (prob_grad - delta)).astype(jnp.bfloat16)
    query_part = jnp.dot(score_grad, kh, preferred_element_type=jnp.float32) * scale
    key_part = (
        lax.dot_general(score_grad, qh, contract_first, preferred_element_type=jnp.float32) * scale
    )
    value_part = lax.dot_general(probs_low, doh, contract_first, preferred_element_type=jnp.float32)
    return (query_part, key_part, value_part)


def per_device(queries, keys, values, stream_grad, conv_input, conv_weight, out_weight):
    block = queries.shape[0]
    width = queries.shape[1]
    taps_count = conv_weight.shape[0]
    reach = taps_count // 2
    device = lax.axis_index("ctx")
    stacked = jnp.stack([conv_input, stream_grad])
    padded = with_halo(stacked, (("ctx", 1),), reach)
    input_pad = padded[0].astype(jnp.float32)
    grad_pad = padded[1].astype(jnp.float32)
    grad_f = stream_grad.astype(jnp.float32)
    taps = conv_weight.astype(jnp.float32)
    conv_back = jnp.zeros_like(grad_f)
    tap_rows = []
    for tap in range(taps_count):
        conv_back = conv_back + taps[tap] * grad_pad[2 * reach - tap : 2 * reach - tap + block]
        tap_rows.append(jnp.sum(grad_f * input_pad[tap : tap + block], axis=0))
    total_frames = block * lax.axis_size("ctx")
    kernel_grad = summed(jnp.stack(tap_rows)) / math.sqrt(total_frames)
    grad_stream = (grad_f + conv_back).astype(jnp.bfloat16)
    full_stream = lax.all_gather(grad_stream, "tp", axis=1, tiled=True)
    out_grad = lax.dot_general(
        full_stream, out_weight, (((1,), (1,)), ((), ())), preferred_element_type=jnp.float32
    ).astype(jnp.bfloat16)
    pair = jnp.stack([keys, values])
    earlier = [pair]
    moving = pair
    for hop in range(3):
        moving = shifted(moving, "ctx", 1)
        earlier.append(moving)
    window = jnp.concatenate(earlier[::-1], axis=1)
    rows = jnp.arange(block, dtype=jnp.int32)[:, None]
    cols = jnp.arange(4 * block, dtype=jnp.int32)[None, :]
    valid = (cols <= 3 * block + rows) & (cols >= (3 - device) * block)
    scale = 1.0 / math.sqrt(HEAD)
    query_parts, key_parts, value_parts = ([], [], [])
    for head in range(width // HEAD):
        lo, hi = (head * HEAD, (head + 1) * HEAD)
        qp, kp, vp = head_grads(
            queries[:, lo:hi],
            window[0][:, lo:hi],
            window[1][:, lo:hi],
            out_grad[:, lo:hi],
            valid,
            scale,
        )
        query_parts.append(qp)
        key_parts.append(kp)
        value_parts.append(vp)
    query_grad = jnp.concatenate(query_parts, axis=1).astype(jnp.bfloat16)
    terms = jnp.stack(
        [jnp.concatenate(key_parts, axis=1), jnp.concatenate(value_parts, axis=1)]
    ).astype(jnp.bfloat16)
    total = terms[:, 3 * block :].astype(jnp.float32)
    bundle = terms[:, : 3 * block]
    for hop in range(3):
        arrived = shifted(bundle, "ctx", -1)
        total = total + arrived[:, arrived.shape[1] - block :].astype(jnp.float32)
        bundle = arrived[:, : arrived.shape[1] - block]
    key_grad = total[0].astype(jnp.bfloat16)
    value_grad = total[1].astype(jnp.bfloat16)
    return (query_grad, key_grad, value_grad, grad_stream, kernel_grad)


def solution(mesh):
    return jax.shard_map(
        per_device,
        mesh=mesh,
        in_specs=(
            P("ctx", "tp"),
            P("ctx", "tp"),
            P("ctx", "tp"),
            P("ctx", "tp"),
            P("ctx", "tp"),
            P(None, "tp"),
            P("tp", None),
        ),
        out_specs=(P("ctx", "tp"), P("ctx", "tp"), P("ctx", "tp"), P("ctx", "tp"), P(None, "tp")),
        check_vma=False,
    )
```

```python
import functools
import math

import jax
import jax.numpy as jnp
from jax import lax
from jax.experimental import pallas as pl
from jax.experimental.pallas import tpu as pltpu
from jax.sharding import PartitionSpec as P

HEAD = 128
EDGE = 16
NT = (((1,), (1,)), ((), ()))
BIG = 1e30


def rotated(part, by):
    count = lax.axis_size("ctx")
    return lax.ppermute(part, "ctx", [(i, (i + by) % count) for i in range(count)])


def exchanged(part, by):
    count = lax.axis_size("ctx")
    return lax.ppermute(part, "ctx", [(i, i ^ by) for i in range(count)])


def summed(part):
    part = part + exchanged(part, 1)
    for low in (2, 8, 32):
        one, two, three = (exchanged(part, low * k) for k in (1, 2, 3))
        part = (part + one) + (two + three)
    return part


def conv_kernel(last, idx_ref, grad_ref, input_ref, low_ref, high_ref, taps_ref, out_ref, rows_ref, gpad, cpad):
    block = grad_ref.shape[0]
    taps_count = taps_ref.shape[0]
    reach = taps_count // 2
    device = idx_ref[0]
    f32 = jnp.float32
    low = jnp.where(device > 0, low_ref[...].astype(f32), 0.0)
    high = jnp.where(device < last, high_ref[...].astype(f32), 0.0)
    grad = grad_ref[...].astype(f32)
    cpad[:EDGE] = low[:EDGE]
    gpad[:EDGE] = low[EDGE:]
    cpad[EDGE : EDGE + block] = input_ref[...].astype(f32)
    gpad[EDGE : EDGE + block] = grad
    cpad[EDGE + block :] = high[:EDGE]
    gpad[EDGE + block :] = high[EDGE:]
    taps = taps_ref[...].astype(f32)
    total = jnp.zeros_like(grad)
    for tap in range(taps_count):
        total = total + taps[tap : tap + 1] * gpad[pl.ds(EDGE + reach - tap, block), :]
    out_ref[...] = (grad + total).astype(out_ref.dtype)
    for tap in range(taps_count):
        prod = grad * cpad[pl.ds(EDGE - reach + tap, block), :]
        rows_ref[tap : tap + 1, :] = jnp.sum(prod, axis=0, keepdims=True)


def conv(device, grad, inputs, low, high, taps, last):
    block, width = grad.shape
    count = taps.shape[0]
    lanes = 128
    column = lambda rows: pl.BlockSpec((rows, lanes), lambda c: (0, c))
    return pl.pallas_call(
        functools.partial(conv_kernel, last),
        grid=(width // lanes,),
        in_specs=[
            pl.BlockSpec(memory_space=pltpu.SMEM),
            column(block),
            column(block),
            column(2 * EDGE),
            column(2 * EDGE),
            column(count),
        ],
        out_specs=[column(block), column(count)],
        out_shape=[
            jax.ShapeDtypeStruct((block, width), jnp.bfloat16),
            jax.ShapeDtypeStruct((count, width), jnp.float32),
        ],
        scratch_shapes=[
            pltpu.VMEM((block + 2 * EDGE, lanes), jnp.float32),
            pltpu.VMEM((block + 2 * EDGE, lanes), jnp.float32),
        ],
        compiler_params=pltpu.CompilerParams(vmem_limit_bytes=8 * 2**20),
        cost_estimate=pl.CostEstimate(flops=8 * block * width * count, bytes_accessed=4 * block * width, transcendentals=0),
    )(device, grad, inputs, low, high, taps)


def project_kernel(idx_ref, own_ref, other_ref, weight_ref, out_ref):
    half = own_ref.shape[1]
    tp = idx_ref[0]
    first = weight_ref[:, pl.ds(pl.multiple_of(tp * half, half), half)]
    second = weight_ref[:, pl.ds(pl.multiple_of((1 - tp) * half, half), half)]
    total = lax.dot_general(own_ref[...], first, NT, preferred_element_type=jnp.float32)
    total = total + lax.dot_general(other_ref[...], second, NT, preferred_element_type=jnp.float32)
    out_ref[...] = total.astype(out_ref.dtype)


def project(tp, own, other, weight):
    block, half = own.shape
    rows, full = weight.shape
    step = 256
    return pl.pallas_call(
        project_kernel,
        grid=(rows // step,),
        in_specs=[
            pl.BlockSpec(memory_space=pltpu.SMEM),
            pl.BlockSpec((block, half), lambda n: (0, 0)),
            pl.BlockSpec((block, half), lambda n: (0, 0)),
            pl.BlockSpec((step, full), lambda n: (n, 0)),
        ],
        out_specs=pl.BlockSpec((block, step), lambda n: (0, n)),
        out_shape=jax.ShapeDtypeStruct((block, rows), jnp.bfloat16),
        compiler_params=pltpu.CompilerParams(vmem_limit_bytes=16 * 2**20),
        cost_estimate=pl.CostEstimate(flops=2 * block * rows * full, bytes_accessed=2 * rows * full, transcendentals=0),
    )(tp, own, other, weight)


def query_kernel(scale, idx_ref, q_ref, do_ref, k3, k2, k1, k0, v3, v2, v1, v0, out_ref, stats_ref, bias, columns):
    head = pl.program_id(0)
    heads = pl.num_programs(0)
    block = q_ref.shape[0]
    f32 = jnp.float32

    @pl.when(head == 0)
    def _():
        rows = lax.broadcasted_iota(jnp.int32, bias.shape, 0)
        cols = lax.broadcasted_iota(jnp.int32, bias.shape, 1)
        valid = (cols <= 3 * block + rows) & (cols >= (3 - idx_ref[0]) * block)
        bias[...] = jnp.where(valid, 0.0, -jnp.inf)
        columns[...] = jnp.zeros_like(columns)

    keys = jnp.concatenate([k3[...], k2[...], k1[...], k0[...]], axis=0)
    values = jnp.concatenate([v3[...], v2[...], v1[...], v0[...]], axis=0)
    do = do_ref[...]
    scores = lax.dot_general(q_ref[...], keys, NT, preferred_element_type=f32) * scale + bias[...]
    top = jnp.max(scores, axis=1, keepdims=True)
    expo = jnp.exp(scores - top)
    denom = jnp.sum(expo, axis=1, keepdims=True)
    probs = expo * (1.0 / denom)
    prob_grad = lax.dot_general(do, values, NT, preferred_element_type=f32)
    delta = jnp.sum(probs.astype(jnp.bfloat16).astype(f32) * prob_grad, axis=1, keepdims=True)
    score_grad = (probs * (prob_grad - delta)).astype(jnp.bfloat16)
    out = jnp.dot(score_grad, keys, preferred_element_type=f32) * scale
    out_ref[...] = out.astype(out_ref.dtype)
    lane = lax.broadcasted_iota(jnp.int32, columns.shape, 1)
    both = jnp.where(lane == head, top + jnp.log(denom), columns[...])
    columns[...] = jnp.where(lane == heads + head, delta, both)

    @pl.when(head == heads - 1)
    def _():
        stats_ref[...] = columns[...].T[: stats_ref.shape[0]]


def query_side(device, queries, out_grad, keys, values, scale):
    block, width = queries.shape
    heads = width // HEAD
    column = pl.BlockSpec((block, HEAD), lambda h: (0, h))
    return pl.pallas_call(
        functools.partial(query_kernel, scale),
        grid=(heads,),
        in_specs=[pl.BlockSpec(memory_space=pltpu.SMEM)] + [column] * 10,
        out_specs=[column, pl.BlockSpec((2 * heads, block), lambda h: (0, 0))],
        out_shape=[
            jax.ShapeDtypeStruct((block, width), jnp.bfloat16),
            jax.ShapeDtypeStruct((2 * heads, block), jnp.float32),
        ],
        scratch_shapes=[
            pltpu.VMEM((block, 4 * block), jnp.float32),
            pltpu.VMEM((block, HEAD), jnp.float32),
        ],
        compiler_params=pltpu.CompilerParams(vmem_limit_bytes=24 * 2**20),
        cost_estimate=pl.CostEstimate(
            flops=40 * block * block * width, bytes_accessed=24 * block * width, transcendentals=4 * block * block * heads
        ),
    )(device, queries, out_grad, *keys, *values)


def key_kernel(scale, last, idx_ref, k_ref, v_ref, q0, q1, q2, q3, d0, d1, d2, d3, s0, s1, s2, s3, dk_ref, dv_ref, bias, lse, delta):
    head = pl.program_id(0)
    heads = pl.num_programs(0)
    block = k_ref.shape[0]
    f32 = jnp.float32
    device = idx_ref[0]

    @pl.when(head == 0)
    def _():
        rows = lax.broadcasted_iota(jnp.int32, bias.shape, 0)
        cols = lax.broadcasted_iota(jnp.int32, bias.shape, 1)
        bias[...] = jnp.where(cols >= rows, 0.0, -jnp.inf)
        parts = [s0[...]]
        for hop, ref in enumerate((s1, s2, s3), 1):
            part = ref[...]
            row = lax.broadcasted_iota(jnp.int32, part.shape, 0)
            parts.append(jnp.where((device + hop > last) & (row < heads), BIG, part))
        stats = jnp.concatenate(parts, axis=1)
        for one in range(lse.shape[0]):
            lse[one] = stats[one : one + 1]
            delta[one] = stats[lse.shape[0] + one : lse.shape[0] + one + 1]

    queries = jnp.concatenate([q0[...], q1[...], q2[...], q3[...]], axis=0)
    dos = jnp.concatenate([d0[...], d1[...], d2[...], d3[...]], axis=0)
    scores = lax.dot_general(k_ref[...], queries, NT, preferred_element_type=f32) * scale - lse[head]
    edge = bias.shape[1]
    scores = jnp.concatenate([scores[:, :edge] + bias[...], scores[:, edge:]], axis=1)
    probs = jnp.exp(scores)
    prob_grad = lax.dot_general(v_ref[...], dos, NT, preferred_element_type=f32)
    score_grad = (probs * (prob_grad - delta[head])).astype(jnp.bfloat16)
    dk_ref[...] = (jnp.dot(score_grad, queries, preferred_element_type=f32) * scale).astype(dk_ref.dtype)
    dv_ref[...] = jnp.dot(probs.astype(jnp.bfloat16), dos, preferred_element_type=f32).astype(dv_ref.dtype)


def key_side(device, keys, values, queries, out_grads, stats, scale, last):
    block, width = keys.shape
    heads = width // HEAD
    column = pl.BlockSpec((block, HEAD), lambda h: (0, h))
    whole = pl.BlockSpec((2 * heads, block), lambda h: (0, 0))
    shape = jax.ShapeDtypeStruct((block, width), jnp.bfloat16)
    return pl.pallas_call(
        functools.partial(key_kernel, scale, last),
        grid=(heads,),
        in_specs=[pl.BlockSpec(memory_space=pltpu.SMEM)] + [column] * 10 + [whole] * 4,
        out_specs=[column, column],
        out_shape=[shape, shape],
        scratch_shapes=[
            pltpu.VMEM((block, 256), jnp.float32),
            pltpu.VMEM((heads, 1, 4 * block), jnp.float32),
            pltpu.VMEM((heads, 1, 4 * block), jnp.float32),
        ],
        compiler_params=pltpu.CompilerParams(vmem_limit_bytes=24 * 2**20),
        cost_estimate=pl.CostEstimate(
            flops=40 * block * block * width, bytes_accessed=24 * block * width, transcendentals=4 * block * block * heads
        ),
    )(device, keys, values, *queries, *out_grads, *stats)


def per_device(queries, keys, values, stream_grad, conv_input, conv_weight, out_weight):
    block = queries.shape[0]
    last = lax.axis_size("ctx") - 1
    scale = 1.0 / math.sqrt(HEAD)
    device = lax.axis_index("ctx").astype(jnp.int32).reshape(1)
    tp = lax.axis_index("tp").astype(jnp.int32).reshape(1)

    low = rotated(jnp.concatenate([conv_input[block - EDGE :], stream_grad[block - EDGE :]], axis=0), 1)
    high = rotated(jnp.concatenate([conv_input[:EDGE], stream_grad[:EDGE]], axis=0), -1)
    key_blocks, value_blocks, query_blocks = [keys], [values], [queries]
    for hop in range(3):
        key_blocks.append(rotated(key_blocks[-1], 1))
        value_blocks.append(rotated(value_blocks[-1], 1))
        query_blocks.append(rotated(query_blocks[-1], -1))

    grad_stream, tap_rows = conv(device, stream_grad, conv_input, low, high, conv_weight, last)
    other = lax.ppermute(grad_stream, "tp", [(0, 1), (1, 0)])
    kernel_grad = summed(tap_rows) / math.sqrt(block * (last + 1))
    out_grad = project(tp, grad_stream, other, out_weight)
    out_grads = [out_grad]
    for hop in range(3):
        out_grads.append(rotated(out_grads[-1], -1))

    query_grad, stats = query_side(device, queries, out_grad, key_blocks[::-1], value_blocks[::-1], scale)
    all_stats = [stats] + [rotated(stats, -hop) for hop in (1, 2, 3)]
    key_grad, value_grad = key_side(device, keys, values, query_blocks, out_grads, all_stats, scale, last)
    return (query_grad, key_grad, value_grad, grad_stream, kernel_grad)


def solution(mesh):
    return jax.shard_map(
        per_device,
        mesh=mesh,
        in_specs=(
            P("ctx", "tp"),
            P("ctx", "tp"),
            P("ctx", "tp"),
            P("ctx", "tp"),
            P("ctx", "tp"),
            P(None, "tp"),
            P("tp", None),
        ),
        out_specs=(P("ctx", "tp"), P("ctx", "tp"), P("ctx", "tp"), P("ctx", "tp"), P(None, "tp")),
        check_vma=False,
    )
```

```python
import functools
import math

import jax
import jax.numpy as jnp
from jax import lax
from jax.experimental import pallas as pl
from jax.experimental.pallas import tpu as pltpu
from jax.sharding import Mesh
from jax.sharding import PartitionSpec as P

HEAD = 128
EDGE = 16
NT = (((1,), (1,)), ((), ()))
BIG = 1e30
CTX = ("far", "near")


def rotated(part, by):
    count = lax.axis_size(CTX)
    return lax.ppermute(part, CTX, [(i, (i + by) % count) for i in range(count)])


def after(parts, done):
    return lax.optimization_barrier(tuple(parts) + tuple(done))[: len(parts)]


def summed(part):
    part = jnp.sum(lax.all_to_all(part, "far", 0, 0, tiled=True), axis=0)
    copies = jnp.broadcast_to(part, (lax.axis_size("near"),) + part.shape)
    part = jnp.sum(lax.all_to_all(copies, "near", 0, 0, tiled=True), axis=0)
    copies = jnp.broadcast_to(part, (lax.axis_size("far"),) + part.shape)
    return lax.all_to_all(copies, "far", 0, 0, tiled=True)


def conv_kernel(last, idx_ref, grad_ref, input_ref, low_ref, high_ref, taps_ref, out_ref, rows_ref, gpad, cpad):
    block = grad_ref.shape[0]
    taps_count = taps_ref.shape[0]
    reach = taps_count // 2
    device = idx_ref[0]
    f32 = jnp.float32
    low = jnp.where(device > 0, low_ref[...].astype(f32), 0.0)
    high = jnp.where(device < last, high_ref[...].astype(f32), 0.0)
    grad = grad_ref[...].astype(f32)
    cpad[:EDGE] = low[:EDGE]
    gpad[:EDGE] = low[EDGE:]
    cpad[EDGE : EDGE + block] = input_ref[...].astype(f32)
    gpad[EDGE : EDGE + block] = grad
    cpad[EDGE + block :] = high[:EDGE]
    gpad[EDGE + block :] = high[EDGE:]
    taps = taps_ref[...].astype(f32)
    total = jnp.zeros_like(grad)
    for tap in range(taps_count):
        total = total + taps[tap : tap + 1] * gpad[pl.ds(EDGE + reach - tap, block), :]
    out_ref[...] = (grad + total).astype(out_ref.dtype)
    for tap in range(taps_count):
        prod = grad * cpad[pl.ds(EDGE - reach + tap, block), :]
        rows_ref[0, tap : tap + 1, :] = jnp.sum(prod, axis=0, keepdims=True)
    rows_ref[0, taps_count:, :] = jnp.zeros_like(rows_ref[0, taps_count:, :])


def conv(device, grad, inputs, low, high, taps, last):
    block, width = grad.shape
    count = taps.shape[0]
    lanes = 128
    rows = 8 * pl.cdiv(count, 8)
    column = lambda rows: pl.BlockSpec((rows, lanes), lambda c: (0, c))
    return pl.pallas_call(
        functools.partial(conv_kernel, last),
        grid=(width // lanes,),
        in_specs=[
            pl.BlockSpec(memory_space=pltpu.SMEM),
            column(block),
            column(block),
            column(2 * EDGE),
            column(2 * EDGE),
            column(count),
        ],
        out_specs=[column(block), pl.BlockSpec((1, rows, lanes), lambda c: (c, 0, 0))],
        out_shape=[
            jax.ShapeDtypeStruct((block, width), jnp.bfloat16),
            jax.ShapeDtypeStruct((width // lanes, rows, lanes), jnp.float32),
        ],
        scratch_shapes=[
            pltpu.VMEM((block + 2 * EDGE, lanes), jnp.float32),
            pltpu.VMEM((block + 2 * EDGE, lanes), jnp.float32),
        ],
        compiler_params=pltpu.CompilerParams(vmem_limit_bytes=56 * 2**20),
        cost_estimate=pl.CostEstimate(flops=8 * block * width * count, bytes_accessed=4 * block * width, transcendentals=0),
    )(device, grad, inputs, low, high, taps)


def project_kernel(idx_ref, own_ref, other_ref, weight_ref, out_ref):
    half = own_ref.shape[1]
    tp = idx_ref[0]
    first = weight_ref[:, pl.ds(pl.multiple_of(tp * half, half), half)]
    second = weight_ref[:, pl.ds(pl.multiple_of((1 - tp) * half, half), half)]
    total = lax.dot_general(own_ref[...], first, NT, preferred_element_type=jnp.float32)
    total = total + lax.dot_general(other_ref[...], second, NT, preferred_element_type=jnp.float32)
    out_ref[...] = total.astype(out_ref.dtype)


def project(tp, own, other, weight):
    block, half = own.shape
    rows, full = weight.shape
    step = 256
    return pl.pallas_call(
        project_kernel,
        grid=(rows // step,),
        in_specs=[
            pl.BlockSpec(memory_space=pltpu.SMEM),
            pl.BlockSpec((block, half), lambda n: (0, 0)),
            pl.BlockSpec((block, half), lambda n: (0, 0)),
            pl.BlockSpec((step, full), lambda n: (n, 0)),
        ],
        out_specs=pl.BlockSpec((block, step), lambda n: (0, n)),
        out_shape=jax.ShapeDtypeStruct((block, rows), jnp.bfloat16),
        compiler_params=pltpu.CompilerParams(vmem_limit_bytes=56 * 2**20),
        cost_estimate=pl.CostEstimate(flops=2 * block * rows * full, bytes_accessed=2 * rows * full, transcendentals=0),
    )(tp, own, other, weight)


def query_kernel(scale, idx_ref, q_ref, do_ref, k3, k2, k1, k0, v3, v2, v1, v0, out_ref, stats_ref, bias, columns):
    head = pl.program_id(0)
    heads = pl.num_programs(0)
    block = q_ref.shape[0]
    f32 = jnp.float32

    @pl.when(head == 0)
    def _():
        rows = lax.broadcasted_iota(jnp.int32, bias.shape, 0)
        cols = lax.broadcasted_iota(jnp.int32, bias.shape, 1)
        valid = (cols <= 3 * block + rows) & (cols >= (3 - idx_ref[0]) * block)
        bias[...] = jnp.where(valid, 0.0, -jnp.inf)
        columns[...] = jnp.zeros_like(columns)

    keys = jnp.concatenate([k3[...], k2[...], k1[...], k0[...]], axis=0)
    values = jnp.concatenate([v3[...], v2[...], v1[...], v0[...]], axis=0)
    do = do_ref[...]
    scores = lax.dot_general(q_ref[...], keys, NT, preferred_element_type=f32) * scale + bias[...]
    top = jnp.max(scores, axis=1, keepdims=True)
    expo = jnp.exp(scores - top)
    denom = jnp.sum(expo, axis=1, keepdims=True)
    probs = expo * (1.0 / denom)
    prob_grad = lax.dot_general(do, values, NT, preferred_element_type=f32)
    delta = jnp.sum(probs.astype(jnp.bfloat16).astype(f32) * prob_grad, axis=1, keepdims=True)
    score_grad = (probs * (prob_grad - delta)).astype(jnp.bfloat16)
    out = jnp.dot(score_grad, keys, preferred_element_type=f32) * scale
    out_ref[...] = out.astype(out_ref.dtype)
    lane = lax.broadcasted_iota(jnp.int32, columns.shape, 1)
    both = jnp.where(lane == head, top + jnp.log(denom), columns[...])
    columns[...] = jnp.where(lane == heads + head, delta, both)

    @pl.when(head == heads - 1)
    def _():
        stats_ref[...] = columns[...].T[: stats_ref.shape[0]]


def query_side(device, queries, out_grad, keys, values, scale):
    block, width = queries.shape
    heads = width // HEAD
    column = pl.BlockSpec((block, HEAD), lambda h: (0, h))
    return pl.pallas_call(
        functools.partial(query_kernel, scale),
        grid=(heads,),
        in_specs=[pl.BlockSpec(memory_space=pltpu.SMEM)] + [column] * 10,
        out_specs=[column, pl.BlockSpec((2 * heads, block), lambda h: (0, 0))],
        out_shape=[
            jax.ShapeDtypeStruct((block, width), jnp.bfloat16),
            jax.ShapeDtypeStruct((2 * heads, block), jnp.float32),
        ],
        scratch_shapes=[
            pltpu.VMEM((block, 4 * block), jnp.float32),
            pltpu.VMEM((block, HEAD), jnp.float32),
        ],
        compiler_params=pltpu.CompilerParams(vmem_limit_bytes=24 * 2**20),
        cost_estimate=pl.CostEstimate(
            flops=40 * block * block * width, bytes_accessed=24 * block * width, transcendentals=4 * block * block * heads
        ),
    )(device, queries, out_grad, *keys, *values)


def key_kernel(
    scale, norm, last, idx_ref, k_ref, v_ref, q0, q1, q2, q3, d0, d1, d2, d3, s0, s1, s2, s3, taps_ref,
    dk_ref, dv_ref, kernel_ref, bias, lse, delta,
):
    head = pl.program_id(0)
    heads = pl.num_programs(0)
    block = k_ref.shape[0]
    f32 = jnp.float32
    device = idx_ref[0]

    @pl.when(head == 0)
    def _():
        rows = lax.broadcasted_iota(jnp.int32, bias.shape, 0)
        cols = lax.broadcasted_iota(jnp.int32, bias.shape, 1)
        bias[...] = jnp.where(cols >= rows, 0.0, -jnp.inf)
        parts = [s0[...]]
        for hop, ref in enumerate((s1, s2, s3), 1):
            part = ref[...]
            row = lax.broadcasted_iota(jnp.int32, part.shape, 0)
            parts.append(jnp.where((device + hop > last) & (row < heads), BIG, part))
        stats = jnp.concatenate(parts, axis=1)
        for one in range(lse.shape[0]):
            lse[one] = stats[one : one + 1]
            delta[one] = stats[lse.shape[0] + one : lse.shape[0] + one + 1]

    kernel_ref[...] = taps_ref[0, : kernel_ref.shape[0]] * norm
    queries = jnp.concatenate([q0[...], q1[...], q2[...], q3[...]], axis=0)
    dos = jnp.concatenate([d0[...], d1[...], d2[...], d3[...]], axis=0)
    scores = lax.dot_general(k_ref[...], queries, NT, preferred_element_type=f32) * scale - lse[head]
    edge = bias.shape[1]
    scores = jnp.concatenate([scores[:, :edge] + bias[...], scores[:, edge:]], axis=1)
    probs = jnp.exp(scores)
    prob_grad = lax.dot_general(v_ref[...], dos, NT, preferred_element_type=f32)
    score_grad = (probs * (prob_grad - delta[head])).astype(jnp.bfloat16)
    dk_ref[...] = (jnp.dot(score_grad, queries, preferred_element_type=f32) * scale).astype(dk_ref.dtype)
    dv_ref[...] = jnp.dot(probs.astype(jnp.bfloat16), dos, preferred_element_type=f32).astype(dv_ref.dtype)


def key_side(device, keys, values, queries, out_grads, stats, tap_sums, taps_count, scale, norm, last):
    block, width = keys.shape
    heads = width // HEAD
    column = pl.BlockSpec((block, HEAD), lambda h: (0, h))
    whole = pl.BlockSpec((2 * heads, block), lambda h: (0, 0))
    shape = jax.ShapeDtypeStruct((block, width), jnp.bfloat16)
    return pl.pallas_call(
        functools.partial(key_kernel, scale, norm, last),
        grid=(heads,),
        in_specs=[pl.BlockSpec(memory_space=pltpu.SMEM)] + [column] * 10 + [whole] * 4
        + [pl.BlockSpec((1,) + tap_sums.shape[1:], lambda h: (h, 0, 0))],
        out_specs=[column, column, pl.BlockSpec((taps_count, HEAD), lambda h: (0, h))],
        out_shape=[shape, shape, jax.ShapeDtypeStruct((taps_count, width), jnp.float32)],
        scratch_shapes=[
            pltpu.VMEM((block, 256), jnp.float32),
            pltpu.VMEM((heads, 1, 4 * block), jnp.float32),
            pltpu.VMEM((heads, 1, 4 * block), jnp.float32),
        ],
        compiler_params=pltpu.CompilerParams(vmem_limit_bytes=24 * 2**20),
        cost_estimate=pl.CostEstimate(
            flops=40 * block * block * width, bytes_accessed=24 * block * width, transcendentals=4 * block * block * heads
        ),
    )(device, keys, values, *queries, *out_grads, *stats, tap_sums)


def per_device(queries, keys, values, stream_grad, conv_input, conv_weight, out_weight):
    block = queries.shape[0]
    last = lax.axis_size(CTX) - 1
    scale = 1.0 / math.sqrt(HEAD)
    device = lax.axis_index(CTX).astype(jnp.int32).reshape(1)
    tp = lax.axis_index("tp").astype(jnp.int32).reshape(1)

    low = rotated(jnp.concatenate([conv_input[block - EDGE :], stream_grad[block - EDGE :]], axis=0), 1)
    high = rotated(jnp.concatenate([conv_input[:EDGE], stream_grad[:EDGE]], axis=0), -1)
    key_blocks, value_blocks, query_blocks = [keys], [values], [queries]
    for hop in range(3):
        key_blocks.append(rotated(key_blocks[-1], 1))
        value_blocks.append(rotated(value_blocks[-1], 1))
        query_blocks.append(rotated(query_blocks[-1], -1))

    low, high = after((low, high), (key_blocks[1], query_blocks[1]))
    grad_stream, tap_rows = conv(device, stream_grad, conv_input, low, high, conv_weight, last)
    (own,) = after((grad_stream,), (value_blocks[1],))
    other = lax.ppermute(own, "tp", [(0, 1), (1, 0)])
    tap_sums = summed(tap_rows)
    (other,) = after((other,), (key_blocks[2], query_blocks[2]))
    out_grad = project(tp, grad_stream, other, out_weight)
    (sent,) = after((out_grad,), (value_blocks[2],))
    out_grads = [out_grad, rotated(sent, -1)]
    for hop in range(2):
        out_grads.append(rotated(out_grads[-1], -1))

    query_grad, stats = query_side(device, queries, out_grad, key_blocks[::-1], value_blocks[::-1], scale)
    all_stats = [stats] + [rotated(stats, -hop) for hop in (1, 2, 3)]
    norm = 1.0 / math.sqrt(block * (last + 1))
    key_grad, value_grad, kernel_grad = key_side(
        device, keys, values, query_blocks, out_grads, all_stats, tap_sums, conv_weight.shape[0], scale, norm, last
    )
    return (query_grad, key_grad, value_grad, grad_stream, kernel_grad)


def solution(mesh):
    count, pair = mesh.devices.shape
    far = 8
    split = Mesh(mesh.devices.reshape(far, count // far, pair), CTX + ("tp",))
    frames = P(CTX, "tp")
    return jax.shard_map(
        per_device,
        mesh=split,
        in_specs=(frames,) * 5 + (P(None, "tp"), P("tp", None)),
        out_specs=(frames,) * 4 + (P(None, "tp"),),
        check_vma=False,
    )
```

```python
import functools
import math

import jax
import jax.numpy as jnp
from jax import lax
from jax.experimental import pallas as pl
from jax.experimental.pallas import tpu as pltpu
from jax.sharding import Mesh
from jax.sharding import PartitionSpec as P

HEAD = 128
EDGE = 16
NT = (((1,), (1,)), ((), ()))
BIG = 1e30
GROUP = 2
CTX = ("far", "near")


def rotated(part, by):
    count = lax.axis_size(CTX)
    return lax.ppermute(part, CTX, [(i, (i + by) % count) for i in range(count)])


def after(parts, done):
    return lax.optimization_barrier(tuple(parts) + tuple(done))[: len(parts)]


def conv_kernel(last, idx_ref, grad_ref, input_ref, low_ref, high_ref, taps_ref, out_ref, rows_ref, gpad, cpad):
    block = grad_ref.shape[0]
    taps_count = taps_ref.shape[0]
    reach = taps_count // 2
    device = idx_ref[0]
    f32 = jnp.float32
    rows_ref[:, taps_count:, :] = jnp.zeros_like(rows_ref[:, taps_count:, :])
    for group in range(rows_ref.shape[0]):
        lanes = slice(group * HEAD, (group + 1) * HEAD)
        low = jnp.where(device > 0, low_ref[block:, lanes].astype(f32), 0.0)
        high = jnp.where(device < last, high_ref[block:, lanes].astype(f32), 0.0)
        grad = grad_ref[:, lanes].astype(f32)
        cpad[:EDGE, lanes] = low[:EDGE]
        gpad[:EDGE, lanes] = low[EDGE:]
        cpad[EDGE : EDGE + block, lanes] = input_ref[:, lanes].astype(f32)
        gpad[EDGE : EDGE + block, lanes] = grad
        cpad[EDGE + block :, lanes] = high[:EDGE]
        gpad[EDGE + block :, lanes] = high[EDGE:]
        taps = taps_ref[:, lanes].astype(f32)
        total = jnp.zeros_like(grad)
        for tap in range(taps_count):
            total = total + taps[tap : tap + 1] * gpad[pl.ds(EDGE + reach - tap, block), lanes]
        out_ref[:, lanes] = (grad + total).astype(out_ref.dtype)
        for tap in range(taps_count):
            prod = grad * cpad[pl.ds(EDGE - reach + tap, block), lanes]
            rows_ref[group, tap : tap + 1, :] = jnp.sum(prod, axis=0, keepdims=True)


def conv(device, grad, inputs, low, high, taps, last):
    block, width = grad.shape
    count = taps.shape[0]
    lanes = GROUP * HEAD
    rows = 8 * pl.cdiv(count, 8)
    column = lambda rows: pl.BlockSpec((rows, lanes), lambda c: (0, c))
    return pl.pallas_call(
        functools.partial(conv_kernel, last),
        grid=(width // lanes,),
        in_specs=[
            pl.BlockSpec(memory_space=pltpu.SMEM),
            column(block),
            column(block),
            column(block + 2 * EDGE),
            column(block + 2 * EDGE),
            column(count),
        ],
        out_specs=[column(block), pl.BlockSpec((GROUP, rows, HEAD), lambda c: (c, 0, 0))],
        out_shape=[
            jax.ShapeDtypeStruct((block, width), jnp.bfloat16),
            jax.ShapeDtypeStruct((width // HEAD, rows, HEAD), jnp.float32),
        ],
        scratch_shapes=[
            pltpu.VMEM((block + 2 * EDGE, lanes), jnp.float32),
            pltpu.VMEM((block + 2 * EDGE, lanes), jnp.float32),
        ],
        compiler_params=pltpu.CompilerParams(vmem_limit_bytes=16 * 2**20),
        cost_estimate=pl.CostEstimate(flops=8 * block * width * count, bytes_accessed=4 * block * width, transcendentals=0),
    )(device, grad, inputs, low, high, taps)


def own_kernel(idx_ref, part_ref, weight_ref, out_ref):
    out_ref[...] = lax.dot_general(part_ref[...], weight_ref[...], NT, preferred_element_type=jnp.float32)


def other_kernel(idx_ref, part_ref, weight_ref, before_ref, out_ref):
    total = lax.dot_general(part_ref[...], weight_ref[...], NT, preferred_element_type=jnp.float32)
    out_ref[...] = (before_ref[...] + total).astype(out_ref.dtype)


def project(place, part, weight, before=None):
    block, half = part.shape
    rows = weight.shape[0]
    step = 256
    columns = pl.BlockSpec((block, step), lambda n, place: (0, n))
    return pl.pallas_call(
        own_kernel if before is None else other_kernel,
        grid_spec=pltpu.PrefetchScalarGridSpec(
            num_scalar_prefetch=1,
            grid=(rows // step,),
            in_specs=[
                pl.BlockSpec((block, half), lambda n, place: (0, 0)),
                pl.BlockSpec((step, half), lambda n, place: (n, place[0])),
            ]
            + [columns] * (before is not None),
            out_specs=columns,
        ),
        out_shape=jax.ShapeDtypeStruct((block, rows), jnp.float32 if before is None else jnp.bfloat16),
        compiler_params=pltpu.CompilerParams(vmem_limit_bytes=56 * 2**20),
        cost_estimate=pl.CostEstimate(flops=2 * block * rows * half, bytes_accessed=2 * rows * half, transcendentals=0),
    )(place, part, weight, *(() if before is None else (before,)))


def query_kernel(scale, idx_ref, q_ref, do_ref, k3, k2, k1, k0, v3, v2, v1, v0, out_ref, stats_ref, bias, columns):
    step = pl.program_id(0)
    steps = pl.num_programs(0)
    block = q_ref.shape[0]
    f32 = jnp.float32

    @pl.when(step == 0)
    def _():
        rows = lax.broadcasted_iota(jnp.int32, bias.shape, 0)
        cols = lax.broadcasted_iota(jnp.int32, bias.shape, 1)
        valid = (cols <= 3 * block + rows) & (cols >= (3 - idx_ref[0]) * block)
        bias[...] = jnp.where(valid, 0.0, -jnp.inf)
        columns[...] = jnp.zeros_like(columns)

    lane = lax.broadcasted_iota(jnp.int32, columns.shape, 1)
    both = columns[...]
    for group in range(GROUP):
        lanes = slice(group * HEAD, (group + 1) * HEAD)
        keys = jnp.concatenate([ref[:block, lanes] for ref in (k3, k2, k1, k0)], axis=0)
        values = jnp.concatenate([ref[:, lanes] for ref in (v3, v2, v1, v0)], axis=0)
        scores = lax.dot_general(q_ref[:, lanes], keys, NT, preferred_element_type=f32) * scale + bias[...]
        top = jnp.max(scores, axis=1, keepdims=True)
        expo = jnp.exp(scores - top)
        denom = jnp.sum(expo, axis=1, keepdims=True)
        probs = expo * (1.0 / denom)
        prob_grad = lax.dot_general(do_ref[:, lanes], values, NT, preferred_element_type=f32)
        delta = jnp.sum(probs.astype(jnp.bfloat16).astype(f32) * prob_grad, axis=1, keepdims=True)
        score_grad = (probs * (prob_grad - delta)).astype(jnp.bfloat16)
        out = jnp.dot(score_grad, keys, preferred_element_type=f32) * scale
        out_ref[:, lanes] = out.astype(out_ref.dtype)
        both = jnp.where(lane == GROUP * step + group, top + jnp.log(denom), both)
        both = jnp.where(lane == GROUP * (steps + step) + group, delta, both)
    columns[...] = both

    @pl.when(step == steps - 1)
    def _():
        stats_ref[...] = columns[...].T[: stats_ref.shape[0]]


def head_columns(array):
    return pl.BlockSpec((array.shape[0], GROUP * HEAD), lambda h: (0, h))


def query_side(device, queries, out_grad, keys, values, scale):
    block, width = queries.shape
    heads = width // HEAD
    operands = (queries, out_grad, *keys, *values)
    return pl.pallas_call(
        functools.partial(query_kernel, scale),
        grid=(heads // GROUP,),
        in_specs=[pl.BlockSpec(memory_space=pltpu.SMEM)] + [head_columns(array) for array in operands],
        out_specs=[head_columns(queries), pl.BlockSpec((2 * heads, block), lambda h: (0, 0))],
        out_shape=[
            jax.ShapeDtypeStruct((block, width), jnp.bfloat16),
            jax.ShapeDtypeStruct((2 * heads, block), jnp.float32),
        ],
        scratch_shapes=[
            pltpu.VMEM((block, 4 * block), jnp.float32),
            pltpu.VMEM((block, HEAD), jnp.float32),
        ],
        compiler_params=pltpu.CompilerParams(vmem_limit_bytes=32 * 2**20),
        cost_estimate=pl.CostEstimate(
            flops=40 * block * block * width, bytes_accessed=24 * block * width, transcendentals=4 * block * block * heads
        ),
    )(device, *operands)


def key_kernel(scale, last, idx_ref, k_ref, v_ref, q0, q1, q2, q3, d0, d1, d2, d3, s0, s1, s2, s3, dk_ref, dv_ref, bias, lse, delta):
    step = pl.program_id(0)
    block = k_ref.shape[0]
    heads = lse.shape[0]
    f32 = jnp.float32

    @pl.when(step == 0)
    def _():
        rows = lax.broadcasted_iota(jnp.int32, bias.shape, 0)
        cols = lax.broadcasted_iota(jnp.int32, bias.shape, 1)
        bias[...] = jnp.where(cols >= rows, 0.0, -jnp.inf)
        parts = [s0[...]]
        for hop, ref in enumerate((s1, s2, s3), 1):
            part = ref[...]
            row = lax.broadcasted_iota(jnp.int32, part.shape, 0)
            parts.append(jnp.where((idx_ref[0] + hop > last) & (row < heads), BIG, part))
        stats = jnp.concatenate(parts, axis=1)
        for one in range(heads):
            lse[one] = stats[one : one + 1]
            delta[one] = stats[heads + one : heads + one + 1]

    edge = bias.shape[1]
    for group in range(GROUP):
        lanes = slice(group * HEAD, (group + 1) * HEAD)
        head = GROUP * step + group
        queries = jnp.concatenate([ref[:block, lanes] for ref in (q0, q1, q2, q3)], axis=0)
        dos = jnp.concatenate([ref[:, lanes] for ref in (d0, d1, d2, d3)], axis=0)
        scores = lax.dot_general(k_ref[:, lanes], queries, NT, preferred_element_type=f32) * scale - lse[head]
        scores = jnp.concatenate([scores[:, :edge] + bias[...], scores[:, edge:]], axis=1)
        probs = jnp.exp(scores)
        prob_grad = lax.dot_general(v_ref[:, lanes], dos, NT, preferred_element_type=f32)
        score_grad = (probs * (prob_grad - delta[head])).astype(jnp.bfloat16)
        dk_ref[:, lanes] = (jnp.dot(score_grad, queries, preferred_element_type=f32) * scale).astype(dk_ref.dtype)
        dv_ref[:, lanes] = jnp.dot(probs.astype(jnp.bfloat16), dos, preferred_element_type=f32).astype(dv_ref.dtype)


def key_side(device, keys, values, queries, out_grads, stats, scale, last):
    block, width = keys.shape
    heads = width // HEAD
    whole = pl.BlockSpec((2 * heads, block), lambda h: (0, 0))
    shape = jax.ShapeDtypeStruct((block, width), jnp.bfloat16)
    operands = (keys, values, *queries, *out_grads)
    return pl.pallas_call(
        functools.partial(key_kernel, scale, last),
        grid=(heads // GROUP,),
        in_specs=[pl.BlockSpec(memory_space=pltpu.SMEM)] + [head_columns(array) for array in operands] + [whole] * 4,
        out_specs=[head_columns(keys)] * 2,
        out_shape=[shape, shape],
        scratch_shapes=[
            pltpu.VMEM((block, 256), jnp.float32),
            pltpu.VMEM((heads, 1, 4 * block), jnp.float32),
            pltpu.VMEM((heads, 1, 4 * block), jnp.float32),
        ],
        compiler_params=pltpu.CompilerParams(vmem_limit_bytes=32 * 2**20),
        cost_estimate=pl.CostEstimate(
            flops=40 * block * block * width, bytes_accessed=24 * block * width, transcendentals=4 * block * block * heads
        ),
    )(device, *operands, *stats)


def per_device(queries, keys, values, stream_grad, conv_input, conv_weight, out_weight):
    block = queries.shape[0]
    last = lax.axis_size(CTX) - 1
    scale = 1.0 / math.sqrt(HEAD)
    device = lax.axis_index(CTX).astype(jnp.int32).reshape(1)
    tp = lax.axis_index("tp").astype(jnp.int32).reshape(1)

    k1 = rotated(jnp.concatenate([keys, conv_input[block - EDGE :], stream_grad[block - EDGE :]], axis=0), 1)
    q1 = rotated(jnp.concatenate([queries, conv_input[:EDGE], stream_grad[:EDGE]], axis=0), -1)
    (first,) = after((values,), (q1,))
    v1 = rotated(first, 1)
    k2, q2 = rotated(k1, 1), rotated(q1, -1)
    v2 = rotated(v1, 1)

    grad_stream, tap_rows = conv(device, stream_grad, conv_input, k1, q1, conv_weight, last)
    other = lax.ppermute(grad_stream, "tp", [(0, 1), (1, 0)])
    before = project(tp, grad_stream, out_weight)
    (tap_rows,) = after((tap_rows,), (k2,))
    tap_sums = jnp.sum(lax.all_to_all(tap_rows, "far", 0, 0, tiled=True), axis=0)
    (other,) = after((other,), (k2, q2, tap_sums))
    out_grad = project(1 - tp, other, out_weight, before)
    k3, q3 = rotated(k2, 1), rotated(q2, -1)
    v3 = rotated(v2, 1)

    (sent,) = after((out_grad,), (v2,))
    d1 = rotated(sent, -1)
    (sent,) = after((d1,), (k3, q3))
    d2 = rotated(sent, -1)
    (sent,) = after((d2,), (v3,))
    d3 = rotated(sent, -1)

    copies = jnp.broadcast_to(tap_sums, (lax.axis_size("near"),) + tap_sums.shape)
    (copies,) = after((copies,), (v2, out_grad))
    tap_sums = jnp.sum(lax.all_to_all(copies, "near", 0, 0, tiled=True), axis=0)
    (inner,) = after((queries,), (tap_sums,))
    query_grad, stats = query_side(device, inner, out_grad, (k3, k2, k1, keys), (v3, v2, v1, values), scale)
    all_stats = [stats] + [rotated(stats, -hop) for hop in (1, 2, 3)]
    copies = jnp.broadcast_to(tap_sums, (lax.axis_size("far"),) + tap_sums.shape)
    (copies,) = after((copies,), (stats,))
    tap_sums = lax.all_to_all(copies, "far", 0, 0, tiled=True)
    (inner,) = after((keys,), (tap_sums,))
    key_grad, value_grad = key_side(
        device, inner, values, (queries, q1, q2, q3), (out_grad, d1, d2, d3), all_stats, scale, last
    )
    rows = jnp.transpose(tap_sums, (1, 0, 2)).reshape(tap_sums.shape[1], -1)[: conv_weight.shape[0]]
    kernel_grad = rows / math.sqrt(block * (last + 1))
    return (query_grad, key_grad, value_grad, grad_stream, kernel_grad)


def solution(mesh):
    count, pair = mesh.devices.shape
    far = 8
    split = Mesh(mesh.devices.reshape(far, count // far, pair), CTX + ("tp",))
    frames = P(CTX, "tp")
    return jax.shard_map(
        per_device,
        mesh=split,
        in_specs=(frames,) * 5 + (P(None, "tp"), P("tp", None)),
        out_specs=(frames,) * 4 + (P(None, "tp"),),
        check_vma=False,
    )
```

```python
import functools
import math

import jax
import jax.numpy as jnp
from jax import lax
from jax.experimental import pallas as pl
from jax.experimental.pallas import tpu as pltpu
from jax.sharding import Mesh
from jax.sharding import PartitionSpec as P

HEAD = 128
EDGE = 16
NT = (((1,), (1,)), ((), ()))
BIG = 1e30
GROUP = 2
PIECES = 4
CTX = ("far", "near")


def rotated(part, by):
    count = lax.axis_size(CTX)
    return lax.ppermute(part, CTX, [(i, (i + by) % count) for i in range(count)])


def exchanged(part, by):
    count = lax.axis_size(CTX)
    return part + lax.ppermute(part, CTX, [(i, i ^ by) for i in range(count)])


def after(parts, done):
    return lax.optimization_barrier(tuple(parts) + tuple(done))[: len(parts)]


def pack_kernel(k_ref, q_ref, input_ref, grad_ref, low_ref, high_ref, sems):
    block = k_ref.shape[0]
    half = block // 2
    pairs = []
    for source, target in ((k_ref, low_ref), (q_ref, high_ref)):
        for start in (0, half):
            pairs.append((source.at[pl.ds(start, half)], target.at[pl.ds(start, half)]))
    for target, start in ((low_ref, block - EDGE), (high_ref, 0)):
        pairs.append((input_ref.at[pl.ds(start, EDGE)], target.at[pl.ds(block, EDGE)]))
        pairs.append((grad_ref.at[pl.ds(start, EDGE)], target.at[pl.ds(block + EDGE, EDGE)]))
    copies = [pltpu.make_async_copy(source, target, sems.at[i]) for i, (source, target) in enumerate(pairs)]
    for copy in copies:
        copy.start()
    for copy in copies:
        copy.wait()


def pack(keys, queries, inputs, grad):
    block, width = keys.shape
    anywhere = pl.BlockSpec(memory_space=pl.ANY)
    shape = jax.ShapeDtypeStruct((block + 2 * EDGE, width), keys.dtype)
    return pl.pallas_call(
        pack_kernel,
        in_specs=[anywhere] * 4,
        out_specs=[anywhere] * 2,
        out_shape=[shape, shape],
        scratch_shapes=[pltpu.SemaphoreType.DMA((8,))],
        compiler_params=pltpu.CompilerParams(vmem_limit_bytes=56 * 2**20),
    )(keys, queries, inputs, grad)


def conv_kernel(last, idx_ref, grad_ref, input_ref, low_ref, high_ref, taps_ref, out_ref, rows_ref, gpad, cpad):
    block = grad_ref.shape[0]
    taps_count = taps_ref.shape[0]
    reach = taps_count // 2
    device = idx_ref[0]
    f32 = jnp.float32
    rows_ref[taps_count:, :] = jnp.zeros_like(rows_ref[taps_count:, :])
    for group in range(GROUP):
        lanes = slice(group * HEAD, (group + 1) * HEAD)
        low = jnp.where(device > 0, low_ref[block:, lanes].astype(f32), 0.0)
        high = jnp.where(device < last, high_ref[block:, lanes].astype(f32), 0.0)
        grad = grad_ref[:, lanes].astype(f32)
        cpad[:EDGE, lanes] = low[:EDGE]
        gpad[:EDGE, lanes] = low[EDGE:]
        cpad[EDGE : EDGE + block, lanes] = input_ref[:, lanes].astype(f32)
        gpad[EDGE : EDGE + block, lanes] = grad
        cpad[EDGE + block :, lanes] = high[:EDGE]
        gpad[EDGE + block :, lanes] = high[EDGE:]
        taps = taps_ref[:, lanes].astype(f32)
        total = grad
        for shift in range(8):
            moved = gpad[pl.ds(shift, block + 24), lanes]
            for start in range(0, 32, 8):
                tap = EDGE + reach - (start + shift)
                if 0 <= tap < taps_count:
                    total = total + taps[tap : tap + 1] * moved[start : start + block]
        out_ref[:, lanes] = total.astype(out_ref.dtype)
        for shift in range(8):
            moved = cpad[pl.ds(shift, block + 24), lanes]
            for start in range(0, 32, 8):
                tap = start + shift - EDGE + reach
                if 0 <= tap < taps_count:
                    prod = grad * moved[start : start + block]
                    rows_ref[tap : tap + 1, lanes] = jnp.sum(prod, axis=0, keepdims=True)


def conv(device, grad, inputs, low, high, taps, last):
    block, width = grad.shape
    count = taps.shape[0]
    lanes = GROUP * HEAD
    rows = 8 * pl.cdiv(count, 8)
    column = lambda rows: pl.BlockSpec((rows, lanes), lambda c: (0, c))
    return pl.pallas_call(
        functools.partial(conv_kernel, last),
        grid=(width // lanes,),
        in_specs=[
            pl.BlockSpec(memory_space=pltpu.SMEM),
            column(block),
            column(block),
            column(block + 2 * EDGE),
            column(block + 2 * EDGE),
            column(count),
        ],
        out_specs=[column(block), column(rows)],
        out_shape=[
            jax.ShapeDtypeStruct((block, width), jnp.bfloat16),
            jax.ShapeDtypeStruct((rows, width), jnp.float32),
        ],
        scratch_shapes=[
            pltpu.VMEM((block + 2 * EDGE, lanes), jnp.float32),
            pltpu.VMEM((block + 2 * EDGE, lanes), jnp.float32),
        ],
        compiler_params=pltpu.CompilerParams(vmem_limit_bytes=56 * 2**20),
        cost_estimate=pl.CostEstimate(flops=8 * block * width * count, bytes_accessed=4 * block * width, transcendentals=0),
    )(device, grad, inputs, low, high, taps)


def project_kernel(idx_ref, part_ref, *refs):
    weights, before, out_ref = refs[:PIECES], refs[PIECES:-1], refs[-1]
    part = part_ref[...]
    for piece, weight in enumerate(weights):
        lanes = slice(piece * HEAD, (piece + 1) * HEAD)
        total = lax.dot_general(part, weight[...], NT, preferred_element_type=jnp.float32)
        for ref in before:
            total = ref[:, lanes] + total
        out_ref[:, lanes] = total.astype(out_ref.dtype)


def project(place, part, weight, before=None):
    block, half = part.shape
    rows = weight.shape[0]
    step = PIECES * HEAD
    columns = pl.BlockSpec((block, step), lambda n, place: (0, n))
    piece = lambda p: pl.BlockSpec((HEAD, half), lambda n, place: (PIECES * n + p, place[0]))
    return pl.pallas_call(
        project_kernel,
        grid_spec=pltpu.PrefetchScalarGridSpec(
            num_scalar_prefetch=1,
            grid=(rows // step,),
            in_specs=[pl.BlockSpec((block, half), lambda n, place: (0, 0))]
            + [piece(p) for p in range(PIECES)]
            + [columns] * (before is not None),
            out_specs=columns,
        ),
        out_shape=jax.ShapeDtypeStruct((block, rows), jnp.float32 if before is None else jnp.bfloat16),
        compiler_params=pltpu.CompilerParams(vmem_limit_bytes=56 * 2**20),
        cost_estimate=pl.CostEstimate(flops=2 * block * rows * half, bytes_accessed=2 * rows * half, transcendentals=0),
    )(place, part, *([weight] * PIECES), *(() if before is None else (before,)))


def query_kernel(scale, idx_ref, q_ref, do_ref, k3, k2, k1, k0, v3, v2, v1, v0, out_ref, stats_ref, bias, columns):
    step = pl.program_id(0)
    steps = pl.num_programs(0)
    block = q_ref.shape[0]
    f32 = jnp.float32

    @pl.when(step == 0)
    def _():
        rows = lax.broadcasted_iota(jnp.int32, bias.shape, 0)
        cols = lax.broadcasted_iota(jnp.int32, bias.shape, 1)
        valid = (cols <= 3 * block + rows) & (cols >= (3 - idx_ref[0]) * block)
        bias[...] = jnp.where(valid, 0.0, -jnp.inf)
        columns[...] = jnp.zeros_like(columns)

    lane = lax.broadcasted_iota(jnp.int32, columns.shape, 1)
    both = columns[...]
    for group in range(GROUP):
        lanes = slice(group * HEAD, (group + 1) * HEAD)
        keys = jnp.concatenate([ref[:block, lanes] for ref in (k3, k2, k1, k0)], axis=0)
        values = jnp.concatenate([ref[:, lanes] for ref in (v3, v2, v1, v0)], axis=0)
        scores = lax.dot_general(q_ref[:, lanes], keys, NT, preferred_element_type=f32) * scale + bias[...]
        top = jnp.max(scores, axis=1, keepdims=True)
        expo = jnp.exp(scores - top)
        denom = jnp.sum(expo, axis=1, keepdims=True)
        probs = expo * (1.0 / denom)
        prob_grad = lax.dot_general(do_ref[:, lanes], values, NT, preferred_element_type=f32)
        delta = jnp.sum(probs.astype(jnp.bfloat16).astype(f32) * prob_grad, axis=1, keepdims=True)
        score_grad = (probs * (prob_grad - delta)).astype(jnp.bfloat16)
        out = jnp.dot(score_grad, keys, preferred_element_type=f32) * scale
        out_ref[:, lanes] = out.astype(out_ref.dtype)
        both = jnp.where(lane == GROUP * step + group, top + jnp.log(denom), both)
        both = jnp.where(lane == GROUP * (steps + step) + group, delta, both)
    columns[...] = both

    @pl.when(step == steps - 1)
    def _():
        stats_ref[...] = columns[...].T[: stats_ref.shape[0]]


def head_columns(array):
    return pl.BlockSpec((array.shape[0], GROUP * HEAD), lambda h: (0, h))


def query_side(device, queries, out_grad, keys, values, scale):
    block, width = queries.shape
    heads = width // HEAD
    operands = (queries, out_grad, *keys, *values)
    return pl.pallas_call(
        functools.partial(query_kernel, scale),
        grid=(heads // GROUP,),
        in_specs=[pl.BlockSpec(memory_space=pltpu.SMEM)] + [head_columns(array) for array in operands],
        out_specs=[head_columns(queries), pl.BlockSpec((2 * heads, block), lambda h: (0, 0))],
        out_shape=[
            jax.ShapeDtypeStruct((block, width), jnp.bfloat16),
            jax.ShapeDtypeStruct((2 * heads, block), jnp.float32),
        ],
        scratch_shapes=[
            pltpu.VMEM((block, 4 * block), jnp.float32),
            pltpu.VMEM((block, HEAD), jnp.float32),
        ],
        compiler_params=pltpu.CompilerParams(vmem_limit_bytes=56 * 2**20),
        cost_estimate=pl.CostEstimate(
            flops=40 * block * block * width, bytes_accessed=24 * block * width, transcendentals=4 * block * block * heads
        ),
    )(device, *operands)


def key_kernel(scale, last, idx_ref, k_ref, v_ref, q0, q1, q2, q3, d0, d1, d2, d3, s0, s1, s2, s3, dk_ref, dv_ref, bias, lse, delta):
    step = pl.program_id(0)
    block = k_ref.shape[0]
    heads = lse.shape[0]
    f32 = jnp.float32

    @pl.when(step == 0)
    def _():
        rows = lax.broadcasted_iota(jnp.int32, bias.shape, 0)
        cols = lax.broadcasted_iota(jnp.int32, bias.shape, 1)
        bias[...] = jnp.where(cols >= rows, 0.0, -jnp.inf)
        parts = [s0[...]]
        for hop, ref in enumerate((s1, s2, s3), 1):
            part = ref[...]
            row = lax.broadcasted_iota(jnp.int32, part.shape, 0)
            parts.append(jnp.where((idx_ref[0] + hop > last) & (row < heads), BIG, part))
        stats = jnp.concatenate(parts, axis=1)
        for one in range(heads):
            lse[one] = stats[one : one + 1]
            delta[one] = stats[heads + one : heads + one + 1]

    edge = bias.shape[1]
    for group in range(GROUP):
        lanes = slice(group * HEAD, (group + 1) * HEAD)
        head = GROUP * step + group
        queries = jnp.concatenate([ref[:block, lanes] for ref in (q0, q1, q2, q3)], axis=0)
        dos = jnp.concatenate([ref[:, lanes] for ref in (d0, d1, d2, d3)], axis=0)
        scores = lax.dot_general(k_ref[:, lanes], queries, NT, preferred_element_type=f32) * scale - lse[head]
        scores = jnp.concatenate([scores[:, :edge] + bias[...], scores[:, edge:]], axis=1)
        probs = jnp.exp(scores)
        prob_grad = lax.dot_general(v_ref[:, lanes], dos, NT, preferred_element_type=f32)
        score_grad = (probs * (prob_grad - delta[head])).astype(jnp.bfloat16)
        dk_ref[:, lanes] = (jnp.dot(score_grad, queries, preferred_element_type=f32) * scale).astype(dk_ref.dtype)
        dv_ref[:, lanes] = jnp.dot(probs.astype(jnp.bfloat16), dos, preferred_element_type=f32).astype(dv_ref.dtype)


def key_side(device, keys, values, queries, out_grads, stats, scale, last):
    block, width = keys.shape
    heads = width // HEAD
    whole = pl.BlockSpec((2 * heads, block), lambda h: (0, 0))
    shape = jax.ShapeDtypeStruct((block, width), jnp.bfloat16)
    operands = (keys, values, *queries, *out_grads)
    return pl.pallas_call(
        functools.partial(key_kernel, scale, last),
        grid=(heads // GROUP,),
        in_specs=[pl.BlockSpec(memory_space=pltpu.SMEM)] + [head_columns(array) for array in operands] + [whole] * 4,
        out_specs=[head_columns(keys)] * 2,
        out_shape=[shape, shape],
        scratch_shapes=[
            pltpu.VMEM((block, 256), jnp.float32),
            pltpu.VMEM((heads, 1, 4 * block), jnp.float32),
            pltpu.VMEM((heads, 1, 4 * block), jnp.float32),
        ],
        compiler_params=pltpu.CompilerParams(vmem_limit_bytes=56 * 2**20),
        cost_estimate=pl.CostEstimate(
            flops=40 * block * block * width, bytes_accessed=24 * block * width, transcendentals=4 * block * block * heads
        ),
    )(device, *operands, *stats)


def per_device(queries, keys, values, stream_grad, conv_input, conv_weight, out_weight):
    block = queries.shape[0]
    last = lax.axis_size(CTX) - 1
    scale = 1.0 / math.sqrt(HEAD)
    device = lax.axis_index(CTX).astype(jnp.int32).reshape(1)
    tp = lax.axis_index("tp").astype(jnp.int32).reshape(1)

    low, high = pack(keys, queries, conv_input, stream_grad)
    k1, q1 = rotated(low, 1), rotated(high, -1)
    (first,) = after((values,), (q1,))
    v1 = rotated(first, 1)
    k2, q2 = rotated(k1, 1), rotated(q1, -1)
    v2 = rotated(v1, 1)

    grad_stream, tap_rows = conv(device, stream_grad, conv_input, k1, q1, conv_weight, last)
    other = lax.ppermute(grad_stream, "tp", [(0, 1), (1, 0)])
    tap_rows = exchanged(tap_rows, 1)
    (own,) = after((grad_stream,), (tap_rows,))
    before = project(tp, own, out_weight)
    tap_rows = exchanged(tap_rows, 2)
    (other,) = after((other,), (k2, q2, tap_rows))
    out_grad = project(1 - tp, other, out_weight, before)
    k3, q3 = rotated(k2, 1), rotated(q2, -1)
    v3 = rotated(v2, 1)

    (sent,) = after((out_grad,), (v2,))
    d1 = rotated(sent, -1)
    tap_rows = exchanged(tap_rows, 4)
    (sent,) = after((d1,), (k3, q3, tap_rows))
    d2 = rotated(sent, -1)
    tap_rows = exchanged(tap_rows, 8)
    (sent,) = after((d2,), (v3,))
    d3 = rotated(sent, -1)

    (inner,) = after((queries,), (tap_rows,))
    tap_rows = exchanged(tap_rows, 64)
    query_grad, stats = query_side(device, inner, out_grad, (k3, k2, k1, keys), (v3, v2, v1, values), scale)
    all_stats = [stats] + [rotated(stats, -hop) for hop in (1, 2, 3)]
    (tap_rows,) = after((tap_rows,), (stats,))
    tap_rows = exchanged(tap_rows, 16)
    (inner,) = after((keys,), (tap_rows,))
    tap_rows = exchanged(tap_rows, 32)
    key_grad, value_grad = key_side(
        device, inner, values, (queries, q1, q2, q3), (out_grad, d1, d2, d3), all_stats, scale, last
    )
    kernel_grad = tap_rows[: conv_weight.shape[0]] / math.sqrt(block * (last + 1))
    return (query_grad, key_grad, value_grad, grad_stream, kernel_grad)


def solution(mesh):
    count, pair = mesh.devices.shape
    far = 8
    split = Mesh(mesh.devices.reshape(far, count // far, pair), CTX + ("tp",))
    frames = P(CTX, "tp")
    return jax.shard_map(
        per_device,
        mesh=split,
        in_specs=(frames,) * 5 + (P(None, "tp"), P("tp", None)),
        out_specs=(frames,) * 4 + (P(None, "tp"),),
        check_vma=False,
    )
```

```python
import functools
import math

import jax
import jax.numpy as jnp
from jax import lax
from jax.experimental import pallas as pl
from jax.experimental.pallas import tpu as pltpu
from jax.sharding import Mesh
from jax.sharding import PartitionSpec as P

HEAD = 128
EDGE = 16
NT = (((1,), (1,)), ((), ()))
BIG = 1e30
GROUP = 4
VMEM_BYTES = 24 * 2**20
INSIDE = pl.BlockSpec(memory_space=pltpu.VMEM)
CTX = ("far", "near")


def rotated(part, by):
    count = lax.axis_size(CTX)
    return lax.ppermute(part, CTX, [(i, (i + by) % count) for i in range(count)])


def exchanged(part, low):
    count = lax.axis_size(CTX)
    one, two, three = (lax.ppermute(part, CTX, [(i, i ^ (low * k)) for i in range(count)]) for k in (1, 2, 3))
    return (part + one) + (two + three)


def after(parts, done):
    return lax.optimization_barrier(tuple(parts) + tuple(done))[: len(parts)]


def pack_kernel(k_ref, q_ref, input_ref, grad_ref, low_ref, high_ref, sems):
    block = k_ref.shape[0]
    pairs = [
        (k_ref, low_ref.at[pl.ds(0, block)]),
        (q_ref, high_ref.at[pl.ds(0, block)]),
    ]
    for target, start in ((low_ref, block - EDGE), (high_ref, 0)):
        pairs.append((input_ref.at[pl.ds(start, EDGE)], target.at[pl.ds(block, EDGE)]))
        pairs.append((grad_ref.at[pl.ds(start, EDGE)], target.at[pl.ds(block + EDGE, EDGE)]))
    copies = [pltpu.make_async_copy(source, target, sems.at[i]) for i, (source, target) in enumerate(pairs)]
    for copy in copies:
        copy.start()
    for copy in copies:
        copy.wait()


def pack(keys, queries, inputs, grad):
    block, width = keys.shape
    shape = jax.ShapeDtypeStruct((block + 2 * EDGE, width), keys.dtype)
    return pl.pallas_call(
        pack_kernel,
        in_specs=[pl.BlockSpec(memory_space=pltpu.HBM)] * 4,
        out_specs=[INSIDE] * 2,
        out_shape=[shape, shape],
        scratch_shapes=[pltpu.SemaphoreType.DMA((6,))],
        compiler_params=pltpu.CompilerParams(vmem_limit_bytes=56 * 2**20),
    )(keys, queries, inputs, grad)


def conv_kernel(last, idx_ref, grad_ref, input_ref, low_ref, high_ref, taps_ref, out_ref, rows_ref, gpad, cpad):
    block = grad_ref.shape[0]
    width = grad_ref.shape[1]
    taps_count = taps_ref.shape[0]
    reach = taps_count // 2
    device = idx_ref[0]
    f32 = jnp.float32
    columns = width // HEAD

    @pl.loop(0, columns)
    def _(column):
        lanes = pl.ds(pl.multiple_of(column * HEAD, HEAD), HEAD)
        low = jnp.where(device > 0, low_ref[pl.ds(block, 2 * EDGE), lanes].astype(f32), 0.0)
        high = jnp.where(device < last, high_ref[pl.ds(block, 2 * EDGE), lanes].astype(f32), 0.0)
        grad = grad_ref[:, lanes].astype(f32)
        cpad[:EDGE] = low[:EDGE]
        gpad[:EDGE] = low[EDGE:]
        cpad[EDGE : EDGE + block] = input_ref[:, lanes].astype(f32)
        gpad[EDGE : EDGE + block] = grad
        cpad[EDGE + block :] = high[:EDGE]
        gpad[EDGE + block :] = high[EDGE:]
        taps = taps_ref[:, lanes].astype(f32)
        total = grad
        for tap in range(taps_count):
            total = total + taps[tap : tap + 1] * gpad[pl.ds(EDGE + reach - tap, block), :]
        out_ref[:, lanes] = total.astype(out_ref.dtype)
        grad = gpad[EDGE : EDGE + block]
        for tap in range(taps_count):
            prod = grad * cpad[pl.ds(EDGE - reach + tap, block), :]
            rows_ref[tap : tap + 1, lanes] = jnp.sum(prod, axis=0, keepdims=True)
        rows_ref[taps_count:, lanes] = jnp.zeros_like(rows_ref[taps_count:, lanes])


def conv(device, grad, inputs, low, high, taps, last):
    block, width = grad.shape
    count = taps.shape[0]
    return pl.pallas_call(
        functools.partial(conv_kernel, last),
        in_specs=[pl.BlockSpec(memory_space=pltpu.SMEM)] + [INSIDE] * 5,
        out_specs=[INSIDE] * 2,
        out_shape=[
            jax.ShapeDtypeStruct((block, width), jnp.bfloat16),
            jax.ShapeDtypeStruct((8 * pl.cdiv(count, 8), width), jnp.float32),
        ],
        scratch_shapes=[
            pltpu.VMEM((block + 2 * EDGE, HEAD), jnp.float32),
            pltpu.VMEM((block + 2 * EDGE, HEAD), jnp.float32),
        ],
        compiler_params=pltpu.CompilerParams(vmem_limit_bytes=VMEM_BYTES),
        cost_estimate=pl.CostEstimate(flops=8 * block * width * count, bytes_accessed=4 * block * width, transcendentals=0),
    )(device, grad, inputs, low, high, taps)


def project(tp, own, other, weight):
    full = jnp.where(tp == 0, jnp.concatenate([own, other], axis=1), jnp.concatenate([other, own], axis=1))
    return lax.dot_general(full, weight, NT, preferred_element_type=jnp.float32).astype(jnp.bfloat16)


def query_kernel(scale, idx_ref, q_ref, do_ref, k3, k2, k1, k0, v3, v2, v1, v0, out_ref, stats_ref, bias, columns):
    block = q_ref.shape[0]
    heads = q_ref.shape[1] // HEAD
    f32 = jnp.float32
    rows = lax.broadcasted_iota(jnp.int32, bias.shape, 0)
    cols = lax.broadcasted_iota(jnp.int32, bias.shape, 1)
    valid = (cols <= 3 * block + rows) & (cols >= (3 - idx_ref[0]) * block)
    bias[...] = jnp.where(valid, 0.0, -jnp.inf)
    columns[...] = jnp.zeros_like(columns)

    @pl.loop(0, heads // GROUP)
    def _(step):
        lane = lax.broadcasted_iota(jnp.int32, columns.shape, 1)
        both = columns[...]
        for group in range(GROUP):
            head = step * GROUP + group
            lanes = pl.ds(pl.multiple_of(head * HEAD, HEAD), HEAD)
            keys = jnp.concatenate([ref[pl.ds(0, block), lanes] for ref in (k3, k2, k1, k0)], axis=0)
            values = jnp.concatenate([ref[:, lanes] for ref in (v3, v2, v1, v0)], axis=0)
            scores = lax.dot_general(q_ref[:, lanes], keys, NT, preferred_element_type=f32) * scale + bias[...]
            top = jnp.max(scores, axis=1, keepdims=True)
            expo = jnp.exp(scores - top)
            denom = jnp.sum(expo, axis=1, keepdims=True)
            probs = expo * (1.0 / denom)
            prob_grad = lax.dot_general(do_ref[:, lanes], values, NT, preferred_element_type=f32)
            delta = jnp.sum(probs.astype(jnp.bfloat16).astype(f32) * prob_grad, axis=1, keepdims=True)
            score_grad = (probs * (prob_grad - delta)).astype(jnp.bfloat16)
            out = jnp.dot(score_grad, keys, preferred_element_type=f32) * scale
            out_ref[:, lanes] = out.astype(out_ref.dtype)
            both = jnp.where(lane == head, top + jnp.log(denom), both)
            both = jnp.where(lane == heads + head, delta, both)
        columns[...] = both

    stats_ref[...] = columns[...].T[: stats_ref.shape[0]]


def query_side(device, queries, out_grad, keys, values, scale):
    block, width = queries.shape
    heads = width // HEAD
    return pl.pallas_call(
        functools.partial(query_kernel, scale),
        in_specs=[pl.BlockSpec(memory_space=pltpu.SMEM)] + [INSIDE] * 10,
        out_specs=[INSIDE] * 2,
        out_shape=[
            jax.ShapeDtypeStruct((block, width), jnp.bfloat16),
            jax.ShapeDtypeStruct((2 * heads, block), jnp.float32),
        ],
        scratch_shapes=[
            pltpu.VMEM((block, 4 * block), jnp.float32),
            pltpu.VMEM((block, HEAD), jnp.float32),
        ],
        compiler_params=pltpu.CompilerParams(vmem_limit_bytes=VMEM_BYTES),
        cost_estimate=pl.CostEstimate(
            flops=40 * block * block * width, bytes_accessed=24 * block * width, transcendentals=4 * block * block * heads
        ),
    )(device, queries, out_grad, *keys, *values)


def key_kernel(scale, last, idx_ref, k_ref, v_ref, q0, q1, q2, q3, d0, d1, d2, d3, s0, s1, s2, s3, dk_ref, dv_ref, bias, lse, delta):
    block = k_ref.shape[0]
    heads = lse.shape[0]
    f32 = jnp.float32
    rows = lax.broadcasted_iota(jnp.int32, bias.shape, 0)
    cols = lax.broadcasted_iota(jnp.int32, bias.shape, 1)
    bias[...] = jnp.where(cols >= rows, 0.0, -jnp.inf)
    parts = [s0[...]]
    for hop, ref in enumerate((s1, s2, s3), 1):
        part = ref[...]
        row = lax.broadcasted_iota(jnp.int32, part.shape, 0)
        parts.append(jnp.where((idx_ref[0] + hop > last) & (row < heads), BIG, part))
    stats = jnp.concatenate(parts, axis=1)
    for one in range(heads):
        lse[one] = stats[one : one + 1]
        delta[one] = stats[heads + one : heads + one + 1]
    edge = bias.shape[1]

    @pl.loop(0, heads // GROUP)
    def _(step):
        for group in range(GROUP):
            head = GROUP * step + group
            lanes = pl.ds(pl.multiple_of(head * HEAD, HEAD), HEAD)
            queries = jnp.concatenate([ref[pl.ds(0, block), lanes] for ref in (q0, q1, q2, q3)], axis=0)
            dos = jnp.concatenate([ref[:, lanes] for ref in (d0, d1, d2, d3)], axis=0)
            scores = lax.dot_general(k_ref[:, lanes], queries, NT, preferred_element_type=f32) * scale - lse[head]
            scores = jnp.concatenate([scores[:, :edge] + bias[...], scores[:, edge:]], axis=1)
            probs = jnp.exp(scores)
            prob_grad = lax.dot_general(v_ref[:, lanes], dos, NT, preferred_element_type=f32)
            score_grad = (probs * (prob_grad - delta[head])).astype(jnp.bfloat16)
            dk_ref[:, lanes] = (jnp.dot(score_grad, queries, preferred_element_type=f32) * scale).astype(dk_ref.dtype)
            dv_ref[:, lanes] = jnp.dot(probs.astype(jnp.bfloat16), dos, preferred_element_type=f32).astype(dv_ref.dtype)


def key_side(device, keys, values, queries, out_grads, stats, scale, last):
    block, width = keys.shape
    heads = width // HEAD
    shape = jax.ShapeDtypeStruct((block, width), jnp.bfloat16)
    return pl.pallas_call(
        functools.partial(key_kernel, scale, last),
        in_specs=[pl.BlockSpec(memory_space=pltpu.SMEM)] + [INSIDE] * 14,
        out_specs=[INSIDE] * 2,
        out_shape=[shape, shape],
        scratch_shapes=[
            pltpu.VMEM((block, 256), jnp.float32),
            pltpu.VMEM((heads, 1, 4 * block), jnp.float32),
            pltpu.VMEM((heads, 1, 4 * block), jnp.float32),
        ],
        compiler_params=pltpu.CompilerParams(vmem_limit_bytes=VMEM_BYTES),
        cost_estimate=pl.CostEstimate(
            flops=40 * block * block * width, bytes_accessed=24 * block * width, transcendentals=4 * block * block * heads
        ),
    )(device, keys, values, *queries, *out_grads, *stats)


def per_device(queries, keys, values, stream_grad, conv_input, conv_weight, out_weight):
    block = queries.shape[0]
    last = lax.axis_size(CTX) - 1
    scale = 1.0 / math.sqrt(HEAD)
    device = lax.axis_index(CTX).astype(jnp.int32).reshape(1)
    tp = lax.axis_index("tp")

    low, high = pack(keys, queries, conv_input, stream_grad)
    k1, q1 = rotated(low, 1), rotated(high, -1)
    (first,) = after((values,), (q1,))
    v1 = rotated(first, 1)
    k2, q2 = rotated(k1, 1), rotated(q1, -1)
    v2 = rotated(v1, 1)

    grad_stream, tap_rows = conv(device, stream_grad, conv_input, k1, q1, conv_weight, last)
    other = lax.ppermute(grad_stream, "tp", [(0, 1), (1, 0)])
    tap_rows = tap_rows + lax.ppermute(tap_rows, CTX, [(i, i ^ 1) for i in range(last + 1)])
    tap_rows = exchanged(tap_rows, 2)
    (other,) = after((other,), (k2, q2))
    out_grad = project(tp, grad_stream, other, out_weight)
    k3, q3 = rotated(k2, 1), rotated(q2, -1)
    v3 = rotated(v2, 1)

    (sent,) = after((out_grad,), (v2,))
    d1 = rotated(sent, -1)
    (sent,) = after((d1,), (k3, q3, tap_rows))
    d2 = rotated(sent, -1)
    (sent,) = after((d2,), (v3,))
    d3 = rotated(sent, -1)

    tap_rows = exchanged(tap_rows, 8)
    query_grad, stats = query_side(device, queries, out_grad, (k3, k2, k1, keys), (v3, v2, v1, values), scale)
    (stats,) = after((stats,), (tap_rows,))
    all_stats = [stats] + [rotated(stats, -hop) for hop in (1, 2, 3)]
    (tap_rows,) = after((tap_rows,), (*all_stats[1:], d3))
    tap_rows = exchanged(tap_rows, 32)
    key_grad, value_grad = key_side(
        device, keys, values, (queries, q1, q2, q3), (out_grad, d1, d2, d3), all_stats, scale, last
    )
    kernel_grad = tap_rows[: conv_weight.shape[0]] / math.sqrt(block * (last + 1))
    return (query_grad, key_grad, value_grad, grad_stream, kernel_grad)


def solution(mesh):
    count, pair = mesh.devices.shape
    far = 8
    split = Mesh(mesh.devices.reshape(far, count // far, pair), CTX + ("tp",))
    frames = P(CTX, "tp")
    return jax.shard_map(
        per_device,
        mesh=split,
        in_specs=(frames,) * 5 + (P(None, "tp"), P("tp", None)),
        out_specs=(frames,) * 4 + (P(None, "tp"),),
        check_vma=False,
    )
```

```python
import functools
import math

import jax
import jax.numpy as jnp
from jax import lax
from jax.experimental import pallas as pl
from jax.experimental.pallas import tpu as pltpu
from jax.sharding import Mesh
from jax.sharding import PartitionSpec as P

HEAD = 128
EDGE = 16
NT = (((1,), (1,)), ((), ()))
BIG = 1e30
GROUP = 4
VMEM_BYTES = 24 * 2**20
INSIDE = pl.BlockSpec(memory_space=pltpu.VMEM)
CTX = ("z", "near")


def rotated(part, by):
    count = lax.axis_size(CTX)
    return lax.ppermute(part, CTX, [(i, (i + by) % count) for i in range(count)])


def swapped(part, first):
    count = lax.axis_size(CTX)
    partner = lambda i: ((i - first) ^ 1) + first
    return lax.ppermute(part, CTX, [(i, partner(i) if 0 <= partner(i) < count and i >= first else i) for i in range(count)])


def after(parts, done):
    return lax.optimization_barrier(tuple(parts) + tuple(done))[: len(parts)]


def pack_kernel(idx_ref, k_ref, v_ref, input_ref, grad_ref, both_ref, inside_ref, across_ref, sems):
    block = k_ref.shape[0]
    odd = lax.rem(idx_ref[0], 2)
    pairs = [(k_ref, both_ref.at[pl.ds(0, block)]), (v_ref, both_ref.at[pl.ds(block, block)])]
    for target, start in ((inside_ref, (1 - odd) * (block - EDGE)), (across_ref, odd * (block - EDGE))):
        rows = pl.ds(pl.multiple_of(start, EDGE), EDGE)
        pairs.append((input_ref.at[rows], target.at[pl.ds(0, EDGE)]))
        pairs.append((grad_ref.at[rows], target.at[pl.ds(EDGE, EDGE)]))
    copies = [pltpu.make_async_copy(source, target, sems.at[i]) for i, (source, target) in enumerate(pairs)]
    for copy in copies:
        copy.start()
    for copy in copies:
        copy.wait()


def pack(device, keys, values, inputs, grad):
    block, width = keys.shape
    edge = jax.ShapeDtypeStruct((2 * EDGE, width), keys.dtype)
    return pl.pallas_call(
        pack_kernel,
        in_specs=[pl.BlockSpec(memory_space=pltpu.SMEM)] + [pl.BlockSpec(memory_space=pltpu.HBM)] * 4,
        out_specs=[INSIDE] * 3,
        out_shape=[jax.ShapeDtypeStruct((2 * block, width), keys.dtype), edge, edge],
        scratch_shapes=[pltpu.SemaphoreType.DMA((6,))],
        compiler_params=pltpu.CompilerParams(vmem_limit_bytes=56 * 2**20),
    )(device, keys, values, inputs, grad)


def conv_kernel(last, idx_ref, grad_ref, input_ref, inside_ref, across_ref, taps_ref, out_ref, rows_ref, gpad, cpad):
    block = grad_ref.shape[0]
    width = grad_ref.shape[1]
    taps_count = taps_ref.shape[0]
    reach = taps_count // 2
    device = idx_ref[0]
    f32 = jnp.float32
    columns = width // HEAD

    @pl.loop(0, columns)
    def _(column):
        lanes = pl.ds(pl.multiple_of(column * HEAD, HEAD), HEAD)
        inside = inside_ref[:, lanes].astype(f32)
        across = across_ref[:, lanes].astype(f32)
        even = lax.rem(device, 2) == 0
        low = jnp.where(device > 0, jnp.where(even, across, inside), 0.0)
        high = jnp.where(device < last, jnp.where(even, inside, across), 0.0)
        grad = grad_ref[:, lanes].astype(f32)
        cpad[:EDGE] = low[:EDGE]
        gpad[:EDGE] = low[EDGE:]
        cpad[EDGE : EDGE + block] = input_ref[:, lanes].astype(f32)
        gpad[EDGE : EDGE + block] = grad
        cpad[EDGE + block :] = high[:EDGE]
        gpad[EDGE + block :] = high[EDGE:]
        taps = taps_ref[:, lanes].astype(f32)
        total = grad
        for tap in range(taps_count):
            total = total + taps[tap : tap + 1] * gpad[pl.ds(EDGE + reach - tap, block), :]
        out_ref[:, lanes] = total.astype(out_ref.dtype)
        grad = gpad[EDGE : EDGE + block]
        for tap in range(taps_count):
            prod = grad * cpad[pl.ds(EDGE - reach + tap, block), :]
            rows_ref[tap : tap + 1, lanes] = jnp.sum(prod, axis=0, keepdims=True)
        rows_ref[taps_count:, lanes] = jnp.zeros_like(rows_ref[taps_count:, lanes])


def conv(device, grad, inputs, inside, across, taps, last):
    block, width = grad.shape
    count = taps.shape[0]
    return pl.pallas_call(
        functools.partial(conv_kernel, last),
        in_specs=[pl.BlockSpec(memory_space=pltpu.SMEM)] + [INSIDE] * 5,
        out_specs=[INSIDE] * 2,
        out_shape=[
            jax.ShapeDtypeStruct((block, width), jnp.bfloat16),
            jax.ShapeDtypeStruct((8 * pl.cdiv(count, 8), width), jnp.float32),
        ],
        scratch_shapes=[
            pltpu.VMEM((block + 2 * EDGE, HEAD), jnp.float32),
            pltpu.VMEM((block + 2 * EDGE, HEAD), jnp.float32),
        ],
        compiler_params=pltpu.CompilerParams(vmem_limit_bytes=VMEM_BYTES),
        cost_estimate=pl.CostEstimate(flops=block * width, bytes_accessed=block * width // 16, transcendentals=0),
    )(device, grad, inputs, inside, across, taps)


def project(tp, own, other, weight):
    full = jnp.where(tp == 0, jnp.concatenate([own, other], axis=1), jnp.concatenate([other, own], axis=1))
    return lax.dot_general(full, weight, NT, preferred_element_type=jnp.float32).astype(jnp.bfloat16)


def query_kernel(scale, idx_ref, q_ref, do_ref, both3, both2, both1, both0, out_ref, stats_ref, bias, columns):
    block = q_ref.shape[0]
    heads = q_ref.shape[1] // HEAD
    f32 = jnp.float32
    rows = lax.broadcasted_iota(jnp.int32, bias.shape, 0)
    cols = lax.broadcasted_iota(jnp.int32, bias.shape, 1)
    valid = (cols <= 3 * block + rows) & (cols >= (3 - idx_ref[0]) * block)
    bias[...] = jnp.where(valid, 0.0, -jnp.inf)
    columns[...] = jnp.zeros_like(columns)

    @pl.loop(0, heads // GROUP)
    def _(step):
        lane = lax.broadcasted_iota(jnp.int32, columns.shape, 1)
        both = columns[...]
        for group in range(GROUP):
            head = step * GROUP + group
            lanes = pl.ds(pl.multiple_of(head * HEAD, HEAD), HEAD)
            keys, values = (
                jnp.concatenate([ref[pl.ds(start, block), lanes] for ref in (both3, both2, both1, both0)], axis=0)
                for start in (0, block)
            )
            scores = lax.dot_general(q_ref[:, lanes], keys, NT, preferred_element_type=f32) * scale + bias[...]
            top = jnp.max(scores, axis=1, keepdims=True)
            expo = jnp.exp(scores - top)
            denom = jnp.sum(expo, axis=1, keepdims=True)
            probs = expo * (1.0 / denom)
            prob_grad = lax.dot_general(do_ref[:, lanes], values, NT, preferred_element_type=f32)
            delta = jnp.sum(probs.astype(jnp.bfloat16).astype(f32) * prob_grad, axis=1, keepdims=True)
            score_grad = (probs * (prob_grad - delta)).astype(jnp.bfloat16)
            out = jnp.dot(score_grad, keys, preferred_element_type=f32) * scale
            out_ref[:, lanes] = out.astype(out_ref.dtype)
            both = jnp.where(lane == head, top + jnp.log(denom), both)
            both = jnp.where(lane == heads + head, delta, both)
        columns[...] = both

    stats_ref[...] = columns[...].T[: stats_ref.shape[0]]


def query_side(device, queries, out_grad, blocks, scale):
    block, width = queries.shape
    heads = width // HEAD
    return pl.pallas_call(
        functools.partial(query_kernel, scale),
        in_specs=[pl.BlockSpec(memory_space=pltpu.SMEM)] + [INSIDE] * 6,
        out_specs=[INSIDE] * 2,
        out_shape=[
            jax.ShapeDtypeStruct((block, width), jnp.bfloat16),
            jax.ShapeDtypeStruct((2 * heads, block), jnp.float32),
        ],
        scratch_shapes=[
            pltpu.VMEM((block, 4 * block), jnp.float32),
            pltpu.VMEM((block, HEAD), jnp.float32),
        ],
        compiler_params=pltpu.CompilerParams(vmem_limit_bytes=VMEM_BYTES),
        cost_estimate=pl.CostEstimate(
            flops=40 * block * block * width, bytes_accessed=24 * block * width, transcendentals=4 * block * block * heads
        ),
    )(device, queries, out_grad, *blocks)


def key_kernel(scale, last, idx_ref, both_ref, q0, q1, q2, q3, d0, d1, d2, d3, s0, s1, s2, s3, dk_ref, dv_ref, bias, lse, delta):
    block = q0.shape[0]
    heads = lse.shape[0]
    f32 = jnp.float32
    rows = lax.broadcasted_iota(jnp.int32, bias.shape, 0)
    cols = lax.broadcasted_iota(jnp.int32, bias.shape, 1)
    bias[...] = jnp.where(cols >= rows, 0.0, -jnp.inf)
    parts = [s0[...]]
    for hop, ref in enumerate((s1, s2, s3), 1):
        part = ref[...]
        row = lax.broadcasted_iota(jnp.int32, part.shape, 0)
        parts.append(jnp.where((idx_ref[0] + hop > last) & (row < heads), BIG, part))
    stats = jnp.concatenate(parts, axis=1)
    for one in range(heads):
        lse[one] = stats[one : one + 1]
        delta[one] = stats[heads + one : heads + one + 1]
    edge = bias.shape[1]

    @pl.loop(0, heads // GROUP)
    def _(step):
        for group in range(GROUP):
            head = GROUP * step + group
            lanes = pl.ds(pl.multiple_of(head * HEAD, HEAD), HEAD)
            queries = jnp.concatenate([ref[:, lanes] for ref in (q0, q1, q2, q3)], axis=0)
            dos = jnp.concatenate([ref[:, lanes] for ref in (d0, d1, d2, d3)], axis=0)
            scores = lax.dot_general(both_ref[pl.ds(0, block), lanes], queries, NT, preferred_element_type=f32) * scale - lse[head]
            scores = jnp.concatenate([scores[:, :edge] + bias[...], scores[:, edge:]], axis=1)
            probs = jnp.exp(scores)
            prob_grad = lax.dot_general(both_ref[pl.ds(block, block), lanes], dos, NT, preferred_element_type=f32)
            score_grad = (probs * (prob_grad - delta[head])).astype(jnp.bfloat16)
            dk_ref[:, lanes] = (jnp.dot(score_grad, queries, preferred_element_type=f32) * scale).astype(dk_ref.dtype)
            dv_ref[:, lanes] = jnp.dot(probs.astype(jnp.bfloat16), dos, preferred_element_type=f32).astype(dv_ref.dtype)


def key_side(device, both, queries, out_grads, stats, scale, last):
    block, width = queries[0].shape
    heads = width // HEAD
    shape = jax.ShapeDtypeStruct((block, width), jnp.bfloat16)
    return pl.pallas_call(
        functools.partial(key_kernel, scale, last),
        in_specs=[pl.BlockSpec(memory_space=pltpu.SMEM)] + [INSIDE] * 13,
        out_specs=[INSIDE] * 2,
        out_shape=[shape, shape],
        scratch_shapes=[
            pltpu.VMEM((block, 256), jnp.float32),
            pltpu.VMEM((heads, 1, 4 * block), jnp.float32),
            pltpu.VMEM((heads, 1, 4 * block), jnp.float32),
        ],
        compiler_params=pltpu.CompilerParams(vmem_limit_bytes=VMEM_BYTES),
        cost_estimate=pl.CostEstimate(
            flops=40 * block * block * width, bytes_accessed=24 * block * width, transcendentals=4 * block * block * heads
        ),
    )(device, both, *queries, *out_grads, *stats)


def per_device(queries, keys, values, stream_grad, conv_input, conv_weight, out_weight):
    block = queries.shape[0]
    last = lax.axis_size(CTX) - 1
    scale = 1.0 / math.sqrt(HEAD)
    device = lax.axis_index(CTX).astype(jnp.int32).reshape(1)
    tp = lax.axis_index("tp")

    kv0, inside, across = pack(device, keys, values, conv_input, stream_grad)
    inside, across = swapped(inside, 0), swapped(across, 1)
    kv1, q1 = rotated(kv0, 1), rotated(queries, -1)
    q2 = rotated(q1, -1)
    q3 = rotated(q2, -1)

    grad_stream, tap_rows = conv(device, stream_grad, conv_input, inside, across, conv_weight, last)
    near_rows = lax.all_gather(tap_rows, "near", axis=0)
    other = lax.ppermute(grad_stream, "tp", [(0, 1), (1, 0)])
    other, sent = lax.optimization_barrier((other, kv1))
    kv2 = rotated(sent, 1)
    out_grad = project(tp, grad_stream, other, out_weight)
    (sent,) = after((kv2,), (out_grad, q1))
    kv3 = rotated(sent, 1)
    (sent,) = after((out_grad,), (q1,))
    d1 = rotated(sent, -1)
    (sent,) = after((d1,), (kv2, q2))
    d2 = rotated(sent, -1)
    d3 = rotated(d2, -1)

    (near_rows,) = after((near_rows,), (kv3, d2, q2))
    all_rows = lax.all_gather(jnp.sum(near_rows, axis=0), "z", axis=0)
    query_grad, stats = query_side(device, queries, out_grad, (kv3, kv2, kv1, kv0), scale)
    all_stats = [stats] + [rotated(stats, -hop) for hop in (1, 2, 3)]
    key_grad, value_grad = key_side(device, kv0, (queries, q1, q2, q3), (out_grad, d1, d2, d3), all_stats, scale, last)
    tap_rows = jnp.sum(all_rows, axis=0)[: conv_weight.shape[0]]
    kernel_grad = tap_rows / math.sqrt(block * (last + 1))
    return (query_grad, key_grad, value_grad, grad_stream, kernel_grad)


def solution(mesh):
    count, pair = mesh.devices.shape
    far = 8
    split = Mesh(mesh.devices.reshape(far, count // far, pair), CTX + ("tp",))
    frames = P(CTX, "tp")
    return jax.shard_map(
        per_device,
        mesh=split,
        in_specs=(frames,) * 5 + (P(None, "tp"), P("tp", None)),
        out_specs=(frames,) * 4 + (P(None, "tp"),),
        check_vma=False,
    )
```

```python
import functools
import math

import jax
import jax.numpy as jnp
from jax import lax
from jax.experimental import pallas as pl
from jax.experimental.pallas import tpu as pltpu
from jax.sharding import Mesh
from jax.sharding import PartitionSpec as P

HEAD = 128
EDGE = 16
NT = (((1,), (1,)), ((), ()))
BIG = 1e30
GROUP = 4
VMEM_BYTES = 24 * 2**20
INSIDE = pl.BlockSpec(memory_space=pltpu.VMEM)
CTX = ("z", "near")


def rotated(part, by):
    count = lax.axis_size(CTX)
    return lax.ppermute(part, CTX, [(i, (i + by) % count) for i in range(count)])


def swapped(part, first):
    count = lax.axis_size(CTX)
    partner = lambda i: ((i - first) ^ 1) + first
    return lax.ppermute(part, CTX, [(i, partner(i) if 0 <= partner(i) < count and i >= first else i) for i in range(count)])


def after(parts, done):
    return lax.optimization_barrier(tuple(parts) + tuple(done))[: len(parts)]


def pack_kernel(idx_ref, k_ref, v_ref, input_ref, grad_ref, both_ref, inside_ref, across_ref, sems):
    block = k_ref.shape[0]
    odd = lax.rem(idx_ref[0], 2)
    pairs = [(k_ref, both_ref.at[pl.ds(0, block)]), (v_ref, both_ref.at[pl.ds(block, block)])]
    for target, start in ((inside_ref, (1 - odd) * (block - EDGE)), (across_ref, odd * (block - EDGE))):
        rows = pl.ds(pl.multiple_of(start, EDGE), EDGE)
        pairs.append((input_ref.at[rows], target.at[pl.ds(0, EDGE)]))
        pairs.append((grad_ref.at[rows], target.at[pl.ds(EDGE, EDGE)]))
    copies = [pltpu.make_async_copy(source, target, sems.at[i]) for i, (source, target) in enumerate(pairs)]
    for copy in copies:
        copy.start()
    for copy in copies:
        copy.wait()


def pack(device, keys, values, inputs, grad):
    block, width = keys.shape
    edge = jax.ShapeDtypeStruct((2 * EDGE, width), keys.dtype)
    return pl.pallas_call(
        pack_kernel,
        in_specs=[pl.BlockSpec(memory_space=pltpu.SMEM)] + [pl.BlockSpec(memory_space=pltpu.HBM)] * 4,
        out_specs=[INSIDE] * 3,
        out_shape=[jax.ShapeDtypeStruct((2 * block, width), keys.dtype), edge, edge],
        scratch_shapes=[pltpu.SemaphoreType.DMA((6,))],
        compiler_params=pltpu.CompilerParams(vmem_limit_bytes=56 * 2**20),
    )(device, keys, values, inputs, grad)


def conv_back(padded, grad, taps):
    block = grad.shape[0]
    taps_count = taps.shape[0]
    total = grad
    for tap in range(taps_count):
        total = total + taps[tap : tap + 1] * padded[pl.ds(EDGE + taps_count // 2 - tap, block), :]
    return total


def conv_kernel(last, idx_ref, grad_ref, input_ref, inside_ref, across_ref, taps_ref, out_ref, rows_ref, gpad, cpad):
    block = grad_ref.shape[0]
    taps_count = taps_ref.shape[0]
    device = idx_ref[0]
    even = lax.rem(device, 2) == 0
    f32 = jnp.float32

    @pl.loop(0, grad_ref.shape[1] // HEAD)
    def _(column):
        lanes = pl.ds(pl.multiple_of(column * HEAD, HEAD), HEAD)
        inside = inside_ref[:, lanes].astype(f32)
        across = across_ref[:, lanes].astype(f32)
        low = jnp.where(device > 0, jnp.where(even, across, inside), 0.0)
        high = jnp.where(device < last, jnp.where(even, inside, across), 0.0)
        grad = grad_ref[:, lanes].astype(f32)
        cpad[:EDGE] = low[:EDGE]
        gpad[:EDGE] = low[EDGE:]
        cpad[EDGE : EDGE + block] = input_ref[:, lanes].astype(f32)
        gpad[EDGE : EDGE + block] = grad
        cpad[EDGE + block :] = high[:EDGE]
        gpad[EDGE + block :] = high[EDGE:]
        out_ref[:, lanes] = conv_back(gpad, grad, taps_ref[:, lanes].astype(f32)).astype(out_ref.dtype)
        grad = gpad[EDGE : EDGE + block]
        for tap in range(taps_count):
            prod = grad * cpad[pl.ds(EDGE - taps_count // 2 + tap, block), :]
            rows_ref[column, tap : tap + 1, :] = jnp.sum(prod, axis=0, keepdims=True)
        rows_ref[column, taps_count:, :] = jnp.zeros_like(rows_ref[column, taps_count:, :])


def conv(device, grad, inputs, inside, across, taps, last):
    block, width = grad.shape
    count = taps.shape[0]
    return pl.pallas_call(
        functools.partial(conv_kernel, last),
        in_specs=[pl.BlockSpec(memory_space=pltpu.SMEM)] + [INSIDE] * 5,
        out_specs=[INSIDE] * 2,
        out_shape=[
            jax.ShapeDtypeStruct((block, width), jnp.bfloat16),
            jax.ShapeDtypeStruct((width // HEAD, 8 * pl.cdiv(count, 8), HEAD), jnp.float32),
        ],
        scratch_shapes=[pltpu.VMEM((block + 2 * EDGE, HEAD), jnp.float32)] * 2,
        compiler_params=pltpu.CompilerParams(vmem_limit_bytes=VMEM_BYTES),
        cost_estimate=pl.CostEstimate(flops=block * width, bytes_accessed=block * width // 16, transcendentals=0),
    )(device, grad, inputs, inside, across, taps)


def other_kernel(last, count, idx_ref, grad_ref, edges_ref, out_ref, gpad):
    block = grad_ref.shape[0]
    device = idx_ref[0]
    even = lax.rem(device, 2) == 0
    f32 = jnp.float32

    @pl.loop(0, grad_ref.shape[1] // HEAD)
    def _(column):
        lanes = pl.ds(pl.multiple_of(column * HEAD, HEAD), HEAD)
        edges = edges_ref[:, lanes].astype(f32)
        inside, across = edges[:EDGE], edges[EDGE : 2 * EDGE]
        grad = grad_ref[:, lanes].astype(f32)
        gpad[:EDGE] = jnp.where(device > 0, jnp.where(even, across, inside), 0.0)
        gpad[EDGE : EDGE + block] = grad
        gpad[EDGE + block :] = jnp.where(device < last, jnp.where(even, inside, across), 0.0)
        out_ref[:, lanes] = conv_back(gpad, grad, edges[2 * EDGE : 2 * EDGE + count]).astype(out_ref.dtype)


def conv_other(device, grad, edges, count, last):
    block, width = grad.shape
    return pl.pallas_call(
        functools.partial(other_kernel, last, count),
        in_specs=[pl.BlockSpec(memory_space=pltpu.SMEM)] + [INSIDE] * 2,
        out_specs=INSIDE,
        out_shape=jax.ShapeDtypeStruct((block, width), jnp.bfloat16),
        scratch_shapes=[pltpu.VMEM((block + 2 * EDGE, HEAD), jnp.float32)],
        compiler_params=pltpu.CompilerParams(vmem_limit_bytes=VMEM_BYTES),
        cost_estimate=pl.CostEstimate(flops=block * width, bytes_accessed=block * width // 16, transcendentals=0),
    )(device, grad, edges)


def project(tp, own, other, weight):
    full = jnp.where(tp == 0, jnp.concatenate([own, other], axis=1), jnp.concatenate([other, own], axis=1))
    return lax.dot_general(full, weight, NT, preferred_element_type=jnp.float32).astype(jnp.bfloat16)


def query_kernel(scale, idx_ref, q_ref, do_ref, both3, both2, both1, both0, out_ref, stats_ref, bias, columns):
    block = q_ref.shape[0]
    heads = q_ref.shape[1] // HEAD
    f32 = jnp.float32
    rows = lax.broadcasted_iota(jnp.int32, bias.shape, 0)
    cols = lax.broadcasted_iota(jnp.int32, bias.shape, 1)
    valid = (cols <= 3 * block + rows) & (cols >= (3 - idx_ref[0]) * block)
    bias[...] = jnp.where(valid, 0.0, -jnp.inf)
    columns[...] = jnp.zeros_like(columns)

    @pl.loop(0, heads // GROUP)
    def _(step):
        lane = lax.broadcasted_iota(jnp.int32, columns.shape, 1)
        both = columns[...]
        for group in range(GROUP):
            head = step * GROUP + group
            lanes = pl.ds(pl.multiple_of(head * HEAD, HEAD), HEAD)
            keys, values = (
                jnp.concatenate([ref[pl.ds(start, block), lanes] for ref in (both3, both2, both1, both0)], axis=0)
                for start in (0, block)
            )
            scores = lax.dot_general(q_ref[:, lanes], keys, NT, preferred_element_type=f32) * scale + bias[...]
            top = jnp.max(scores, axis=1, keepdims=True)
            expo = jnp.exp(scores - top)
            denom = jnp.sum(expo, axis=1, keepdims=True)
            probs = expo * (1.0 / denom)
            prob_grad = lax.dot_general(do_ref[:, lanes], values, NT, preferred_element_type=f32)
            delta = jnp.sum(probs.astype(jnp.bfloat16).astype(f32) * prob_grad, axis=1, keepdims=True)
            score_grad = (probs * (prob_grad - delta)).astype(jnp.bfloat16)
            out = jnp.dot(score_grad, keys, preferred_element_type=f32) * scale
            out_ref[:, lanes] = out.astype(out_ref.dtype)
            both = jnp.where(lane == head, top + jnp.log(denom), both)
            both = jnp.where(lane == heads + head, delta, both)
        columns[...] = both

    stats_ref[...] = columns[...].T[: stats_ref.shape[0]]


def query_side(device, queries, out_grad, blocks, scale):
    block, width = queries.shape
    heads = width // HEAD
    return pl.pallas_call(
        functools.partial(query_kernel, scale),
        in_specs=[pl.BlockSpec(memory_space=pltpu.SMEM)] + [INSIDE] * 6,
        out_specs=[INSIDE] * 2,
        out_shape=[
            jax.ShapeDtypeStruct((block, width), jnp.bfloat16),
            jax.ShapeDtypeStruct((2 * heads, block), jnp.float32),
        ],
        scratch_shapes=[
            pltpu.VMEM((block, 4 * block), jnp.float32),
            pltpu.VMEM((block, HEAD), jnp.float32),
        ],
        compiler_params=pltpu.CompilerParams(vmem_limit_bytes=VMEM_BYTES),
        cost_estimate=pl.CostEstimate(
            flops=40 * block * block * width, bytes_accessed=24 * block * width, transcendentals=4 * block * block * heads
        ),
    )(device, queries, out_grad, *blocks)


def key_kernel(scale, last, idx_ref, both_ref, q0, q1, q2, q3, d0, d1, d2, d3, s0, s1, s2, s3, dk_ref, dv_ref, bias, lse, delta):
    block = q0.shape[0]
    heads = lse.shape[0]
    f32 = jnp.float32
    rows = lax.broadcasted_iota(jnp.int32, bias.shape, 0)
    cols = lax.broadcasted_iota(jnp.int32, bias.shape, 1)
    bias[...] = jnp.where(cols >= rows, 0.0, -jnp.inf)
    parts = [s0[...]]
    for hop, ref in enumerate((s1, s2, s3), 1):
        part = ref[...]
        row = lax.broadcasted_iota(jnp.int32, part.shape, 0)
        parts.append(jnp.where((idx_ref[0] + hop > last) & (row < heads), BIG, part))
    stats = jnp.concatenate(parts, axis=1)
    for one in range(heads):
        lse[one] = stats[one : one + 1]
        delta[one] = stats[heads + one : heads + one + 1]
    edge = bias.shape[1]

    @pl.loop(0, heads // GROUP)
    def _(step):
        for group in range(GROUP):
            head = GROUP * step + group
            lanes = pl.ds(pl.multiple_of(head * HEAD, HEAD), HEAD)
            queries = jnp.concatenate([ref[:, lanes] for ref in (q0, q1, q2, q3)], axis=0)
            dos = jnp.concatenate([ref[:, lanes] for ref in (d0, d1, d2, d3)], axis=0)
            scores = lax.dot_general(both_ref[pl.ds(0, block), lanes], queries, NT, preferred_element_type=f32) * scale - lse[head]
            scores = jnp.concatenate([scores[:, :edge] + bias[...], scores[:, edge:]], axis=1)
            probs = jnp.exp(scores)
            prob_grad = lax.dot_general(both_ref[pl.ds(block, block), lanes], dos, NT, preferred_element_type=f32)
            score_grad = (probs * (prob_grad - delta[head])).astype(jnp.bfloat16)
            dk_ref[:, lanes] = (jnp.dot(score_grad, queries, preferred_element_type=f32) * scale).astype(dk_ref.dtype)
            dv_ref[:, lanes] = jnp.dot(probs.astype(jnp.bfloat16), dos, preferred_element_type=f32).astype(dv_ref.dtype)


def key_side(device, both, queries, out_grads, stats, scale, last):
    block, width = queries[0].shape
    heads = width // HEAD
    shape = jax.ShapeDtypeStruct((block, width), jnp.bfloat16)
    return pl.pallas_call(
        functools.partial(key_kernel, scale, last),
        in_specs=[pl.BlockSpec(memory_space=pltpu.SMEM)] + [INSIDE] * 13,
        out_specs=[INSIDE] * 2,
        out_shape=[shape, shape],
        scratch_shapes=[
            pltpu.VMEM((block, 256), jnp.float32),
            pltpu.VMEM((heads, 1, 4 * block), jnp.float32),
            pltpu.VMEM((heads, 1, 4 * block), jnp.float32),
        ],
        compiler_params=pltpu.CompilerParams(vmem_limit_bytes=VMEM_BYTES),
        cost_estimate=pl.CostEstimate(
            flops=40 * block * block * width, bytes_accessed=24 * block * width, transcendentals=4 * block * block * heads
        ),
    )(device, both, *queries, *out_grads, *stats)


def per_device(queries, keys, values, stream_grad, conv_input, conv_weight, out_weight):
    block = queries.shape[0]
    last = lax.axis_size(CTX) - 1
    scale = 1.0 / math.sqrt(HEAD)
    device = lax.axis_index(CTX).astype(jnp.int32).reshape(1)
    tp = lax.axis_index("tp")

    pair = [(0, 1), (1, 0)]
    kv0, inside, across = pack(device, keys, values, conv_input, stream_grad)
    inside, across = swapped(inside, 0), swapped(across, 1)
    other = lax.ppermute(stream_grad, "tp", pair)
    (sent,) = after((kv0,), (across,))
    kv1, q1 = rotated(sent, 1), rotated(queries, -1)
    q2 = rotated(q1, -1)
    q3 = rotated(q2, -1)

    taps_count = conv_weight.shape[0]
    padding = jnp.zeros((2 * EDGE - taps_count, conv_weight.shape[1]), conv_weight.dtype)
    edges = lax.ppermute(jnp.concatenate([inside[EDGE:], across[EDGE:], conv_weight, padding], axis=0), "tp", pair)
    grad_stream, tap_rows = conv(device, stream_grad, conv_input, inside, across, conv_weight, last)
    other, edges, sent = after((other, edges, kv1), (q1, grad_stream))
    kv2 = rotated(sent, 1)
    out_grad = project(tp, grad_stream, conv_other(device, other, edges, taps_count, last), out_weight)
    (sent,) = after((kv2,), (out_grad, q1))
    kv3 = rotated(sent, 1)

    (tap_rows,) = after((tap_rows,), (kv1,))
    tap_sums = jnp.sum(lax.all_to_all(tap_rows, "z", 0, 0, tiled=True), axis=0)
    d1 = rotated(out_grad, -1)
    (sent,) = after((d1,), (kv2, q2, tap_sums))
    d2 = rotated(sent, -1)
    copies = jnp.broadcast_to(tap_sums, (lax.axis_size("near"),) + tap_sums.shape)
    (copies,) = after((copies,), (d1,))
    tap_sums = jnp.sum(lax.all_to_all(copies, "near", 0, 0, tiled=True), axis=0)
    (sent,) = after((d2,), (kv3, q3))
    d3 = rotated(sent, -1)

    (near,) = after((queries,), (tap_sums,))
    query_grad, stats = query_side(device, near, out_grad, (kv3, kv2, kv1, kv0), scale)
    all_stats = [stats] + [rotated(stats, -hop) for hop in (1, 2, 3)]
    copies = jnp.broadcast_to(tap_sums, (lax.axis_size("z"),) + tap_sums.shape)
    (copies,) = after((copies,), (*all_stats[1:], d3))
    tap_sums = lax.all_to_all(copies, "z", 0, 0, tiled=True)
    key_grad, value_grad = key_side(device, kv0, (queries, q1, q2, q3), (out_grad, d1, d2, d3), all_stats, scale, last)
    rows = jnp.transpose(tap_sums, (1, 0, 2)).reshape(tap_sums.shape[1], -1)[:taps_count]
    kernel_grad = rows / math.sqrt(block * (last + 1))
    return (query_grad, key_grad, value_grad, grad_stream, kernel_grad)


def solution(mesh):
    count, pair = mesh.devices.shape
    far = 8
    split = Mesh(mesh.devices.reshape(far, count // far, pair), CTX + ("tp",))
    frames = P(CTX, "tp")
    return jax.shard_map(
        per_device,
        mesh=split,
        in_specs=(frames,) * 5 + (P(None, "tp"), P("tp", None)),
        out_specs=(frames,) * 4 + (P(None, "tp"),),
        check_vma=False,
    )
```

```python
import functools
import math

import jax
import jax.numpy as jnp
from jax import lax
from jax.experimental import pallas as pl
from jax.experimental.pallas import tpu as pltpu
from jax.sharding import Mesh
from jax.sharding import PartitionSpec as P

HEAD = 128
EDGE = 16
NT = (((1,), (1,)), ((), ()))
BIG = 1e30
GROUP = 4
VMEM_BYTES = 24 * 2**20
INSIDE = pl.BlockSpec(memory_space=pltpu.VMEM)
CTX = ("z", "near")


def rotated(part, by):
    count = lax.axis_size(CTX)
    return lax.ppermute(part, CTX, [(i, (i + by) % count) for i in range(count)])


def exchanged(part, by):
    count = lax.axis_size(CTX)
    return part + lax.ppermute(part, CTX, [(i, i ^ by) for i in range(count)])


def swapped(part, first):
    count = lax.axis_size(CTX)
    partner = lambda i: ((i - first) ^ 1) + first
    return lax.ppermute(part, CTX, [(i, partner(i) if 0 <= partner(i) < count and i >= first else i) for i in range(count)])


def after(parts, done):
    return lax.optimization_barrier(tuple(parts) + tuple(done))[: len(parts)]


def pack_kernel(idx_ref, k_ref, v_ref, input_ref, grad_ref, both_ref, inside_ref, across_ref, sems):
    block = k_ref.shape[0]
    odd = lax.rem(idx_ref[0], 2)
    pairs = [(k_ref, both_ref.at[pl.ds(0, block)]), (v_ref, both_ref.at[pl.ds(block, block)])]
    for target, start in ((inside_ref, (1 - odd) * (block - EDGE)), (across_ref, odd * (block - EDGE))):
        rows = pl.ds(pl.multiple_of(start, EDGE), EDGE)
        pairs.append((input_ref.at[rows], target.at[pl.ds(0, EDGE)]))
        pairs.append((grad_ref.at[rows], target.at[pl.ds(EDGE, EDGE)]))
    copies = [pltpu.make_async_copy(source, target, sems.at[i]) for i, (source, target) in enumerate(pairs)]
    for copy in copies:
        copy.start()
    for copy in copies:
        copy.wait()


def pack(device, keys, values, inputs, grad):
    block, width = keys.shape
    edge = jax.ShapeDtypeStruct((2 * EDGE, width), keys.dtype)
    return pl.pallas_call(
        pack_kernel,
        in_specs=[pl.BlockSpec(memory_space=pltpu.SMEM)] + [pl.BlockSpec(memory_space=pltpu.HBM)] * 4,
        out_specs=[INSIDE] * 3,
        out_shape=[jax.ShapeDtypeStruct((2 * block, width), keys.dtype), edge, edge],
        scratch_shapes=[pltpu.SemaphoreType.DMA((6,))],
        compiler_params=pltpu.CompilerParams(vmem_limit_bytes=56 * 2**20),
    )(device, keys, values, inputs, grad)


def conv_back(padded, grad, taps):
    block = grad.shape[0]
    taps_count = taps.shape[0]
    total = grad
    for tap in range(taps_count):
        total = total + taps[tap : tap + 1] * padded[pl.ds(EDGE + taps_count // 2 - tap, block), :]
    return total


def conv_kernel(last, idx_ref, grad_ref, input_ref, inside_ref, across_ref, taps_ref, out_ref, rows_ref, gpad, cpad):
    block = grad_ref.shape[0]
    taps_count = taps_ref.shape[0]
    device = idx_ref[0]
    even = lax.rem(device, 2) == 0
    f32 = jnp.float32

    @pl.loop(0, grad_ref.shape[1] // HEAD)
    def _(column):
        lanes = pl.ds(pl.multiple_of(column * HEAD, HEAD), HEAD)
        inside = inside_ref[:, lanes].astype(f32)
        across = across_ref[:, lanes].astype(f32)
        low = jnp.where(device > 0, jnp.where(even, across, inside), 0.0)
        high = jnp.where(device < last, jnp.where(even, inside, across), 0.0)
        grad = grad_ref[:, lanes].astype(f32)
        cpad[:EDGE] = low[:EDGE]
        gpad[:EDGE] = low[EDGE:]
        cpad[EDGE : EDGE + block] = input_ref[:, lanes].astype(f32)
        gpad[EDGE : EDGE + block] = grad
        cpad[EDGE + block :] = high[:EDGE]
        gpad[EDGE + block :] = high[EDGE:]
        out_ref[:, lanes] = conv_back(gpad, grad, taps_ref[:, lanes].astype(f32)).astype(out_ref.dtype)
        grad = gpad[EDGE : EDGE + block]
        for tap in range(taps_count):
            prod = grad * cpad[pl.ds(EDGE - taps_count // 2 + tap, block), :]
            rows_ref[tap : tap + 1, lanes] = jnp.sum(prod, axis=0, keepdims=True)
        rows_ref[taps_count:, lanes] = jnp.zeros_like(rows_ref[taps_count:, lanes])


def conv(device, grad, inputs, inside, across, taps, last):
    block, width = grad.shape
    count = taps.shape[0]
    return pl.pallas_call(
        functools.partial(conv_kernel, last),
        in_specs=[pl.BlockSpec(memory_space=pltpu.SMEM)] + [INSIDE] * 5,
        out_specs=[INSIDE] * 2,
        out_shape=[
            jax.ShapeDtypeStruct((block, width), jnp.bfloat16),
            jax.ShapeDtypeStruct((8 * pl.cdiv(count, 8), width), jnp.float32),
        ],
        scratch_shapes=[pltpu.VMEM((block + 2 * EDGE, HEAD), jnp.float32)] * 2,
        compiler_params=pltpu.CompilerParams(vmem_limit_bytes=VMEM_BYTES),
        cost_estimate=pl.CostEstimate(flops=block * width, bytes_accessed=block * width // 16, transcendentals=0),
    )(device, grad, inputs, inside, across, taps)


def other_kernel(last, count, idx_ref, grad_ref, edges_ref, out_ref, gpad):
    block = grad_ref.shape[0]
    device = idx_ref[0]
    even = lax.rem(device, 2) == 0
    f32 = jnp.float32

    @pl.loop(0, grad_ref.shape[1] // HEAD)
    def _(column):
        lanes = pl.ds(pl.multiple_of(column * HEAD, HEAD), HEAD)
        edges = edges_ref[:, lanes].astype(f32)
        inside, across = edges[:EDGE], edges[EDGE : 2 * EDGE]
        grad = grad_ref[:, lanes].astype(f32)
        gpad[:EDGE] = jnp.where(device > 0, jnp.where(even, across, inside), 0.0)
        gpad[EDGE : EDGE + block] = grad
        gpad[EDGE + block :] = jnp.where(device < last, jnp.where(even, inside, across), 0.0)
        out_ref[:, lanes] = conv_back(gpad, grad, edges[2 * EDGE : 2 * EDGE + count]).astype(out_ref.dtype)


def conv_other(device, grad, edges, count, last):
    block, width = grad.shape
    return pl.pallas_call(
        functools.partial(other_kernel, last, count),
        in_specs=[pl.BlockSpec(memory_space=pltpu.SMEM)] + [INSIDE] * 2,
        out_specs=INSIDE,
        out_shape=jax.ShapeDtypeStruct((block, width), jnp.bfloat16),
        scratch_shapes=[pltpu.VMEM((block + 2 * EDGE, HEAD), jnp.float32)],
        compiler_params=pltpu.CompilerParams(vmem_limit_bytes=VMEM_BYTES),
        cost_estimate=pl.CostEstimate(flops=block * width, bytes_accessed=block * width // 16, transcendentals=0),
    )(device, grad, edges)


def project(tp, own, other, weight):
    full = jnp.where(tp == 0, jnp.concatenate([own, other], axis=1), jnp.concatenate([other, own], axis=1))
    full = lax.optimization_barrier(full)
    return lax.dot_general(full, weight, NT, preferred_element_type=jnp.float32).astype(jnp.bfloat16)


def query_kernel(scale, idx_ref, q_ref, do_ref, both3, both2, both1, both0, out_ref, stats_ref, bias, columns):
    block = q_ref.shape[0]
    heads = q_ref.shape[1] // HEAD
    f32 = jnp.float32
    rows = lax.broadcasted_iota(jnp.int32, bias.shape, 0)
    cols = lax.broadcasted_iota(jnp.int32, bias.shape, 1)
    valid = (cols <= 3 * block + rows) & (cols >= (3 - idx_ref[0]) * block)
    bias[...] = jnp.where(valid, 0.0, -jnp.inf)
    columns[...] = jnp.zeros_like(columns)

    @pl.loop(0, heads // GROUP)
    def _(step):
        lane = lax.broadcasted_iota(jnp.int32, columns.shape, 1)
        both = columns[...]
        for group in range(GROUP):
            head = step * GROUP + group
            lanes = pl.ds(pl.multiple_of(head * HEAD, HEAD), HEAD)
            keys, values = (
                jnp.concatenate([ref[pl.ds(start, block), lanes] for ref in (both3, both2, both1, both0)], axis=0)
                for start in (0, block)
            )
            scores = lax.dot_general(q_ref[:, lanes], keys, NT, preferred_element_type=f32) * scale + bias[...]
            top = jnp.max(scores, axis=1, keepdims=True)
            expo = jnp.exp(scores - top)
            denom = jnp.sum(expo, axis=1, keepdims=True)
            probs = expo * (1.0 / denom)
            prob_grad = lax.dot_general(do_ref[:, lanes], values, NT, preferred_element_type=f32)
            delta = jnp.sum(probs.astype(jnp.bfloat16).astype(f32) * prob_grad, axis=1, keepdims=True)
            score_grad = (probs * (prob_grad - delta)).astype(jnp.bfloat16)
            out = jnp.dot(score_grad, keys, preferred_element_type=f32) * scale
            out_ref[:, lanes] = out.astype(out_ref.dtype)
            both = jnp.where(lane == head, top + jnp.log(denom), both)
            both = jnp.where(lane == heads + head, delta, both)
        columns[...] = both

    stats_ref[...] = columns[...].T[: stats_ref.shape[0]]


def query_side(device, queries, out_grad, blocks, scale):
    block, width = queries.shape
    heads = width // HEAD
    return pl.pallas_call(
        functools.partial(query_kernel, scale),
        in_specs=[pl.BlockSpec(memory_space=pltpu.SMEM)] + [INSIDE] * 6,
        out_specs=[INSIDE] * 2,
        out_shape=[
            jax.ShapeDtypeStruct((block, width), jnp.bfloat16),
            jax.ShapeDtypeStruct((2 * heads, block), jnp.float32),
        ],
        scratch_shapes=[
            pltpu.VMEM((block, 4 * block), jnp.float32),
            pltpu.VMEM((block, HEAD), jnp.float32),
        ],
        compiler_params=pltpu.CompilerParams(vmem_limit_bytes=VMEM_BYTES),
        cost_estimate=pl.CostEstimate(
            flops=40 * block * block * width, bytes_accessed=24 * block * width, transcendentals=4 * block * block * heads
        ),
    )(device, queries, out_grad, *blocks)


def key_kernel(scale, last, idx_ref, both_ref, q0, q1, q2, q3, d0, d1, d2, d3, s0, s1, s2, s3, dk_ref, dv_ref, bias, lse, delta):
    block = q0.shape[0]
    heads = lse.shape[0]
    f32 = jnp.float32
    rows = lax.broadcasted_iota(jnp.int32, bias.shape, 0)
    cols = lax.broadcasted_iota(jnp.int32, bias.shape, 1)
    bias[...] = jnp.where(cols >= rows, 0.0, -jnp.inf)
    parts = [s0[...]]
    for hop, ref in enumerate((s1, s2, s3), 1):
        part = ref[...]
        row = lax.broadcasted_iota(jnp.int32, part.shape, 0)
        parts.append(jnp.where((idx_ref[0] + hop > last) & (row < heads), BIG, part))
    stats = jnp.concatenate(parts, axis=1)
    for one in range(heads):
        lse[one] = stats[one : one + 1]
        delta[one] = stats[heads + one : heads + one + 1]
    edge = bias.shape[1]

    @pl.loop(0, heads // GROUP)
    def _(step):
        for group in range(GROUP):
            head = GROUP * step + group
            lanes = pl.ds(pl.multiple_of(head * HEAD, HEAD), HEAD)
            queries = jnp.concatenate([ref[:, lanes] for ref in (q0, q1, q2, q3)], axis=0)
            dos = jnp.concatenate([ref[:, lanes] for ref in (d0, d1, d2, d3)], axis=0)
            scores = lax.dot_general(both_ref[pl.ds(0, block), lanes], queries, NT, preferred_element_type=f32) * scale - lse[head]
            scores = jnp.concatenate([scores[:, :edge] + bias[...], scores[:, edge:]], axis=1)
            probs = jnp.exp(scores)
            prob_grad = lax.dot_general(both_ref[pl.ds(block, block), lanes], dos, NT, preferred_element_type=f32)
            score_grad = (probs * (prob_grad - delta[head])).astype(jnp.bfloat16)
            dk_ref[:, lanes] = (jnp.dot(score_grad, queries, preferred_element_type=f32) * scale).astype(dk_ref.dtype)
            dv_ref[:, lanes] = jnp.dot(probs.astype(jnp.bfloat16), dos, preferred_element_type=f32).astype(dv_ref.dtype)


def key_side(device, both, queries, out_grads, stats, scale, last):
    block, width = queries[0].shape
    heads = width // HEAD
    shape = jax.ShapeDtypeStruct((block, width), jnp.bfloat16)
    return pl.pallas_call(
        functools.partial(key_kernel, scale, last),
        in_specs=[pl.BlockSpec(memory_space=pltpu.SMEM)] + [INSIDE] * 13,
        out_specs=[INSIDE] * 2,
        out_shape=[shape, shape],
        scratch_shapes=[
            pltpu.VMEM((block, 256), jnp.float32),
            pltpu.VMEM((heads, 1, 4 * block), jnp.float32),
            pltpu.VMEM((heads, 1, 4 * block), jnp.float32),
        ],
        compiler_params=pltpu.CompilerParams(vmem_limit_bytes=VMEM_BYTES),
        cost_estimate=pl.CostEstimate(
            flops=40 * block * block * width, bytes_accessed=24 * block * width, transcendentals=4 * block * block * heads
        ),
    )(device, both, *queries, *out_grads, *stats)


def per_device(queries, keys, values, stream_grad, conv_input, conv_weight, out_weight):
    block = queries.shape[0]
    last = lax.axis_size(CTX) - 1
    scale = 1.0 / math.sqrt(HEAD)
    device = lax.axis_index(CTX).astype(jnp.int32).reshape(1)
    tp = lax.axis_index("tp")

    pair = [(0, 1), (1, 0)]
    kv0, inside, across = pack(device, keys, values, conv_input, stream_grad)
    inside, across = swapped(inside, 0), swapped(across, 1)
    other = lax.ppermute(stream_grad, "tp", pair)
    (sent,) = after((kv0,), (across,))
    kv1, q1 = rotated(sent, 1), rotated(queries, -1)
    q2 = rotated(q1, -1)
    q3 = rotated(q2, -1)

    taps_count = conv_weight.shape[0]
    padding = jnp.zeros((2 * EDGE - taps_count, conv_weight.shape[1]), conv_weight.dtype)
    edges = jnp.concatenate([inside[EDGE:], across[EDGE:], conv_weight, padding], axis=0)
    (edges,) = after((edges,), (other,))
    edges = lax.ppermute(edges, "tp", pair)
    grad_stream, tap_rows = conv(device, stream_grad, conv_input, inside, across, conv_weight, last)
    tap_rows = exchanged(exchanged(tap_rows, 1), 2)
    other, edges, sent = after((other, edges, kv1), (q1, tap_rows))
    kv2 = rotated(sent, 1)
    tap_rows = exchanged(tap_rows, 4)
    out_grad = project(tp, grad_stream, conv_other(device, other, edges, taps_count, last), out_weight)
    (sent,) = after((kv2,), (out_grad, q1))
    kv3 = rotated(sent, 1)

    (sent,) = after((out_grad,), (tap_rows,))
    d1 = rotated(sent, -1)
    tap_rows = exchanged(tap_rows, 8)
    (sent,) = after((d1,), (kv2, q2, tap_rows))
    d2 = rotated(sent, -1)
    tap_rows = exchanged(tap_rows, 16)
    (sent,) = after((d2,), (q3, tap_rows))
    d3 = rotated(sent, -1)
    tap_rows = exchanged(tap_rows, 32)

    query_grad, stats = query_side(device, queries, out_grad, (kv3, kv2, kv1, kv0), scale)
    (stats,) = after((stats,), (tap_rows,))
    all_stats = [stats] + [rotated(stats, -hop) for hop in (1, 2, 3)]
    (tap_rows,) = after((tap_rows,), (*all_stats[1:], d3))
    tap_rows = exchanged(tap_rows, 64)
    key_grad, value_grad = key_side(device, kv0, (queries, q1, q2, q3), (out_grad, d1, d2, d3), all_stats, scale, last)
    kernel_grad = tap_rows[:taps_count] / math.sqrt(block * (last + 1))
    return (query_grad, key_grad, value_grad, grad_stream, kernel_grad)


def solution(mesh):
    count, pair = mesh.devices.shape
    far = 8
    split = Mesh(mesh.devices.reshape(far, count // far, pair), CTX + ("tp",))
    frames = P(CTX, "tp")
    return jax.shard_map(
        per_device,
        mesh=split,
        in_specs=(frames,) * 5 + (P(None, "tp"), P("tp", None)),
        out_specs=(frames,) * 4 + (P(None, "tp"),),
        check_vma=False,
    )
```

```python
import functools
import math

import jax
import jax.numpy as jnp
from jax import lax
from jax.experimental import pallas as pl
from jax.experimental.pallas import tpu as pltpu
from jax.sharding import Mesh
from jax.sharding import PartitionSpec as P

HEAD = 128
EDGE = 16
NT = (((1,), (1,)), ((), ()))
BIG = 1e30
GROUP = 4
VMEM_BYTES = 24 * 2**20
INSIDE = pl.BlockSpec(memory_space=pltpu.VMEM)
CTX = ("far", "near")


def rotated(part, by):
    count = lax.axis_size(CTX)
    return lax.ppermute(part, CTX, [(i, (i + by) % count) for i in range(count)])


def after(parts, done):
    return lax.optimization_barrier(tuple(parts) + tuple(done))[: len(parts)]


def pack_kernel(k_ref, q_ref, input_ref, grad_ref, low_ref, high_ref, sems):
    block = k_ref.shape[0]
    pairs = [
        (k_ref, low_ref.at[pl.ds(0, block)]),
        (q_ref, high_ref.at[pl.ds(0, block)]),
    ]
    for target, start in ((low_ref, block - EDGE), (high_ref, 0)):
        pairs.append((input_ref.at[pl.ds(start, EDGE)], target.at[pl.ds(block, EDGE)]))
        pairs.append((grad_ref.at[pl.ds(start, EDGE)], target.at[pl.ds(block + EDGE, EDGE)]))
    copies = [pltpu.make_async_copy(source, target, sems.at[i]) for i, (source, target) in enumerate(pairs)]
    for copy in copies:
        copy.start()
    for copy in copies:
        copy.wait()


def pack(keys, queries, inputs, grad):
    block, width = keys.shape
    shape = jax.ShapeDtypeStruct((block + 2 * EDGE, width), keys.dtype)
    return pl.pallas_call(
        pack_kernel,
        in_specs=[pl.BlockSpec(memory_space=pltpu.HBM)] * 4,
        out_specs=[INSIDE] * 2,
        out_shape=[shape, shape],
        scratch_shapes=[pltpu.SemaphoreType.DMA((6,))],
        compiler_params=pltpu.CompilerParams(vmem_limit_bytes=56 * 2**20),
    )(keys, queries, inputs, grad)


def conv_kernel(last, idx_ref, grad_ref, input_ref, low_ref, high_ref, taps_ref, out_ref, rows_ref, gpad, cpad):
    block = grad_ref.shape[0]
    width = grad_ref.shape[1]
    taps_count = taps_ref.shape[0]
    reach = taps_count // 2
    device = idx_ref[0]
    f32 = jnp.float32
    columns = width // HEAD

    @pl.loop(0, columns)
    def _(column):
        lanes = pl.ds(pl.multiple_of(column * HEAD, HEAD), HEAD)
        low = jnp.where(device > 0, low_ref[pl.ds(block, 2 * EDGE), lanes].astype(f32), 0.0)
        high = jnp.where(device < last, high_ref[pl.ds(block, 2 * EDGE), lanes].astype(f32), 0.0)
        grad = grad_ref[:, lanes].astype(f32)
        cpad[:EDGE] = low[:EDGE]
        gpad[:EDGE] = low[EDGE:]
        cpad[EDGE : EDGE + block] = input_ref[:, lanes].astype(f32)
        gpad[EDGE : EDGE + block] = grad
        cpad[EDGE + block :] = high[:EDGE]
        gpad[EDGE + block :] = high[EDGE:]
        taps = taps_ref[:, lanes].astype(f32)
        total = grad
        for tap in range(taps_count):
            total = total + taps[tap : tap + 1] * gpad[pl.ds(EDGE + reach - tap, block), :]
        out_ref[:, lanes] = total.astype(out_ref.dtype)
        grad = gpad[EDGE : EDGE + block]
        for tap in range(taps_count):
            prod = grad * cpad[pl.ds(EDGE - reach + tap, block), :]
            rows_ref[column, tap : tap + 1, :] = jnp.sum(prod, axis=0, keepdims=True)
        rows_ref[column, taps_count:, :] = jnp.zeros_like(rows_ref[column, taps_count:, :])


def conv(device, grad, inputs, low, high, taps, last):
    block, width = grad.shape
    count = taps.shape[0]
    return pl.pallas_call(
        functools.partial(conv_kernel, last),
        in_specs=[pl.BlockSpec(memory_space=pltpu.SMEM)] + [INSIDE] * 5,
        out_specs=[INSIDE] * 2,
        out_shape=[
            jax.ShapeDtypeStruct((block, width), jnp.bfloat16),
            jax.ShapeDtypeStruct((width // HEAD, 8 * pl.cdiv(count, 8), HEAD), jnp.float32),
        ],
        scratch_shapes=[
            pltpu.VMEM((block + 2 * EDGE, HEAD), jnp.float32),
            pltpu.VMEM((block + 2 * EDGE, HEAD), jnp.float32),
        ],
        compiler_params=pltpu.CompilerParams(vmem_limit_bytes=VMEM_BYTES),
        cost_estimate=pl.CostEstimate(flops=8 * block * width * count, bytes_accessed=4 * block * width, transcendentals=0),
    )(device, grad, inputs, low, high, taps)


def project(tp, own, other, weight):
    full = jnp.where(tp == 0, jnp.concatenate([own, other], axis=1), jnp.concatenate([other, own], axis=1))
    return lax.dot_general(full, weight, NT, preferred_element_type=jnp.float32).astype(jnp.bfloat16)


def query_kernel(scale, idx_ref, q_ref, do_ref, k3, k2, k1, k0, v3, v2, v1, v0, out_ref, stats_ref, bias, columns):
    block = q_ref.shape[0]
    heads = q_ref.shape[1] // HEAD
    f32 = jnp.float32
    rows = lax.broadcasted_iota(jnp.int32, bias.shape, 0)
    cols = lax.broadcasted_iota(jnp.int32, bias.shape, 1)
    valid = (cols <= 3 * block + rows) & (cols >= (3 - idx_ref[0]) * block)
    bias[...] = jnp.where(valid, 0.0, -jnp.inf)
    columns[...] = jnp.zeros_like(columns)

    @pl.loop(0, heads // GROUP)
    def _(step):
        lane = lax.broadcasted_iota(jnp.int32, columns.shape, 1)
        both = columns[...]
        for group in range(GROUP):
            head = step * GROUP + group
            lanes = pl.ds(pl.multiple_of(head * HEAD, HEAD), HEAD)
            keys = jnp.concatenate([ref[pl.ds(0, block), lanes] for ref in (k3, k2, k1, k0)], axis=0)
            values = jnp.concatenate([ref[:, lanes] for ref in (v3, v2, v1, v0)], axis=0)
            scores = lax.dot_general(q_ref[:, lanes], keys, NT, preferred_element_type=f32) * scale + bias[...]
            top = jnp.max(scores, axis=1, keepdims=True)
            expo = jnp.exp(scores - top)
            denom = jnp.sum(expo, axis=1, keepdims=True)
            probs = expo * (1.0 / denom)
            prob_grad = lax.dot_general(do_ref[:, lanes], values, NT, preferred_element_type=f32)
            delta = jnp.sum(probs.astype(jnp.bfloat16).astype(f32) * prob_grad, axis=1, keepdims=True)
            score_grad = (probs * (prob_grad - delta)).astype(jnp.bfloat16)
            out = jnp.dot(score_grad, keys, preferred_element_type=f32) * scale
            out_ref[:, lanes] = out.astype(out_ref.dtype)
            both = jnp.where(lane == head, top + jnp.log(denom), both)
            both = jnp.where(lane == heads + head, delta, both)
        columns[...] = both

    stats_ref[...] = columns[...].T[: stats_ref.shape[0]]


def query_side(device, queries, out_grad, keys, values, scale):
    block, width = queries.shape
    heads = width // HEAD
    return pl.pallas_call(
        functools.partial(query_kernel, scale),
        in_specs=[pl.BlockSpec(memory_space=pltpu.SMEM)] + [INSIDE] * 10,
        out_specs=[INSIDE] * 2,
        out_shape=[
            jax.ShapeDtypeStruct((block, width), jnp.bfloat16),
            jax.ShapeDtypeStruct((2 * heads, block), jnp.float32),
        ],
        scratch_shapes=[
            pltpu.VMEM((block, 4 * block), jnp.float32),
            pltpu.VMEM((block, HEAD), jnp.float32),
        ],
        compiler_params=pltpu.CompilerParams(vmem_limit_bytes=VMEM_BYTES),
        cost_estimate=pl.CostEstimate(
            flops=40 * block * block * width, bytes_accessed=24 * block * width, transcendentals=4 * block * block * heads
        ),
    )(device, queries, out_grad, *keys, *values)


def key_kernel(scale, last, idx_ref, k_ref, v_ref, q0, q1, q2, q3, d0, d1, d2, d3, s0, s1, s2, s3, dk_ref, dv_ref, bias, lse, delta):
    block = k_ref.shape[0]
    heads = lse.shape[0]
    f32 = jnp.float32
    rows = lax.broadcasted_iota(jnp.int32, bias.shape, 0)
    cols = lax.broadcasted_iota(jnp.int32, bias.shape, 1)
    bias[...] = jnp.where(cols >= rows, 0.0, -jnp.inf)
    parts = [s0[...]]
    for hop, ref in enumerate((s1, s2, s3), 1):
        part = ref[...]
        row = lax.broadcasted_iota(jnp.int32, part.shape, 0)
        parts.append(jnp.where((idx_ref[0] + hop > last) & (row < heads), BIG, part))
    stats = jnp.concatenate(parts, axis=1)
    for one in range(heads):
        lse[one] = stats[one : one + 1]
        delta[one] = stats[heads + one : heads + one + 1]
    edge = bias.shape[1]

    @pl.loop(0, heads // GROUP)
    def _(step):
        for group in range(GROUP):
            head = GROUP * step + group
            lanes = pl.ds(pl.multiple_of(head * HEAD, HEAD), HEAD)
            queries = jnp.concatenate([ref[pl.ds(0, block), lanes] for ref in (q0, q1, q2, q3)], axis=0)
            dos = jnp.concatenate([ref[:, lanes] for ref in (d0, d1, d2, d3)], axis=0)
            scores = lax.dot_general(k_ref[:, lanes], queries, NT, preferred_element_type=f32) * scale - lse[head]
            scores = jnp.concatenate([scores[:, :edge] + bias[...], scores[:, edge:]], axis=1)
            probs = jnp.exp(scores)
            prob_grad = lax.dot_general(v_ref[:, lanes], dos, NT, preferred_element_type=f32)
            score_grad = (probs * (prob_grad - delta[head])).astype(jnp.bfloat16)
            dk_ref[:, lanes] = (jnp.dot(score_grad, queries, preferred_element_type=f32) * scale).astype(dk_ref.dtype)
            dv_ref[:, lanes] = jnp.dot(probs.astype(jnp.bfloat16), dos, preferred_element_type=f32).astype(dv_ref.dtype)


def key_side(device, keys, values, queries, out_grads, stats, scale, last):
    block, width = keys.shape
    heads = width // HEAD
    shape = jax.ShapeDtypeStruct((block, width), jnp.bfloat16)
    return pl.pallas_call(
        functools.partial(key_kernel, scale, last),
        in_specs=[pl.BlockSpec(memory_space=pltpu.SMEM)] + [INSIDE] * 14,
        out_specs=[INSIDE] * 2,
        out_shape=[shape, shape],
        scratch_shapes=[
            pltpu.VMEM((block, 256), jnp.float32),
            pltpu.VMEM((heads, 1, 4 * block), jnp.float32),
            pltpu.VMEM((heads, 1, 4 * block), jnp.float32),
        ],
        compiler_params=pltpu.CompilerParams(vmem_limit_bytes=VMEM_BYTES),
        cost_estimate=pl.CostEstimate(
            flops=40 * block * block * width, bytes_accessed=24 * block * width, transcendentals=4 * block * block * heads
        ),
    )(device, keys, values, *queries, *out_grads, *stats)


def per_device(queries, keys, values, stream_grad, conv_input, conv_weight, out_weight):
    block = queries.shape[0]
    last = lax.axis_size(CTX) - 1
    scale = 1.0 / math.sqrt(HEAD)
    device = lax.axis_index(CTX).astype(jnp.int32).reshape(1)
    tp = lax.axis_index("tp")

    low, high = pack(keys, queries, conv_input, stream_grad)
    k1, q1 = rotated(low, 1), rotated(high, -1)
    (first,) = after((values,), (q1,))
    v1 = rotated(first, 1)
    k2, q2 = rotated(k1, 1), rotated(q1, -1)
    v2 = rotated(v1, 1)

    grad_stream, tap_rows = conv(device, stream_grad, conv_input, k1, q1, conv_weight, last)
    other = lax.ppermute(grad_stream, "tp", [(0, 1), (1, 0)])
    (tap_rows,) = after((tap_rows,), (k2,))
    tap_sums = jnp.sum(lax.all_to_all(tap_rows, "far", 0, 0, tiled=True), axis=0)
    (other,) = after((other,), (k2, q2, tap_sums))
    out_grad = project(tp, grad_stream, other, out_weight)
    k3, q3 = rotated(k2, 1), rotated(q2, -1)
    v3 = rotated(v2, 1)

    (sent,) = after((out_grad,), (v2,))
    d1 = rotated(sent, -1)
    (sent,) = after((d1,), (k3, q3))
    d2 = rotated(sent, -1)
    (sent,) = after((d2,), (v3,))
    d3 = rotated(sent, -1)

    copies = jnp.broadcast_to(tap_sums, (lax.axis_size("near"),) + tap_sums.shape)
    (copies,) = after((copies,), (v2, out_grad))
    tap_sums = jnp.sum(lax.all_to_all(copies, "near", 0, 0, tiled=True), axis=0)
    (near,) = after((queries,), (tap_sums,))
    query_grad, stats = query_side(device, near, out_grad, (k3, k2, k1, keys), (v3, v2, v1, values), scale)
    all_stats = [stats] + [rotated(stats, -hop) for hop in (1, 2, 3)]
    copies = jnp.broadcast_to(tap_sums, (lax.axis_size("far"),) + tap_sums.shape)
    (copies,) = after((copies,), (*all_stats[1:], d3))
    tap_sums = lax.all_to_all(copies, "far", 0, 0, tiled=True)
    key_grad, value_grad = key_side(
        device, keys, values, (queries, q1, q2, q3), (out_grad, d1, d2, d3), all_stats, scale, last
    )
    rows = jnp.transpose(tap_sums, (1, 0, 2)).reshape(tap_sums.shape[1], -1)[: conv_weight.shape[0]]
    kernel_grad = rows / math.sqrt(block * (last + 1))
    return (query_grad, key_grad, value_grad, grad_stream, kernel_grad)


def solution(mesh):
    count, pair = mesh.devices.shape
    far = 8
    split = Mesh(mesh.devices.reshape(far, count // far, pair), CTX + ("tp",))
    frames = P(CTX, "tp")
    return jax.shard_map(
        per_device,
        mesh=split,
        in_specs=(frames,) * 5 + (P(None, "tp"), P("tp", None)),
        out_specs=(frames,) * 4 + (P(None, "tp"),),
        check_vma=False,
    )
```

```python
import functools
import math

import jax
import jax.numpy as jnp
from jax import lax
from jax.experimental import pallas as pl
from jax.experimental.pallas import tpu as pltpu
from jax.sharding import Mesh
from jax.sharding import PartitionSpec as P

HEAD = 128
EDGE = 16
NT = (((1,), (1,)), ((), ()))
BIG = 1e30
GROUP = 4
VMEM_BYTES = 24 * 2**20
INSIDE = pl.BlockSpec(memory_space=pltpu.VMEM)
CTX = ("z", "near")


def rotated(part, by):
    count = lax.axis_size(CTX)
    return lax.ppermute(part, CTX, [(i, (i + by) % count) for i in range(count)])


def swapped(part, first):
    count = lax.axis_size(CTX)
    partner = lambda i: ((i - first) ^ 1) + first
    return lax.ppermute(part, CTX, [(i, partner(i) if 0 <= partner(i) < count and i >= first else i) for i in range(count)])


def after(parts, done):
    return lax.optimization_barrier(tuple(parts) + tuple(done))[: len(parts)]


def pack_kernel(idx_ref, k_ref, v_ref, input_ref, grad_ref, both_ref, inside_ref, across_ref, sems):
    block = k_ref.shape[0]
    odd = lax.rem(idx_ref[0], 2)
    pairs = [(k_ref, both_ref.at[pl.ds(0, block)]), (v_ref, both_ref.at[pl.ds(block, block)])]
    for target, start in ((inside_ref, (1 - odd) * (block - EDGE)), (across_ref, odd * (block - EDGE))):
        rows = pl.ds(pl.multiple_of(start, EDGE), EDGE)
        pairs.append((input_ref.at[rows], target.at[pl.ds(0, EDGE)]))
        pairs.append((grad_ref.at[rows], target.at[pl.ds(EDGE, EDGE)]))
    copies = [pltpu.make_async_copy(source, target, sems.at[i]) for i, (source, target) in enumerate(pairs)]
    for copy in copies:
        copy.start()
    for copy in copies:
        copy.wait()


def pack(device, keys, values, inputs, grad):
    block, width = keys.shape
    edge = jax.ShapeDtypeStruct((2 * EDGE, width), keys.dtype)
    return pl.pallas_call(
        pack_kernel,
        in_specs=[pl.BlockSpec(memory_space=pltpu.SMEM)] + [pl.BlockSpec(memory_space=pltpu.HBM)] * 4,
        out_specs=[INSIDE] * 3,
        out_shape=[jax.ShapeDtypeStruct((2 * block, width), keys.dtype), edge, edge],
        scratch_shapes=[pltpu.SemaphoreType.DMA((6,))],
        compiler_params=pltpu.CompilerParams(vmem_limit_bytes=56 * 2**20),
    )(device, keys, values, inputs, grad)


def conv_back(padded, grad, taps):
    block = grad.shape[0]
    taps_count = taps.shape[0]
    total = grad
    for tap in range(taps_count):
        total = total + taps[tap : tap + 1] * padded[pl.ds(EDGE + taps_count // 2 - tap, block), :]
    return total


def conv_kernel(last, idx_ref, grad_ref, input_ref, inside_ref, across_ref, taps_ref, out_ref, rows_ref, gpad, cpad):
    block = grad_ref.shape[0]
    taps_count = taps_ref.shape[0]
    device = idx_ref[0]
    even = lax.rem(device, 2) == 0
    f32 = jnp.float32

    @pl.loop(0, grad_ref.shape[1] // HEAD)
    def _(column):
        lanes = pl.ds(pl.multiple_of(column * HEAD, HEAD), HEAD)
        inside = inside_ref[:, lanes].astype(f32)
        across = across_ref[:, lanes].astype(f32)
        low = jnp.where(device > 0, jnp.where(even, across, inside), 0.0)
        high = jnp.where(device < last, jnp.where(even, inside, across), 0.0)
        grad = grad_ref[:, lanes].astype(f32)
        cpad[:EDGE] = low[:EDGE]
        gpad[:EDGE] = low[EDGE:]
        cpad[EDGE : EDGE + block] = input_ref[:, lanes].astype(f32)
        gpad[EDGE : EDGE + block] = grad
        cpad[EDGE + block :] = high[:EDGE]
        gpad[EDGE + block :] = high[EDGE:]
        out_ref[:, lanes] = conv_back(gpad, grad, taps_ref[:, lanes].astype(f32)).astype(out_ref.dtype)
        grad = gpad[EDGE : EDGE + block]
        for tap in range(taps_count):
            prod = grad * cpad[pl.ds(EDGE - taps_count // 2 + tap, block), :]
            rows_ref[column, tap : tap + 1, :] = jnp.sum(prod, axis=0, keepdims=True)
        rows_ref[column, taps_count:, :] = jnp.zeros_like(rows_ref[column, taps_count:, :])


def conv(device, grad, inputs, inside, across, taps, last):
    block, width = grad.shape
    count = taps.shape[0]
    return pl.pallas_call(
        functools.partial(conv_kernel, last),
        in_specs=[pl.BlockSpec(memory_space=pltpu.SMEM)] + [INSIDE] * 5,
        out_specs=[INSIDE] * 2,
        out_shape=[
            jax.ShapeDtypeStruct((block, width), jnp.bfloat16),
            jax.ShapeDtypeStruct((width // HEAD, 8 * pl.cdiv(count, 8), HEAD), jnp.float32),
        ],
        scratch_shapes=[pltpu.VMEM((block + 2 * EDGE, HEAD), jnp.float32)] * 2,
        compiler_params=pltpu.CompilerParams(vmem_limit_bytes=VMEM_BYTES),
        cost_estimate=pl.CostEstimate(flops=block * width, bytes_accessed=block * width // 16, transcendentals=0),
    )(device, grad, inputs, inside, across, taps)


def other_kernel(last, count, idx_ref, grad_ref, edges_ref, out_ref, gpad):
    block = grad_ref.shape[0]
    device = idx_ref[0]
    even = lax.rem(device, 2) == 0
    f32 = jnp.float32

    @pl.loop(0, grad_ref.shape[1] // HEAD)
    def _(column):
        lanes = pl.ds(pl.multiple_of(column * HEAD, HEAD), HEAD)
        edges = edges_ref[:, lanes].astype(f32)
        inside, across = edges[:EDGE], edges[EDGE : 2 * EDGE]
        grad = grad_ref[:, lanes].astype(f32)
        gpad[:EDGE] = jnp.where(device > 0, jnp.where(even, across, inside), 0.0)
        gpad[EDGE : EDGE + block] = grad
        gpad[EDGE + block :] = jnp.where(device < last, jnp.where(even, inside, across), 0.0)
        out_ref[:, lanes] = conv_back(gpad, grad, edges[2 * EDGE : 2 * EDGE + count]).astype(out_ref.dtype)


def conv_other(device, grad, edges, count, last):
    block, width = grad.shape
    return pl.pallas_call(
        functools.partial(other_kernel, last, count),
        in_specs=[pl.BlockSpec(memory_space=pltpu.SMEM)] + [INSIDE] * 2,
        out_specs=INSIDE,
        out_shape=jax.ShapeDtypeStruct((block, width), jnp.bfloat16),
        scratch_shapes=[pltpu.VMEM((block + 2 * EDGE, HEAD), jnp.float32)],
        compiler_params=pltpu.CompilerParams(vmem_limit_bytes=VMEM_BYTES),
        cost_estimate=pl.CostEstimate(flops=block * width, bytes_accessed=block * width // 16, transcendentals=0),
    )(device, grad, edges)


def project(tp, own, other, weight):
    full = jnp.where(tp == 0, jnp.concatenate([own, other], axis=1), jnp.concatenate([other, own], axis=1))
    full = lax.optimization_barrier(full)
    return lax.dot_general(full, weight, NT, preferred_element_type=jnp.float32).astype(jnp.bfloat16)


def query_kernel(scale, idx_ref, q_ref, do_ref, both3, both2, both1, both0, out_ref, stats_ref, bias, columns):
    block = q_ref.shape[0]
    heads = q_ref.shape[1] // HEAD
    f32 = jnp.float32
    rows = lax.broadcasted_iota(jnp.int32, bias.shape, 0)
    cols = lax.broadcasted_iota(jnp.int32, bias.shape, 1)
    valid = (cols <= 3 * block + rows) & (cols >= (3 - idx_ref[0]) * block)
    bias[...] = jnp.where(valid, 0.0, -jnp.inf)
    columns[...] = jnp.zeros_like(columns)

    @pl.loop(0, heads // GROUP)
    def _(step):
        lane = lax.broadcasted_iota(jnp.int32, columns.shape, 1)
        both = columns[...]
        for group in range(GROUP):
            head = step * GROUP + group
            lanes = pl.ds(pl.multiple_of(head * HEAD, HEAD), HEAD)
            keys, values = (
                jnp.concatenate([ref[pl.ds(start, block), lanes] for ref in (both3, both2, both1, both0)], axis=0)
                for start in (0, block)
            )
            scores = lax.dot_general(q_ref[:, lanes], keys, NT, preferred_element_type=f32) * scale + bias[...]
            top = jnp.max(scores, axis=1, keepdims=True)
            expo = jnp.exp(scores - top)
            denom = jnp.sum(expo, axis=1, keepdims=True)
            probs = expo * (1.0 / denom)
            prob_grad = lax.dot_general(do_ref[:, lanes], values, NT, preferred_element_type=f32)
            delta = jnp.sum(probs.astype(jnp.bfloat16).astype(f32) * prob_grad, axis=1, keepdims=True)
            score_grad = (probs * (prob_grad - delta)).astype(jnp.bfloat16)
            out = jnp.dot(score_grad, keys, preferred_element_type=f32) * scale
            out_ref[:, lanes] = out.astype(out_ref.dtype)
            both = jnp.where(lane == head, top + jnp.log(denom), both)
            both = jnp.where(lane == heads + head, delta, both)
        columns[...] = both

    stats_ref[...] = columns[...].T[: stats_ref.shape[0]]


def query_side(device, queries, out_grad, blocks, scale):
    block, width = queries.shape
    heads = width // HEAD
    return pl.pallas_call(
        functools.partial(query_kernel, scale),
        in_specs=[pl.BlockSpec(memory_space=pltpu.SMEM)] + [INSIDE] * 6,
        out_specs=[INSIDE] * 2,
        out_shape=[
            jax.ShapeDtypeStruct((block, width), jnp.bfloat16),
            jax.ShapeDtypeStruct((2 * heads, block), jnp.float32),
        ],
        scratch_shapes=[
            pltpu.VMEM((block, 4 * block), jnp.float32),
            pltpu.VMEM((block, HEAD), jnp.float32),
        ],
        compiler_params=pltpu.CompilerParams(vmem_limit_bytes=VMEM_BYTES),
        cost_estimate=pl.CostEstimate(
            flops=40 * block * block * width, bytes_accessed=24 * block * width, transcendentals=4 * block * block * heads
        ),
    )(device, queries, out_grad, *blocks)


def key_kernel(scale, last, idx_ref, both_ref, q0, q1, q2, q3, d0, d1, d2, d3, s0, s1, s2, s3, dk_ref, dv_ref, bias, lse, delta):
    block = q0.shape[0]
    heads = lse.shape[0]
    f32 = jnp.float32
    rows = lax.broadcasted_iota(jnp.int32, bias.shape, 0)
    cols = lax.broadcasted_iota(jnp.int32, bias.shape, 1)
    bias[...] = jnp.where(cols >= rows, 0.0, -jnp.inf)
    parts = [s0[...]]
    for hop, ref in enumerate((s1, s2, s3), 1):
        part = ref[...]
        row = lax.broadcasted_iota(jnp.int32, part.shape, 0)
        parts.append(jnp.where((idx_ref[0] + hop > last) & (row < heads), BIG, part))
    stats = jnp.concatenate(parts, axis=1)
    for one in range(heads):
        lse[one] = stats[one : one + 1]
        delta[one] = stats[heads + one : heads + one + 1]
    edge = bias.shape[1]

    @pl.loop(0, heads // GROUP)
    def _(step):
        for group in range(GROUP):
            head = GROUP * step + group
            lanes = pl.ds(pl.multiple_of(head * HEAD, HEAD), HEAD)
            queries = jnp.concatenate([ref[:, lanes] for ref in (q0, q1, q2, q3)], axis=0)
            dos = jnp.concatenate([ref[:, lanes] for ref in (d0, d1, d2, d3)], axis=0)
            scores = lax.dot_general(both_ref[pl.ds(0, block), lanes], queries, NT, preferred_element_type=f32) * scale - lse[head]
            scores = jnp.concatenate([scores[:, :edge] + bias[...], scores[:, edge:]], axis=1)
            probs = jnp.exp(scores)
            prob_grad = lax.dot_general(both_ref[pl.ds(block, block), lanes], dos, NT, preferred_element_type=f32)
            score_grad = (probs * (prob_grad - delta[head])).astype(jnp.bfloat16)
            dk_ref[:, lanes] = (jnp.dot(score_grad, queries, preferred_element_type=f32) * scale).astype(dk_ref.dtype)
            dv_ref[:, lanes] = jnp.dot(probs.astype(jnp.bfloat16), dos, preferred_element_type=f32).astype(dv_ref.dtype)


def key_side(device, both, queries, out_grads, stats, scale, last):
    block, width = queries[0].shape
    heads = width // HEAD
    shape = jax.ShapeDtypeStruct((block, width), jnp.bfloat16)
    return pl.pallas_call(
        functools.partial(key_kernel, scale, last),
        in_specs=[pl.BlockSpec(memory_space=pltpu.SMEM)] + [INSIDE] * 13,
        out_specs=[INSIDE] * 2,
        out_shape=[shape, shape],
        scratch_shapes=[
            pltpu.VMEM((block, 256), jnp.float32),
            pltpu.VMEM((heads, 1, 4 * block), jnp.float32),
            pltpu.VMEM((heads, 1, 4 * block), jnp.float32),
        ],
        compiler_params=pltpu.CompilerParams(vmem_limit_bytes=VMEM_BYTES),
        cost_estimate=pl.CostEstimate(
            flops=40 * block * block * width, bytes_accessed=24 * block * width, transcendentals=4 * block * block * heads
        ),
    )(device, both, *queries, *out_grads, *stats)


def per_device(queries, keys, values, stream_grad, conv_input, conv_weight, out_weight):
    block = queries.shape[0]
    last = lax.axis_size(CTX) - 1
    scale = 1.0 / math.sqrt(HEAD)
    device = lax.axis_index(CTX).astype(jnp.int32).reshape(1)
    tp = lax.axis_index("tp")

    pair = [(0, 1), (1, 0)]
    kv0, inside, across = pack(device, keys, values, conv_input, stream_grad)
    inside, across = swapped(inside, 0), swapped(across, 1)
    other = lax.ppermute(stream_grad, "tp", pair)
    (sent,) = after((kv0,), (across, other))
    kv1, q1 = rotated(sent, 1), rotated(queries, -1)
    q2 = rotated(q1, -1)
    q3 = rotated(q2, -1)

    taps_count = conv_weight.shape[0]
    padding = jnp.zeros((2 * EDGE - taps_count, conv_weight.shape[1]), conv_weight.dtype)
    edges = lax.ppermute(jnp.concatenate([inside[EDGE:], across[EDGE:], conv_weight, padding], axis=0), "tp", pair)
    grad_stream, tap_rows = conv(device, stream_grad, conv_input, inside, across, conv_weight, last)
    out_grad = project(tp, grad_stream, conv_other(device, other, edges, taps_count, last), out_weight)
    (sent,) = after((kv1,), (q1, out_grad))
    kv2 = rotated(sent, 1)
    kv3 = rotated(kv2, 1)
    d1 = rotated(out_grad, -1)
    (sent,) = after((d1,), (kv2, q2))
    d2 = rotated(sent, -1)
    (sent,) = after((d2,), (q3,))
    d3 = rotated(sent, -1)

    (tap_rows,) = after((tap_rows,), (kv1, d1))
    tap_sums = jnp.sum(lax.all_to_all(tap_rows, "z", 0, 0, tiled=True), axis=0)
    copies = jnp.broadcast_to(tap_sums, (lax.axis_size("near"),) + tap_sums.shape)
    (copies,) = after((copies,), (kv3,))
    tap_sums = jnp.sum(lax.all_to_all(copies, "near", 0, 0, tiled=True), axis=0)
    query_grad, stats = query_side(device, queries, out_grad, (kv3, kv2, kv1, kv0), scale)
    all_stats = [stats] + [rotated(stats, -hop) for hop in (1, 2, 3)]
    copies = jnp.broadcast_to(tap_sums, (lax.axis_size("z"),) + tap_sums.shape)
    (copies,) = after((copies,), (*all_stats[1:], d3))
    tap_sums = lax.all_to_all(copies, "z", 0, 0, tiled=True)
    key_grad, value_grad = key_side(device, kv0, (queries, q1, q2, q3), (out_grad, d1, d2, d3), all_stats, scale, last)
    rows = jnp.transpose(tap_sums, (1, 0, 2)).reshape(tap_sums.shape[1], -1)[:taps_count]
    kernel_grad = rows / math.sqrt(block * (last + 1))
    return (query_grad, key_grad, value_grad, grad_stream, kernel_grad)


def solution(mesh):
    count, pair = mesh.devices.shape
    far = 8
    split = Mesh(mesh.devices.reshape(far, count // far, pair), CTX + ("tp",))
    frames = P(CTX, "tp")
    return jax.shard_map(
        per_device,
        mesh=split,
        in_specs=(frames,) * 5 + (P(None, "tp"), P("tp", None)),
        out_specs=(frames,) * 4 + (P(None, "tp"),),
        check_vma=False,
    )
```

```python
import functools
import math

import jax
import jax.numpy as jnp
from jax import lax
from jax.experimental import pallas as pl
from jax.experimental.pallas import tpu as pltpu
from jax.sharding import Mesh
from jax.sharding import PartitionSpec as P

HEAD = 128
EDGE = 16
NT = (((1,), (1,)), ((), ()))
BIG = 1e30
GROUP = 4
VMEM_BYTES = 24 * 2**20
INSIDE = pl.BlockSpec(memory_space=pltpu.VMEM)
CTX = ("z", "near")


def rotated(part, by):
    count = lax.axis_size(CTX)
    return lax.ppermute(part, CTX, [(i, i + by) for i in range(count) if 0 <= i + by < count])


def swapped(part, first):
    count = lax.axis_size(CTX)
    partner = lambda i: ((i - first) ^ 1) + first
    return lax.ppermute(part, CTX, [(i, partner(i) if 0 <= partner(i) < count and i >= first else i) for i in range(count)])


def after(parts, done):
    return lax.optimization_barrier(tuple(parts) + tuple(done))[: len(parts)]


def pack_kernel(idx_ref, k_ref, v_ref, input_ref, grad_ref, both_ref, inside_ref, across_ref, sems):
    block = k_ref.shape[0]
    odd = lax.rem(idx_ref[0], 2)
    pairs = [(k_ref, both_ref.at[pl.ds(0, block)]), (v_ref, both_ref.at[pl.ds(block, block)])]
    for target, start in ((inside_ref, (1 - odd) * (block - EDGE)), (across_ref, odd * (block - EDGE))):
        rows = pl.ds(pl.multiple_of(start, EDGE), EDGE)
        pairs.append((input_ref.at[rows], target.at[pl.ds(0, EDGE)]))
        pairs.append((grad_ref.at[rows], target.at[pl.ds(EDGE, EDGE)]))
    copies = [pltpu.make_async_copy(source, target, sems.at[i]) for i, (source, target) in enumerate(pairs)]
    for copy in copies:
        copy.start()
    for copy in copies:
        copy.wait()


def pack(device, keys, values, inputs, grad):
    block, width = keys.shape
    edge = jax.ShapeDtypeStruct((2 * EDGE, width), keys.dtype)
    return pl.pallas_call(
        pack_kernel,
        in_specs=[pl.BlockSpec(memory_space=pltpu.SMEM)] + [pl.BlockSpec(memory_space=pltpu.HBM)] * 4,
        out_specs=[INSIDE] * 3,
        out_shape=[jax.ShapeDtypeStruct((2 * block, width), keys.dtype), edge, edge],
        scratch_shapes=[pltpu.SemaphoreType.DMA((6,))],
        compiler_params=pltpu.CompilerParams(vmem_limit_bytes=56 * 2**20),
    )(device, keys, values, inputs, grad)


def conv_back(padded, grad, taps):
    block = grad.shape[0]
    taps_count = taps.shape[0]
    total = grad
    for tap in range(taps_count):
        total = total + taps[tap : tap + 1] * padded[pl.ds(EDGE + taps_count // 2 - tap, block), :]
    return total


def conv_kernel(last, idx_ref, grad_ref, input_ref, inside_ref, across_ref, taps_ref, out_ref, rows_ref, gpad, cpad):
    block = grad_ref.shape[0]
    taps_count = taps_ref.shape[0]
    device = idx_ref[0]
    even = lax.rem(device, 2) == 0
    f32 = jnp.float32

    @pl.loop(0, grad_ref.shape[1] // HEAD)
    def _(column):
        lanes = pl.ds(pl.multiple_of(column * HEAD, HEAD), HEAD)
        inside = inside_ref[:, lanes].astype(f32)
        across = across_ref[:, lanes].astype(f32)
        low = jnp.where(device > 0, jnp.where(even, across, inside), 0.0)
        high = jnp.where(device < last, jnp.where(even, inside, across), 0.0)
        grad = grad_ref[:, lanes].astype(f32)
        cpad[:EDGE] = low[:EDGE]
        gpad[:EDGE] = low[EDGE:]
        cpad[EDGE : EDGE + block] = input_ref[:, lanes].astype(f32)
        gpad[EDGE : EDGE + block] = grad
        cpad[EDGE + block :] = high[:EDGE]
        gpad[EDGE + block :] = high[EDGE:]
        out_ref[:, lanes] = conv_back(gpad, grad, taps_ref[:, lanes].astype(f32)).astype(out_ref.dtype)
        grad = gpad[EDGE : EDGE + block]
        for tap in range(taps_count):
            prod = grad * cpad[pl.ds(EDGE - taps_count // 2 + tap, block), :]
            rows_ref[column, tap : tap + 1, :] = jnp.sum(prod, axis=0, keepdims=True)
        rows_ref[column, taps_count:, :] = jnp.zeros_like(rows_ref[column, taps_count:, :])


def conv(device, grad, inputs, inside, across, taps, last):
    block, width = grad.shape
    count = taps.shape[0]
    return pl.pallas_call(
        functools.partial(conv_kernel, last),
        in_specs=[pl.BlockSpec(memory_space=pltpu.SMEM)] + [INSIDE] * 5,
        out_specs=[INSIDE] * 2,
        out_shape=[
            jax.ShapeDtypeStruct((block, width), jnp.bfloat16),
            jax.ShapeDtypeStruct((width // HEAD, 8 * pl.cdiv(count, 8), HEAD), jnp.float32),
        ],
        scratch_shapes=[pltpu.VMEM((block + 2 * EDGE, HEAD), jnp.float32)] * 2,
        compiler_params=pltpu.CompilerParams(vmem_limit_bytes=VMEM_BYTES),
        cost_estimate=pl.CostEstimate(flops=block * width, bytes_accessed=block * width // 16, transcendentals=0),
    )(device, grad, inputs, inside, across, taps)


def other_kernel(last, count, idx_ref, grad_ref, edges_ref, out_ref, gpad):
    block = grad_ref.shape[0]
    device = idx_ref[0]
    even = lax.rem(device, 2) == 0
    f32 = jnp.float32

    @pl.loop(0, grad_ref.shape[1] // HEAD)
    def _(column):
        lanes = pl.ds(pl.multiple_of(column * HEAD, HEAD), HEAD)
        edges = edges_ref[:, lanes].astype(f32)
        inside, across = edges[:EDGE], edges[EDGE : 2 * EDGE]
        grad = grad_ref[:, lanes].astype(f32)
        gpad[:EDGE] = jnp.where(device > 0, jnp.where(even, across, inside), 0.0)
        gpad[EDGE : EDGE + block] = grad
        gpad[EDGE + block :] = jnp.where(device < last, jnp.where(even, inside, across), 0.0)
        out_ref[:, lanes] = conv_back(gpad, grad, edges[2 * EDGE : 2 * EDGE + count]).astype(out_ref.dtype)


def conv_other(device, grad, edges, count, last):
    block, width = grad.shape
    return pl.pallas_call(
        functools.partial(other_kernel, last, count),
        in_specs=[pl.BlockSpec(memory_space=pltpu.SMEM)] + [INSIDE] * 2,
        out_specs=INSIDE,
        out_shape=jax.ShapeDtypeStruct((block, width), jnp.bfloat16),
        scratch_shapes=[pltpu.VMEM((block + 2 * EDGE, HEAD), jnp.float32)],
        compiler_params=pltpu.CompilerParams(vmem_limit_bytes=VMEM_BYTES),
        cost_estimate=pl.CostEstimate(flops=block * width, bytes_accessed=block * width // 16, transcendentals=0),
    )(device, grad, edges)


def project(tp, own, other, weight):
    full = jnp.where(tp == 0, jnp.concatenate([own, other], axis=1), jnp.concatenate([other, own], axis=1))
    full = lax.optimization_barrier(full)
    return lax.dot_general(full, weight, NT, preferred_element_type=jnp.float32).astype(jnp.bfloat16)


def query_kernel(scale, idx_ref, q_ref, do_ref, both3, both2, both1, both0, out_ref, stats_ref, bias, columns):
    block = q_ref.shape[0]
    heads = q_ref.shape[1] // HEAD
    f32 = jnp.float32
    rows = lax.broadcasted_iota(jnp.int32, bias.shape, 0)
    cols = lax.broadcasted_iota(jnp.int32, bias.shape, 1)
    valid = (cols <= 3 * block + rows) & (cols >= (3 - idx_ref[0]) * block)
    bias[...] = jnp.where(valid, 0.0, -jnp.inf)
    columns[...] = jnp.zeros_like(columns)

    @pl.loop(0, heads // GROUP)
    def _(step):
        lane = lax.broadcasted_iota(jnp.int32, columns.shape, 1)
        both = columns[...]
        for group in range(GROUP):
            head = step * GROUP + group
            lanes = pl.ds(pl.multiple_of(head * HEAD, HEAD), HEAD)
            keys, values = (
                jnp.concatenate([ref[pl.ds(start, block), lanes] for ref in (both3, both2, both1, both0)], axis=0)
                for start in (0, block)
            )
            scores = lax.dot_general(q_ref[:, lanes], keys, NT, preferred_element_type=f32) * scale + bias[...]
            top = jnp.max(scores, axis=1, keepdims=True)
            expo = jnp.exp(scores - top)
            denom = jnp.sum(expo, axis=1, keepdims=True)
            probs = expo * (1.0 / denom)
            prob_grad = lax.dot_general(do_ref[:, lanes], values, NT, preferred_element_type=f32)
            delta = jnp.sum(probs.astype(jnp.bfloat16).astype(f32) * prob_grad, axis=1, keepdims=True)
            score_grad = (probs * (prob_grad - delta)).astype(jnp.bfloat16)
            out = jnp.dot(score_grad, keys, preferred_element_type=f32) * scale
            out_ref[:, lanes] = out.astype(out_ref.dtype)
            both = jnp.where(lane == head, top + jnp.log(denom), both)
            both = jnp.where(lane == heads + head, delta, both)
        columns[...] = both

    stats_ref[...] = columns[...].T[: stats_ref.shape[0]]


def query_side(device, queries, out_grad, blocks, scale):
    block, width = queries.shape
    heads = width // HEAD
    return pl.pallas_call(
        functools.partial(query_kernel, scale),
        in_specs=[pl.BlockSpec(memory_space=pltpu.SMEM)] + [INSIDE] * 6,
        out_specs=[INSIDE] * 2,
        out_shape=[
            jax.ShapeDtypeStruct((block, width), jnp.bfloat16),
            jax.ShapeDtypeStruct((2 * heads, block), jnp.float32),
        ],
        scratch_shapes=[
            pltpu.VMEM((block, 4 * block), jnp.float32),
            pltpu.VMEM((block, HEAD), jnp.float32),
        ],
        compiler_params=pltpu.CompilerParams(vmem_limit_bytes=VMEM_BYTES),
        cost_estimate=pl.CostEstimate(
            flops=40 * block * block * width, bytes_accessed=24 * block * width, transcendentals=4 * block * block * heads
        ),
    )(device, queries, out_grad, *blocks)


def key_kernel(scale, last, idx_ref, both_ref, q0, q1, q2, q3, d0, d1, d2, d3, s0, s1, s2, s3, dk_ref, dv_ref, bias, lse, delta):
    block = q0.shape[0]
    heads = lse.shape[0]
    f32 = jnp.float32
    rows = lax.broadcasted_iota(jnp.int32, bias.shape, 0)
    cols = lax.broadcasted_iota(jnp.int32, bias.shape, 1)
    bias[...] = jnp.where(cols >= rows, 0.0, -jnp.inf)
    parts = [s0[...]]
    for hop, ref in enumerate((s1, s2, s3), 1):
        part = ref[...]
        row = lax.broadcasted_iota(jnp.int32, part.shape, 0)
        parts.append(jnp.where((idx_ref[0] + hop > last) & (row < heads), BIG, part))
    stats = jnp.concatenate(parts, axis=1)
    for one in range(heads):
        lse[one] = stats[one : one + 1]
        delta[one] = stats[heads + one : heads + one + 1]
    edge = bias.shape[1]

    @pl.loop(0, heads // GROUP)
    def _(step):
        for group in range(GROUP):
            head = GROUP * step + group
            lanes = pl.ds(pl.multiple_of(head * HEAD, HEAD), HEAD)
            queries = jnp.concatenate([ref[:, lanes] for ref in (q0, q1, q2, q3)], axis=0)
            dos = jnp.concatenate([ref[:, lanes] for ref in (d0, d1, d2, d3)], axis=0)
            scores = lax.dot_general(both_ref[pl.ds(0, block), lanes], queries, NT, preferred_element_type=f32) * scale - lse[head]
            scores = jnp.concatenate([scores[:, :edge] + bias[...], scores[:, edge:]], axis=1)
            probs = jnp.exp(scores)
            prob_grad = lax.dot_general(both_ref[pl.ds(block, block), lanes], dos, NT, preferred_element_type=f32)
            score_grad = (probs * (prob_grad - delta[head])).astype(jnp.bfloat16)
            dk_ref[:, lanes] = (jnp.dot(score_grad, queries, preferred_element_type=f32) * scale).astype(dk_ref.dtype)
            dv_ref[:, lanes] = jnp.dot(probs.astype(jnp.bfloat16), dos, preferred_element_type=f32).astype(dv_ref.dtype)


def key_side(device, both, queries, out_grads, stats, scale, last):
    block, width = queries[0].shape
    heads = width // HEAD
    shape = jax.ShapeDtypeStruct((block, width), jnp.bfloat16)
    return pl.pallas_call(
        functools.partial(key_kernel, scale, last),
        in_specs=[pl.BlockSpec(memory_space=pltpu.SMEM)] + [INSIDE] * 13,
        out_specs=[INSIDE] * 2,
        out_shape=[shape, shape],
        scratch_shapes=[
            pltpu.VMEM((block, 256), jnp.float32),
            pltpu.VMEM((heads, 1, 4 * block), jnp.float32),
            pltpu.VMEM((heads, 1, 4 * block), jnp.float32),
        ],
        compiler_params=pltpu.CompilerParams(vmem_limit_bytes=VMEM_BYTES),
        cost_estimate=pl.CostEstimate(
            flops=40 * block * block * width, bytes_accessed=24 * block * width, transcendentals=4 * block * block * heads
        ),
    )(device, both, *queries, *out_grads, *stats)


def per_device(queries, keys, values, stream_grad, conv_input, conv_weight, out_weight):
    block = queries.shape[0]
    last = lax.axis_size(CTX) - 1
    scale = 1.0 / math.sqrt(HEAD)
    device = lax.axis_index(CTX).astype(jnp.int32).reshape(1)
    tp = lax.axis_index("tp")

    pair = [(0, 1), (1, 0)]
    kv0, inside, across = pack(device, keys, values, conv_input, stream_grad)
    inside, across = swapped(inside, 0), swapped(across, 1)
    other = lax.ppermute(stream_grad, "tp", pair)
    (sent,) = after((kv0,), (across, other))
    kv1, q1 = rotated(sent, 1), rotated(queries, -1)
    q2 = rotated(q1, -1)
    q3 = rotated(q2, -1)

    taps_count = conv_weight.shape[0]
    padding = jnp.zeros((2 * EDGE - taps_count, conv_weight.shape[1]), conv_weight.dtype)
    edges = lax.ppermute(jnp.concatenate([inside[EDGE:], across[EDGE:], conv_weight, padding], axis=0), "tp", pair)
    grad_stream, tap_rows = conv(device, stream_grad, conv_input, inside, across, conv_weight, last)
    out_grad = project(tp, grad_stream, conv_other(device, other, edges, taps_count, last), out_weight)
    (sent,) = after((kv1,), (q1, out_grad))
    kv2 = rotated(sent, 1)
    kv3 = rotated(kv2, 1)
    d1 = rotated(out_grad, -1)
    (sent,) = after((d1,), (kv2, q2))
    d2 = rotated(sent, -1)
    (sent,) = after((d2,), (q3,))
    d3 = rotated(sent, -1)

    (tap_rows,) = after((tap_rows,), (kv1, d1))
    tap_sums = jnp.sum(lax.all_to_all(tap_rows, "z", 0, 0, tiled=True), axis=0)
    copies = jnp.broadcast_to(tap_sums, (lax.axis_size("near"),) + tap_sums.shape)
    (copies,) = after((copies,), (kv3,))
    tap_sums = jnp.sum(lax.all_to_all(copies, "near", 0, 0, tiled=True), axis=0)
    query_grad, stats = query_side(device, queries, out_grad, (kv3, kv2, kv1, kv0), scale)
    all_stats = [stats] + [rotated(stats, -hop) for hop in (1, 2, 3)]
    copies = jnp.broadcast_to(tap_sums, (lax.axis_size("z"),) + tap_sums.shape)
    (copies,) = after((copies,), (*all_stats[1:], d3))
    tap_sums = lax.all_to_all(copies, "z", 0, 0, tiled=True)
    key_grad, value_grad = key_side(device, kv0, (queries, q1, q2, q3), (out_grad, d1, d2, d3), all_stats, scale, last)
    rows = jnp.transpose(tap_sums, (1, 0, 2)).reshape(tap_sums.shape[1], -1)[:taps_count]
    kernel_grad = rows / math.sqrt(block * (last + 1))
    return (query_grad, key_grad, value_grad, grad_stream, kernel_grad)


def solution(mesh):
    count, pair = mesh.devices.shape
    far = 8
    split = Mesh(mesh.devices.reshape(far, count // far, pair), CTX + ("tp",))
    frames = P(CTX, "tp")
    return jax.shard_map(
        per_device,
        mesh=split,
        in_specs=(frames,) * 5 + (P(None, "tp"), P("tp", None)),
        out_specs=(frames,) * 4 + (P(None, "tp"),),
        check_vma=False,
    )
```

```python
import functools
import math

import jax
import jax.numpy as jnp
from jax import lax
from jax.experimental import pallas as pl
from jax.experimental.pallas import tpu as pltpu
from jax.sharding import Mesh
from jax.sharding import PartitionSpec as P

HEAD = 128
EDGE = 16
NT = (((1,), (1,)), ((), ()))
BIG = 1e30
GROUP = 4
VMEM_BYTES = 24 * 2**20
INSIDE = pl.BlockSpec(memory_space=pltpu.VMEM)
CTX = ("z", "near")


def rotated(part, by):
    count = lax.axis_size(CTX)
    return lax.ppermute(part, CTX, [(i, (i + by) % count) for i in range(count)])


def swapped(part, first):
    count = lax.axis_size(CTX)
    partner = lambda i: ((i - first) ^ 1) + first
    return lax.ppermute(part, CTX, [(i, partner(i) if 0 <= partner(i) < count and i >= first else i) for i in range(count)])


def after(parts, done):
    return lax.optimization_barrier(tuple(parts) + tuple(done))[: len(parts)]


def pack_kernel(idx_ref, k_ref, v_ref, input_ref, grad_ref, both_ref, inside_ref, across_ref, sems):
    block = k_ref.shape[0]
    odd = lax.rem(idx_ref[0], 2)
    pairs = [(k_ref, both_ref.at[pl.ds(0, block)]), (v_ref, both_ref.at[pl.ds(block, block)])]
    for target, start in ((inside_ref, (1 - odd) * (block - EDGE)), (across_ref, odd * (block - EDGE))):
        rows = pl.ds(pl.multiple_of(start, EDGE), EDGE)
        pairs.append((input_ref.at[rows], target.at[pl.ds(0, EDGE)]))
        pairs.append((grad_ref.at[rows], target.at[pl.ds(EDGE, EDGE)]))
    copies = [pltpu.make_async_copy(source, target, sems.at[i]) for i, (source, target) in enumerate(pairs)]
    for copy in copies:
        copy.start()
    for copy in copies:
        copy.wait()


def pack(device, keys, values, inputs, grad):
    block, width = keys.shape
    edge = jax.ShapeDtypeStruct((2 * EDGE, width), keys.dtype)
    return pl.pallas_call(
        pack_kernel,
        in_specs=[pl.BlockSpec(memory_space=pltpu.SMEM)] + [pl.BlockSpec(memory_space=pltpu.HBM)] * 4,
        out_specs=[INSIDE] * 3,
        out_shape=[jax.ShapeDtypeStruct((2 * block, width), keys.dtype), edge, edge],
        scratch_shapes=[pltpu.SemaphoreType.DMA((6,))],
        compiler_params=pltpu.CompilerParams(vmem_limit_bytes=56 * 2**20),
    )(device, keys, values, inputs, grad)


def conv_back(padded, grad, taps):
    block = grad.shape[0]
    taps_count = taps.shape[0]
    total = grad
    for tap in range(taps_count):
        total = total + taps[tap : tap + 1] * padded[pl.ds(EDGE + taps_count // 2 - tap, block), :]
    return total


def conv_kernel(last, idx_ref, grad_ref, input_ref, inside_ref, across_ref, taps_ref, out_ref, rows_ref, gpad, cpad):
    block = grad_ref.shape[0]
    taps_count = taps_ref.shape[0]
    device = idx_ref[0]
    even = lax.rem(device, 2) == 0
    f32 = jnp.float32

    @pl.loop(0, grad_ref.shape[1] // HEAD)
    def _(column):
        lanes = pl.ds(pl.multiple_of(column * HEAD, HEAD), HEAD)
        inside = inside_ref[:, lanes].astype(f32)
        across = across_ref[:, lanes].astype(f32)
        low = jnp.where(device > 0, jnp.where(even, across, inside), 0.0)
        high = jnp.where(device < last, jnp.where(even, inside, across), 0.0)
        grad = grad_ref[:, lanes].astype(f32)
        cpad[:EDGE] = low[:EDGE]
        gpad[:EDGE] = low[EDGE:]
        cpad[EDGE : EDGE + block] = input_ref[:, lanes].astype(f32)
        gpad[EDGE : EDGE + block] = grad
        cpad[EDGE + block :] = high[:EDGE]
        gpad[EDGE + block :] = high[EDGE:]
        out_ref[:, lanes] = conv_back(gpad, grad, taps_ref[:, lanes].astype(f32)).astype(out_ref.dtype)
        grad = gpad[EDGE : EDGE + block]
        for tap in range(taps_count):
            prod = grad * cpad[pl.ds(EDGE - taps_count // 2 + tap, block), :]
            rows_ref[column, tap : tap + 1, :] = jnp.sum(prod, axis=0, keepdims=True)
        rows_ref[column, taps_count:, :] = jnp.zeros_like(rows_ref[column, taps_count:, :])


def conv(device, grad, inputs, inside, across, taps, last):
    block, width = grad.shape
    count = taps.shape[0]
    return pl.pallas_call(
        functools.partial(conv_kernel, last),
        in_specs=[pl.BlockSpec(memory_space=pltpu.SMEM)] + [INSIDE] * 5,
        out_specs=[INSIDE] * 2,
        out_shape=[
            jax.ShapeDtypeStruct((block, width), jnp.bfloat16),
            jax.ShapeDtypeStruct((width // HEAD, 8 * pl.cdiv(count, 8), HEAD), jnp.float32),
        ],
        scratch_shapes=[pltpu.VMEM((block + 2 * EDGE, HEAD), jnp.float32)] * 2,
        compiler_params=pltpu.CompilerParams(vmem_limit_bytes=VMEM_BYTES),
        cost_estimate=pl.CostEstimate(flops=block * width, bytes_accessed=block * width // 16, transcendentals=0),
    )(device, grad, inputs, inside, across, taps)


def other_kernel(last, count, idx_ref, grad_ref, edges_ref, out_ref, gpad):
    block = grad_ref.shape[0]
    device = idx_ref[0]
    even = lax.rem(device, 2) == 0
    f32 = jnp.float32

    @pl.loop(0, grad_ref.shape[1] // HEAD)
    def _(column):
        lanes = pl.ds(pl.multiple_of(column * HEAD, HEAD), HEAD)
        edges = edges_ref[:, lanes].astype(f32)
        inside, across = edges[:EDGE], edges[EDGE : 2 * EDGE]
        grad = grad_ref[:, lanes].astype(f32)
        gpad[:EDGE] = jnp.where(device > 0, jnp.where(even, across, inside), 0.0)
        gpad[EDGE : EDGE + block] = grad
        gpad[EDGE + block :] = jnp.where(device < last, jnp.where(even, inside, across), 0.0)
        out_ref[:, lanes] = conv_back(gpad, grad, edges[2 * EDGE : 2 * EDGE + count]).astype(out_ref.dtype)


def conv_other(device, grad, edges, count, last):
    block, width = grad.shape
    return pl.pallas_call(
        functools.partial(other_kernel, last, count),
        in_specs=[pl.BlockSpec(memory_space=pltpu.SMEM)] + [INSIDE] * 2,
        out_specs=INSIDE,
        out_shape=jax.ShapeDtypeStruct((block, width), jnp.bfloat16),
        scratch_shapes=[pltpu.VMEM((block + 2 * EDGE, HEAD), jnp.float32)],
        compiler_params=pltpu.CompilerParams(vmem_limit_bytes=VMEM_BYTES),
        cost_estimate=pl.CostEstimate(flops=block * width, bytes_accessed=block * width // 16, transcendentals=0),
    )(device, grad, edges)


def project(tp, own, other, weight):
    full = jnp.where(tp == 0, jnp.concatenate([own, other], axis=1), jnp.concatenate([other, own], axis=1))
    full = lax.optimization_barrier(full)
    return lax.dot_general(full, weight, NT, preferred_element_type=jnp.float32).astype(jnp.bfloat16)


def query_kernel(scale, idx_ref, q_ref, do_ref, both3, both2, both1, both0, out_ref, stats_ref, bias, columns):
    block = q_ref.shape[0]
    heads = q_ref.shape[1] // HEAD
    f32 = jnp.float32
    rows = lax.broadcasted_iota(jnp.int32, bias.shape, 0)
    cols = lax.broadcasted_iota(jnp.int32, bias.shape, 1)
    valid = (cols <= 3 * block + rows) & (cols >= (3 - idx_ref[0]) * block)
    bias[...] = jnp.where(valid, 0.0, -jnp.inf)
    columns[...] = jnp.zeros_like(columns)

    @pl.loop(0, heads // GROUP)
    def _(step):
        lane = lax.broadcasted_iota(jnp.int32, columns.shape, 1)
        both = columns[...]
        for group in range(GROUP):
            head = step * GROUP + group
            lanes = pl.ds(pl.multiple_of(head * HEAD, HEAD), HEAD)
            keys, values = (
                jnp.concatenate([ref[pl.ds(start, block), lanes] for ref in (both3, both2, both1, both0)], axis=0)
                for start in (0, block)
            )
            scores = lax.dot_general(q_ref[:, lanes], keys, NT, preferred_element_type=f32) * scale + bias[...]
            top = jnp.max(scores, axis=1, keepdims=True)
            expo = jnp.exp(scores - top)
            denom = jnp.sum(expo, axis=1, keepdims=True)
            probs = expo * (1.0 / denom)
            prob_grad = lax.dot_general(do_ref[:, lanes], values, NT, preferred_element_type=f32)
            delta = jnp.sum(probs.astype(jnp.bfloat16).astype(f32) * prob_grad, axis=1, keepdims=True)
            score_grad = (probs * (prob_grad - delta)).astype(jnp.bfloat16)
            out = jnp.dot(score_grad, keys, preferred_element_type=f32) * scale
            out_ref[:, lanes] = out.astype(out_ref.dtype)
            both = jnp.where(lane == head, top + jnp.log(denom), both)
            both = jnp.where(lane == heads + head, delta, both)
        columns[...] = both

    stats_ref[...] = columns[...].T[: stats_ref.shape[0]]


def query_side(device, queries, out_grad, blocks, scale):
    block, width = queries.shape
    heads = width // HEAD
    return pl.pallas_call(
        functools.partial(query_kernel, scale),
        in_specs=[pl.BlockSpec(memory_space=pltpu.SMEM)] + [INSIDE] * 6,
        out_specs=[INSIDE] * 2,
        out_shape=[
            jax.ShapeDtypeStruct((block, width), jnp.bfloat16),
            jax.ShapeDtypeStruct((2 * heads, block), jnp.float32),
        ],
        scratch_shapes=[
            pltpu.VMEM((block, 4 * block), jnp.float32),
            pltpu.VMEM((block, HEAD), jnp.float32),
        ],
        compiler_params=pltpu.CompilerParams(vmem_limit_bytes=VMEM_BYTES),
        cost_estimate=pl.CostEstimate(
            flops=40 * block * block * width, bytes_accessed=24 * block * width, transcendentals=4 * block * block * heads
        ),
    )(device, queries, out_grad, *blocks)


def key_kernel(scale, last, idx_ref, both_ref, q0, q1, q2, q3, d0, d1, d2, d3, s0, s1, s2, s3, dk_ref, dv_ref, bias, lse, delta):
    block = q0.shape[0]
    heads = lse.shape[0]
    f32 = jnp.float32
    rows = lax.broadcasted_iota(jnp.int32, bias.shape, 0)
    cols = lax.broadcasted_iota(jnp.int32, bias.shape, 1)
    bias[...] = jnp.where(cols >= rows, 0.0, -jnp.inf)
    parts = [s0[...]]
    for hop, ref in enumerate((s1, s2, s3), 1):
        part = ref[...]
        row = lax.broadcasted_iota(jnp.int32, part.shape, 0)
        parts.append(jnp.where((idx_ref[0] + hop > last) & (row < heads), BIG, part))
    stats = jnp.concatenate(parts, axis=1)
    for one in range(heads):
        lse[one] = stats[one : one + 1]
        delta[one] = stats[heads + one : heads + one + 1]
    edge = bias.shape[1]

    @pl.loop(0, heads // GROUP)
    def _(step):
        for group in range(GROUP):
            head = GROUP * step + group
            lanes = pl.ds(pl.multiple_of(head * HEAD, HEAD), HEAD)
            queries = jnp.concatenate([ref[:, lanes] for ref in (q0, q1, q2, q3)], axis=0)
            dos = jnp.concatenate([ref[:, lanes] for ref in (d0, d1, d2, d3)], axis=0)
            scores = lax.dot_general(both_ref[pl.ds(0, block), lanes], queries, NT, preferred_element_type=f32) * scale - lse[head]
            scores = jnp.concatenate([scores[:, :edge] + bias[...], scores[:, edge:]], axis=1)
            probs = jnp.exp(scores)
            prob_grad = lax.dot_general(both_ref[pl.ds(block, block), lanes], dos, NT, preferred_element_type=f32)
            score_grad = (probs * (prob_grad - delta[head])).astype(jnp.bfloat16)
            dk_ref[:, lanes] = (jnp.dot(score_grad, queries, preferred_element_type=f32) * scale).astype(dk_ref.dtype)
            dv_ref[:, lanes] = jnp.dot(probs.astype(jnp.bfloat16), dos, preferred_element_type=f32).astype(dv_ref.dtype)


def key_side(device, both, queries, out_grads, stats, scale, last):
    block, width = queries[0].shape
    heads = width // HEAD
    shape = jax.ShapeDtypeStruct((block, width), jnp.bfloat16)
    return pl.pallas_call(
        functools.partial(key_kernel, scale, last),
        in_specs=[pl.BlockSpec(memory_space=pltpu.SMEM)] + [INSIDE] * 13,
        out_specs=[INSIDE] * 2,
        out_shape=[shape, shape],
        scratch_shapes=[
            pltpu.VMEM((block, 256), jnp.float32),
            pltpu.VMEM((heads, 1, 4 * block), jnp.float32),
            pltpu.VMEM((heads, 1, 4 * block), jnp.float32),
        ],
        compiler_params=pltpu.CompilerParams(vmem_limit_bytes=VMEM_BYTES),
        cost_estimate=pl.CostEstimate(
            flops=40 * block * block * width, bytes_accessed=24 * block * width, transcendentals=4 * block * block * heads
        ),
    )(device, both, *queries, *out_grads, *stats)


def per_device(queries, keys, values, stream_grad, conv_input, conv_weight, out_weight):
    block = queries.shape[0]
    last = lax.axis_size(CTX) - 1
    scale = 1.0 / math.sqrt(HEAD)
    device = lax.axis_index(CTX).astype(jnp.int32).reshape(1)
    tp = lax.axis_index("tp")

    pair = [(0, 1), (1, 0)]
    kv0, inside, across = pack(device, keys, values, conv_input, stream_grad)
    inside, across = swapped(inside, 0), swapped(across, 1)
    other = lax.ppermute(stream_grad, "tp", pair)
    (sent,) = after((kv0,), (across, other))
    kv1, q1 = rotated(sent, 1), rotated(queries, -1)
    q2 = rotated(q1, -1)
    q3 = rotated(q2, -1)

    taps_count = conv_weight.shape[0]
    padding = jnp.zeros((2 * EDGE - taps_count, conv_weight.shape[1]), conv_weight.dtype)
    edges = lax.ppermute(jnp.concatenate([inside[EDGE:], across[EDGE:], conv_weight, padding], axis=0), "tp", pair)
    grad_stream, tap_rows = conv(device, stream_grad, conv_input, inside, across, conv_weight, last)
    out_grad = project(tp, grad_stream, conv_other(device, other, edges, taps_count, last), out_weight)
    (sent,) = after((kv1,), (q1, out_grad))
    kv2 = rotated(sent, 1)
    d1 = rotated(out_grad, -1)
    (tap_rows,) = after((tap_rows,), (out_grad, q1))
    tap_sums = jnp.sum(lax.all_to_all(tap_rows, "z", 0, 0, tiled=True), axis=0)
    (sent,) = after((kv2,), (tap_sums,))
    kv3 = rotated(sent, 1)
    (sent,) = after((d1,), (kv2, q2))
    d2 = rotated(sent, -1)

    copies = jnp.broadcast_to(tap_sums, (lax.axis_size("near"),) + tap_sums.shape)
    (copies,) = after((copies,), (kv2, d1, q2))
    tap_sums = jnp.sum(lax.all_to_all(copies, "near", 0, 0, tiled=True), axis=0)
    (near,) = after((queries,), (tap_sums,))
    query_grad, stats = query_side(device, near, out_grad, (kv3, kv2, kv1, kv0), scale)
    (sent,) = after((d2,), (stats,))
    d3 = rotated(sent, -1)
    all_stats = [stats] + [rotated(stats, -hop) for hop in (1, 2, 3)]
    copies = jnp.broadcast_to(tap_sums, (lax.axis_size("z"),) + tap_sums.shape)
    (copies,) = after((copies,), (*all_stats[1:], d3))
    tap_sums = lax.all_to_all(copies, "z", 0, 0, tiled=True)
    key_grad, value_grad = key_side(device, kv0, (queries, q1, q2, q3), (out_grad, d1, d2, d3), all_stats, scale, last)
    rows = jnp.transpose(tap_sums, (1, 0, 2)).reshape(tap_sums.shape[1], -1)[:taps_count]
    kernel_grad = rows / math.sqrt(block * (last + 1))
    return (query_grad, key_grad, value_grad, grad_stream, kernel_grad)


def solution(mesh):
    count, pair = mesh.devices.shape
    far = 8
    split = Mesh(mesh.devices.reshape(far, count // far, pair), CTX + ("tp",))
    frames = P(CTX, "tp")
    return jax.shard_map(
        per_device,
        mesh=split,
        in_specs=(frames,) * 5 + (P(None, "tp"), P("tp", None)),
        out_specs=(frames,) * 4 + (P(None, "tp"),),
        check_vma=False,
    )
```

```python
import functools
import math

import jax
import jax.numpy as jnp
from jax import lax
from jax.experimental import pallas as pl
from jax.experimental.pallas import tpu as pltpu
from jax.sharding import Mesh
from jax.sharding import PartitionSpec as P

HEAD = 128
EDGE = 16
NT = (((1,), (1,)), ((), ()))
BIG = 1e30
GROUP = 4
VMEM_BYTES = 24 * 2**20
INSIDE = pl.BlockSpec(memory_space=pltpu.VMEM)
CTX = ("far", "near")


def rotated(part, by):
    count = lax.axis_size(CTX)
    return lax.ppermute(part, CTX, [(i, (i + by) % count) for i in range(count)])


def after(parts, done):
    return lax.optimization_barrier(tuple(parts) + tuple(done))[: len(parts)]


def pack_kernel(k_ref, q_ref, input_ref, grad_ref, low_ref, high_ref, sems):
    block = k_ref.shape[0]
    pairs = [
        (k_ref, low_ref.at[pl.ds(0, block)]),
        (q_ref, high_ref.at[pl.ds(0, block)]),
    ]
    for target, start in ((low_ref, block - EDGE), (high_ref, 0)):
        pairs.append((input_ref.at[pl.ds(start, EDGE)], target.at[pl.ds(block, EDGE)]))
        pairs.append((grad_ref.at[pl.ds(start, EDGE)], target.at[pl.ds(block + EDGE, EDGE)]))
    copies = [pltpu.make_async_copy(source, target, sems.at[i]) for i, (source, target) in enumerate(pairs)]
    for copy in copies:
        copy.start()
    for copy in copies:
        copy.wait()


def pack(keys, queries, inputs, grad):
    block, width = keys.shape
    shape = jax.ShapeDtypeStruct((block + 2 * EDGE, width), keys.dtype)
    return pl.pallas_call(
        pack_kernel,
        in_specs=[pl.BlockSpec(memory_space=pltpu.HBM)] * 4,
        out_specs=[INSIDE] * 2,
        out_shape=[shape, shape],
        scratch_shapes=[pltpu.SemaphoreType.DMA((6,))],
        compiler_params=pltpu.CompilerParams(vmem_limit_bytes=56 * 2**20),
    )(keys, queries, inputs, grad)


def conv_kernel(last, idx_ref, grad_ref, input_ref, low_ref, high_ref, taps_ref, out_ref, rows_ref, gpad, cpad):
    block = grad_ref.shape[0]
    width = grad_ref.shape[1]
    taps_count = taps_ref.shape[0]
    reach = taps_count // 2
    device = idx_ref[0]
    f32 = jnp.float32
    columns = width // HEAD

    @pl.loop(0, columns)
    def _(column):
        lanes = pl.ds(pl.multiple_of(column * HEAD, HEAD), HEAD)
        low = jnp.where(device > 0, low_ref[pl.ds(block, 2 * EDGE), lanes].astype(f32), 0.0)
        high = jnp.where(device < last, high_ref[pl.ds(block, 2 * EDGE), lanes].astype(f32), 0.0)
        grad = grad_ref[:, lanes].astype(f32)
        cpad[:EDGE] = low[:EDGE]
        gpad[:EDGE] = low[EDGE:]
        cpad[EDGE : EDGE + block] = input_ref[:, lanes].astype(f32)
        gpad[EDGE : EDGE + block] = grad
        cpad[EDGE + block :] = high[:EDGE]
        gpad[EDGE + block :] = high[EDGE:]
        taps = taps_ref[:, lanes].astype(f32)
        total = grad
        for tap in range(taps_count):
            total = total + taps[tap : tap + 1] * gpad[pl.ds(EDGE + reach - tap, block), :]
        out_ref[:, lanes] = total.astype(out_ref.dtype)
        grad = gpad[EDGE : EDGE + block]
        for tap in range(taps_count):
            prod = grad * cpad[pl.ds(EDGE - reach + tap, block), :]
            rows_ref[column, tap : tap + 1, :] = jnp.sum(prod, axis=0, keepdims=True)
        rows_ref[column, taps_count:, :] = jnp.zeros_like(rows_ref[column, taps_count:, :])


def conv(device, grad, inputs, low, high, taps, last):
    block, width = grad.shape
    count = taps.shape[0]
    return pl.pallas_call(
        functools.partial(conv_kernel, last),
        in_specs=[pl.BlockSpec(memory_space=pltpu.SMEM)] + [INSIDE] * 5,
        out_specs=[INSIDE] * 2,
        out_shape=[
            jax.ShapeDtypeStruct((block, width), jnp.bfloat16),
            jax.ShapeDtypeStruct((width // HEAD, 8 * pl.cdiv(count, 8), HEAD), jnp.float32),
        ],
        scratch_shapes=[
            pltpu.VMEM((block + 2 * EDGE, HEAD), jnp.float32),
            pltpu.VMEM((block + 2 * EDGE, HEAD), jnp.float32),
        ],
        compiler_params=pltpu.CompilerParams(vmem_limit_bytes=VMEM_BYTES),
        cost_estimate=pl.CostEstimate(flops=8 * block * width * count, bytes_accessed=4 * block * width, transcendentals=0),
    )(device, grad, inputs, low, high, taps)


def project(tp, own, other, weight):
    full = jnp.where(tp == 0, jnp.concatenate([own, other], axis=1), jnp.concatenate([other, own], axis=1))
    return lax.dot_general(full, weight, NT, preferred_element_type=jnp.float32).astype(jnp.bfloat16)


def query_kernel(scale, idx_ref, q_ref, do_ref, k3, k2, k1, k0, v3, v2, v1, v0, out_ref, stats_ref, bias, columns):
    block = q_ref.shape[0]
    heads = q_ref.shape[1] // HEAD
    f32 = jnp.float32
    rows = lax.broadcasted_iota(jnp.int32, bias.shape, 0)
    cols = lax.broadcasted_iota(jnp.int32, bias.shape, 1)
    valid = (cols <= 3 * block + rows) & (cols >= (3 - idx_ref[0]) * block)
    bias[...] = jnp.where(valid, 0.0, -jnp.inf)
    columns[...] = jnp.zeros_like(columns)

    @pl.loop(0, heads // GROUP)
    def _(step):
        lane = lax.broadcasted_iota(jnp.int32, columns.shape, 1)
        both = columns[...]
        for group in range(GROUP):
            head = step * GROUP + group
            lanes = pl.ds(pl.multiple_of(head * HEAD, HEAD), HEAD)
            keys = jnp.concatenate([ref[pl.ds(0, block), lanes] for ref in (k3, k2, k1, k0)], axis=0)
            values = jnp.concatenate([ref[:, lanes] for ref in (v3, v2, v1, v0)], axis=0)
            scores = lax.dot_general(q_ref[:, lanes], keys, NT, preferred_element_type=f32) * scale + bias[...]
            top = jnp.max(scores, axis=1, keepdims=True)
            expo = jnp.exp(scores - top)
            denom = jnp.sum(expo, axis=1, keepdims=True)
            probs = expo * (1.0 / denom)
            prob_grad = lax.dot_general(do_ref[:, lanes], values, NT, preferred_element_type=f32)
            delta = jnp.sum(probs.astype(jnp.bfloat16).astype(f32) * prob_grad, axis=1, keepdims=True)
            score_grad = (probs * (prob_grad - delta)).astype(jnp.bfloat16)
            out = jnp.dot(score_grad, keys, preferred_element_type=f32) * scale
            out_ref[:, lanes] = out.astype(out_ref.dtype)
            both = jnp.where(lane == head, top + jnp.log(denom), both)
            both = jnp.where(lane == heads + head, delta, both)
        columns[...] = both

    stats_ref[...] = columns[...].T[: stats_ref.shape[0]]


def query_side(device, queries, out_grad, keys, values, scale):
    block, width = queries.shape
    heads = width // HEAD
    return pl.pallas_call(
        functools.partial(query_kernel, scale),
        in_specs=[pl.BlockSpec(memory_space=pltpu.SMEM)] + [INSIDE] * 10,
        out_specs=[INSIDE] * 2,
        out_shape=[
            jax.ShapeDtypeStruct((block, width), jnp.bfloat16),
            jax.ShapeDtypeStruct((2 * heads, block), jnp.float32),
        ],
        scratch_shapes=[
            pltpu.VMEM((block, 4 * block), jnp.float32),
            pltpu.VMEM((block, HEAD), jnp.float32),
        ],
        compiler_params=pltpu.CompilerParams(vmem_limit_bytes=VMEM_BYTES),
        cost_estimate=pl.CostEstimate(
            flops=40 * block * block * width, bytes_accessed=24 * block * width, transcendentals=4 * block * block * heads
        ),
    )(device, queries, out_grad, *keys, *values)


def key_kernel(scale, last, idx_ref, k_ref, v_ref, q0, q1, q2, q3, d0, d1, d2, d3, s0, s1, s2, s3, dk_ref, dv_ref, bias, lse, delta):
    block = k_ref.shape[0]
    heads = lse.shape[0]
    f32 = jnp.float32
    rows = lax.broadcasted_iota(jnp.int32, bias.shape, 0)
    cols = lax.broadcasted_iota(jnp.int32, bias.shape, 1)
    bias[...] = jnp.where(cols >= rows, 0.0, -jnp.inf)
    parts = [s0[...]]
    for hop, ref in enumerate((s1, s2, s3), 1):
        part = ref[...]
        row = lax.broadcasted_iota(jnp.int32, part.shape, 0)
        parts.append(jnp.where((idx_ref[0] + hop > last) & (row < heads), BIG, part))
    stats = jnp.concatenate(parts, axis=1)
    for one in range(heads):
        lse[one] = stats[one : one + 1]
        delta[one] = stats[heads + one : heads + one + 1]
    edge = bias.shape[1]

    @pl.loop(0, heads // GROUP)
    def _(step):
        for group in range(GROUP):
            head = GROUP * step + group
            lanes = pl.ds(pl.multiple_of(head * HEAD, HEAD), HEAD)
            queries = jnp.concatenate([ref[pl.ds(0, block), lanes] for ref in (q0, q1, q2, q3)], axis=0)
            dos = jnp.concatenate([ref[:, lanes] for ref in (d0, d1, d2, d3)], axis=0)
            scores = lax.dot_general(k_ref[:, lanes], queries, NT, preferred_element_type=f32) * scale - lse[head]
            scores = jnp.concatenate([scores[:, :edge] + bias[...], scores[:, edge:]], axis=1)
            probs = jnp.exp(scores)
            prob_grad = lax.dot_general(v_ref[:, lanes], dos, NT, preferred_element_type=f32)
            score_grad = (probs * (prob_grad - delta[head])).astype(jnp.bfloat16)
            dk_ref[:, lanes] = (jnp.dot(score_grad, queries, preferred_element_type=f32) * scale).astype(dk_ref.dtype)
            dv_ref[:, lanes] = jnp.dot(probs.astype(jnp.bfloat16), dos, preferred_element_type=f32).astype(dv_ref.dtype)


def key_side(device, keys, values, queries, out_grads, stats, scale, last):
    block, width = keys.shape
    heads = width // HEAD
    shape = jax.ShapeDtypeStruct((block, width), jnp.bfloat16)
    return pl.pallas_call(
        functools.partial(key_kernel, scale, last),
        in_specs=[pl.BlockSpec(memory_space=pltpu.SMEM)] + [INSIDE] * 14,
        out_specs=[INSIDE] * 2,
        out_shape=[shape, shape],
        scratch_shapes=[
            pltpu.VMEM((block, 256), jnp.float32),
            pltpu.VMEM((heads, 1, 4 * block), jnp.float32),
            pltpu.VMEM((heads, 1, 4 * block), jnp.float32),
        ],
        compiler_params=pltpu.CompilerParams(vmem_limit_bytes=VMEM_BYTES),
        cost_estimate=pl.CostEstimate(
            flops=40 * block * block * width, bytes_accessed=24 * block * width, transcendentals=4 * block * block * heads
        ),
    )(device, keys, values, *queries, *out_grads, *stats)


def per_device(queries, keys, values, stream_grad, conv_input, conv_weight, out_weight):
    block = queries.shape[0]
    last = lax.axis_size(CTX) - 1
    scale = 1.0 / math.sqrt(HEAD)
    device = lax.axis_index(CTX).astype(jnp.int32).reshape(1)
    tp = lax.axis_index("tp")

    low, high = pack(keys, queries, conv_input, stream_grad)
    k1, q1 = rotated(low, 1), rotated(high, -1)
    (first,) = after((values,), (q1,))
    v1 = rotated(first, 1)
    k2, q2 = rotated(k1, 1), rotated(q1, -1)
    v2 = rotated(v1, 1)

    grad_stream, tap_rows = conv(device, stream_grad, conv_input, k1, q1, conv_weight, last)
    other = lax.ppermute(grad_stream, "tp", [(0, 1), (1, 0)])
    (tap_rows,) = after((tap_rows,), (k2,))
    tap_sums = jnp.sum(lax.all_to_all(tap_rows, "far", 0, 0, tiled=True), axis=0)
    (other,) = after((other,), (k2, q2, tap_sums))
    out_grad = project(tp, grad_stream, other, out_weight)
    k3, q3 = rotated(k2, 1), rotated(q2, -1)
    v3 = rotated(v2, 1)

    (sent,) = after((out_grad,), (v2,))
    d1 = rotated(sent, -1)
    copies = jnp.broadcast_to(tap_sums, (lax.axis_size("near"),) + tap_sums.shape)
    (copies,) = after((copies,), (v2, out_grad))
    tap_sums = jnp.sum(lax.all_to_all(copies, "near", 0, 0, tiled=True), axis=0)
    (sent,) = after((d1,), (k3, q3, tap_sums))
    d2 = rotated(sent, -1)
    (near,) = after((queries,), (tap_sums,))
    query_grad, stats = query_side(device, near, out_grad, (k3, k2, k1, keys), (v3, v2, v1, values), scale)
    (sent,) = after((d2,), (stats,))
    d3 = rotated(sent, -1)
    all_stats = [stats] + [rotated(stats, -hop) for hop in (1, 2, 3)]
    copies = jnp.broadcast_to(tap_sums, (lax.axis_size("far"),) + tap_sums.shape)
    (copies,) = after((copies,), (*all_stats[1:], d3))
    tap_sums = lax.all_to_all(copies, "far", 0, 0, tiled=True)
    key_grad, value_grad = key_side(
        device, keys, values, (queries, q1, q2, q3), (out_grad, d1, d2, d3), all_stats, scale, last
    )
    rows = jnp.transpose(tap_sums, (1, 0, 2)).reshape(tap_sums.shape[1], -1)[: conv_weight.shape[0]]
    kernel_grad = rows / math.sqrt(block * (last + 1))
    return (query_grad, key_grad, value_grad, grad_stream, kernel_grad)


def solution(mesh):
    count, pair = mesh.devices.shape
    far = 8
    split = Mesh(mesh.devices.reshape(far, count // far, pair), CTX + ("tp",))
    frames = P(CTX, "tp")
    return jax.shard_map(
        per_device,
        mesh=split,
        in_specs=(frames,) * 5 + (P(None, "tp"), P("tp", None)),
        out_specs=(frames,) * 4 + (P(None, "tp"),),
        check_vma=False,
    )
```

```python
import functools
import math

import jax
import jax.numpy as jnp
from jax import lax
from jax.experimental import pallas as pl
from jax.experimental.pallas import tpu as pltpu
from jax.sharding import Mesh
from jax.sharding import PartitionSpec as P

HEAD = 128
EDGE = 16
NT = (((1,), (1,)), ((), ()))
BIG = 1e30
GROUP = 4
VMEM_BYTES = 24 * 2**20
INSIDE = pl.BlockSpec(memory_space=pltpu.VMEM)
CTX = ("far", "near")


def rotated(part, by):
    count = lax.axis_size(CTX)
    return lax.ppermute(part, CTX, [(i, (i + by) % count) for i in range(count)])


def after(parts, done):
    return lax.optimization_barrier(tuple(parts) + tuple(done))[: len(parts)]


def pack_kernel(k_ref, q_ref, input_ref, grad_ref, low_ref, high_ref, sems):
    block = k_ref.shape[0]
    pairs = [
        (k_ref, low_ref.at[pl.ds(0, block)]),
        (q_ref, high_ref.at[pl.ds(0, block)]),
    ]
    for target, start in ((low_ref, block - EDGE), (high_ref, 0)):
        pairs.append((input_ref.at[pl.ds(start, EDGE)], target.at[pl.ds(block, EDGE)]))
        pairs.append((grad_ref.at[pl.ds(start, EDGE)], target.at[pl.ds(block + EDGE, EDGE)]))
    copies = [pltpu.make_async_copy(source, target, sems.at[i]) for i, (source, target) in enumerate(pairs)]
    for copy in copies:
        copy.start()
    for copy in copies:
        copy.wait()


def pack(keys, queries, inputs, grad):
    block, width = keys.shape
    shape = jax.ShapeDtypeStruct((block + 2 * EDGE, width), keys.dtype)
    return pl.pallas_call(
        pack_kernel,
        in_specs=[pl.BlockSpec(memory_space=pltpu.HBM)] * 4,
        out_specs=[INSIDE] * 2,
        out_shape=[shape, shape],
        scratch_shapes=[pltpu.SemaphoreType.DMA((6,))],
        compiler_params=pltpu.CompilerParams(vmem_limit_bytes=56 * 2**20),
    )(keys, queries, inputs, grad)


def conv_kernel(last, idx_ref, grad_ref, input_ref, low_ref, high_ref, taps_ref, out_ref, rows_ref, gpad, cpad):
    block = grad_ref.shape[0]
    width = grad_ref.shape[1]
    taps_count = taps_ref.shape[0]
    reach = taps_count // 2
    device = idx_ref[0]
    f32 = jnp.float32
    columns = width // HEAD

    @pl.loop(0, columns)
    def _(column):
        lanes = pl.ds(pl.multiple_of(column * HEAD, HEAD), HEAD)
        low = jnp.where(device > 0, low_ref[pl.ds(block, 2 * EDGE), lanes].astype(f32), 0.0)
        high = jnp.where(device < last, high_ref[pl.ds(block, 2 * EDGE), lanes].astype(f32), 0.0)
        grad = grad_ref[:, lanes].astype(f32)
        cpad[:EDGE] = low[:EDGE]
        gpad[:EDGE] = low[EDGE:]
        cpad[EDGE : EDGE + block] = input_ref[:, lanes].astype(f32)
        gpad[EDGE : EDGE + block] = grad
        cpad[EDGE + block :] = high[:EDGE]
        gpad[EDGE + block :] = high[EDGE:]
        taps = taps_ref[:, lanes].astype(f32)
        total = grad
        for tap in range(taps_count):
            total = total + taps[tap : tap + 1] * gpad[pl.ds(EDGE + reach - tap, block), :]
        out_ref[:, lanes] = total.astype(out_ref.dtype)
        grad = gpad[EDGE : EDGE + block]
        for tap in range(taps_count):
            prod = grad * cpad[pl.ds(EDGE - reach + tap, block), :]
            rows_ref[column, tap : tap + 1, :] = jnp.sum(prod, axis=0, keepdims=True)
        rows_ref[column, taps_count:, :] = jnp.zeros_like(rows_ref[column, taps_count:, :])


def conv(device, grad, inputs, low, high, taps, last):
    block, width = grad.shape
    count = taps.shape[0]
    return pl.pallas_call(
        functools.partial(conv_kernel, last),
        in_specs=[pl.BlockSpec(memory_space=pltpu.SMEM)] + [INSIDE] * 5,
        out_specs=[INSIDE] * 2,
        out_shape=[
            jax.ShapeDtypeStruct((block, width), jnp.bfloat16),
            jax.ShapeDtypeStruct((width // HEAD, 8 * pl.cdiv(count, 8), HEAD), jnp.float32),
        ],
        scratch_shapes=[
            pltpu.VMEM((block + 2 * EDGE, HEAD), jnp.float32),
            pltpu.VMEM((block + 2 * EDGE, HEAD), jnp.float32),
        ],
        compiler_params=pltpu.CompilerParams(vmem_limit_bytes=VMEM_BYTES),
        cost_estimate=pl.CostEstimate(flops=8 * block * width * count, bytes_accessed=4 * block * width, transcendentals=0),
    )(device, grad, inputs, low, high, taps)


def project(tp, own, other, weight):
    full = jnp.where(tp == 0, jnp.concatenate([own, other], axis=1), jnp.concatenate([other, own], axis=1))
    return lax.dot_general(full, weight, NT, preferred_element_type=jnp.float32).astype(jnp.bfloat16)


def query_kernel(scale, idx_ref, q_ref, do_ref, k3, k2, k1, k0, v3, v2, v1, v0, out_ref, stats_ref, bias, columns):
    block = q_ref.shape[0]
    heads = q_ref.shape[1] // HEAD
    f32 = jnp.float32
    rows = lax.broadcasted_iota(jnp.int32, bias.shape, 0)
    cols = lax.broadcasted_iota(jnp.int32, bias.shape, 1)
    valid = (cols <= 3 * block + rows) & (cols >= (3 - idx_ref[0]) * block)
    bias[...] = jnp.where(valid, 0.0, -jnp.inf)
    columns[...] = jnp.zeros_like(columns)

    @pl.loop(0, heads // GROUP)
    def _(step):
        lane = lax.broadcasted_iota(jnp.int32, columns.shape, 1)
        both = columns[...]
        for group in range(GROUP):
            head = step * GROUP + group
            lanes = pl.ds(pl.multiple_of(head * HEAD, HEAD), HEAD)
            keys = jnp.concatenate([ref[pl.ds(0, block), lanes] for ref in (k3, k2, k1, k0)], axis=0)
            values = jnp.concatenate([ref[:, lanes] for ref in (v3, v2, v1, v0)], axis=0)
            scores = lax.dot_general(q_ref[:, lanes], keys, NT, preferred_element_type=f32) * scale + bias[...]
            top = jnp.max(scores, axis=1, keepdims=True)
            expo = jnp.exp(scores - top)
            denom = jnp.sum(expo, axis=1, keepdims=True)
            probs = expo * (1.0 / denom)
            prob_grad = lax.dot_general(do_ref[:, lanes], values, NT, preferred_element_type=f32)
            delta = jnp.sum(probs.astype(jnp.bfloat16).astype(f32) * prob_grad, axis=1, keepdims=True)
            score_grad = (probs * (prob_grad - delta)).astype(jnp.bfloat16)
            out = jnp.dot(score_grad, keys, preferred_element_type=f32) * scale
            out_ref[:, lanes] = out.astype(out_ref.dtype)
            both = jnp.where(lane == head, top + jnp.log(denom), both)
            both = jnp.where(lane == heads + head, delta, both)
        columns[...] = both

    stats_ref[...] = columns[...].T[: stats_ref.shape[0]]


def query_side(device, queries, out_grad, keys, values, scale):
    block, width = queries.shape
    heads = width // HEAD
    return pl.pallas_call(
        functools.partial(query_kernel, scale),
        in_specs=[pl.BlockSpec(memory_space=pltpu.SMEM)] + [INSIDE] * 10,
        out_specs=[INSIDE] * 2,
        out_shape=[
            jax.ShapeDtypeStruct((block, width), jnp.bfloat16),
            jax.ShapeDtypeStruct((2 * heads, block), jnp.float32),
        ],
        scratch_shapes=[
            pltpu.VMEM((block, 4 * block), jnp.float32),
            pltpu.VMEM((block, HEAD), jnp.float32),
        ],
        compiler_params=pltpu.CompilerParams(vmem_limit_bytes=VMEM_BYTES),
        cost_estimate=pl.CostEstimate(
            flops=40 * block * block * width, bytes_accessed=24 * block * width, transcendentals=4 * block * block * heads
        ),
    )(device, queries, out_grad, *keys, *values)


def key_kernel(scale, last, idx_ref, k_ref, v_ref, q0, q1, q2, q3, d0, d1, d2, d3, s0, s1, s2, s3, dk_ref, dv_ref, bias, lse, delta):
    block = k_ref.shape[0]
    heads = lse.shape[0]
    f32 = jnp.float32
    rows = lax.broadcasted_iota(jnp.int32, bias.shape, 0)
    cols = lax.broadcasted_iota(jnp.int32, bias.shape, 1)
    bias[...] = jnp.where(cols >= rows, 0.0, -jnp.inf)
    parts = [s0[...]]
    for hop, ref in enumerate((s1, s2, s3), 1):
        part = ref[...]
        row = lax.broadcasted_iota(jnp.int32, part.shape, 0)
        parts.append(jnp.where((idx_ref[0] + hop > last) & (row < heads), BIG, part))
    stats = jnp.concatenate(parts, axis=1)
    for one in range(heads):
        lse[one] = stats[one : one + 1]
        delta[one] = stats[heads + one : heads + one + 1]
    edge = bias.shape[1]

    @pl.loop(0, heads // GROUP)
    def _(step):
        for group in range(GROUP):
            head = GROUP * step + group
            lanes = pl.ds(pl.multiple_of(head * HEAD, HEAD), HEAD)
            queries = jnp.concatenate([ref[pl.ds(0, block), lanes] for ref in (q0, q1, q2, q3)], axis=0)
            dos = jnp.concatenate([ref[:, lanes] for ref in (d0, d1, d2, d3)], axis=0)
            scores = lax.dot_general(k_ref[:, lanes], queries, NT, preferred_element_type=f32) * scale - lse[head]
            scores = jnp.concatenate([scores[:, :edge] + bias[...], scores[:, edge:]], axis=1)
            probs = jnp.exp(scores)
            prob_grad = lax.dot_general(v_ref[:, lanes], dos, NT, preferred_element_type=f32)
            score_grad = (probs * (prob_grad - delta[head])).astype(jnp.bfloat16)
            dk_ref[:, lanes] = (jnp.dot(score_grad, queries, preferred_element_type=f32) * scale).astype(dk_ref.dtype)
            dv_ref[:, lanes] = jnp.dot(probs.astype(jnp.bfloat16), dos, preferred_element_type=f32).astype(dv_ref.dtype)


def key_side(device, keys, values, queries, out_grads, stats, scale, last):
    block, width = keys.shape
    heads = width // HEAD
    shape = jax.ShapeDtypeStruct((block, width), jnp.bfloat16)
    return pl.pallas_call(
        functools.partial(key_kernel, scale, last),
        in_specs=[pl.BlockSpec(memory_space=pltpu.SMEM)] + [INSIDE] * 14,
        out_specs=[INSIDE] * 2,
        out_shape=[shape, shape],
        scratch_shapes=[
            pltpu.VMEM((block, 256), jnp.float32),
            pltpu.VMEM((heads, 1, 4 * block), jnp.float32),
            pltpu.VMEM((heads, 1, 4 * block), jnp.float32),
        ],
        compiler_params=pltpu.CompilerParams(vmem_limit_bytes=VMEM_BYTES),
        cost_estimate=pl.CostEstimate(
            flops=40 * block * block * width, bytes_accessed=24 * block * width, transcendentals=4 * block * block * heads
        ),
    )(device, keys, values, *queries, *out_grads, *stats)


def per_device(queries, keys, values, stream_grad, conv_input, conv_weight, out_weight):
    block = queries.shape[0]
    last = lax.axis_size(CTX) - 1
    scale = 1.0 / math.sqrt(HEAD)
    device = lax.axis_index(CTX).astype(jnp.int32).reshape(1)
    tp = lax.axis_index("tp")

    low, high = pack(keys, queries, conv_input, stream_grad)
    k1, q1 = rotated(low, 1), rotated(high, -1)
    (first,) = after((values,), (q1,))
    v1 = rotated(first, 1)
    k2, q2 = rotated(k1, 1), rotated(q1, -1)
    v2 = rotated(v1, 1)

    grad_stream, tap_rows = conv(device, stream_grad, conv_input, k1, q1, conv_weight, last)
    other = lax.ppermute(grad_stream, "tp", [(0, 1), (1, 0)])
    (tap_rows,) = after((tap_rows,), (k2,))
    tap_sums = jnp.sum(lax.all_to_all(tap_rows, "far", 0, 0, tiled=True), axis=0)
    (other,) = after((other,), (k2, q2, tap_sums))
    out_grad = project(tp, grad_stream, other, out_weight)
    k3, q3 = rotated(k2, 1), rotated(q2, -1)
    v3 = rotated(v2, 1)

    (sent,) = after((out_grad,), (v2,))
    d1 = rotated(sent, -1)
    copies = jnp.broadcast_to(tap_sums, (lax.axis_size("near"),) + tap_sums.shape)
    (copies,) = after((copies,), (v2, out_grad))
    tap_sums = jnp.sum(lax.all_to_all(copies, "near", 0, 0, tiled=True), axis=0)
    (sent,) = after((d1,), (k3, q3, tap_sums))
    d2 = rotated(sent, -1)
    (near,) = after((queries,), (tap_sums,))
    query_grad, stats = query_side(device, near, out_grad, (k3, k2, k1, keys), (v3, v2, v1, values), scale)
    (sent,) = after((d2,), (stats,))
    d3 = rotated(sent, -1)
    copies = jnp.broadcast_to(tap_sums, (lax.axis_size("far"),) + tap_sums.shape)
    (copies,) = after((copies,), (d1,))
    tap_sums = lax.all_to_all(copies, "far", 0, 0, tiled=True)
    (stats,) = after((stats,), (tap_sums,))
    all_stats = [stats] + [rotated(stats, -hop) for hop in (1, 2, 3)]
    key_grad, value_grad = key_side(
        device, keys, values, (queries, q1, q2, q3), (out_grad, d1, d2, d3), all_stats, scale, last
    )
    rows = jnp.transpose(tap_sums, (1, 0, 2)).reshape(tap_sums.shape[1], -1)[: conv_weight.shape[0]]
    kernel_grad = rows / math.sqrt(block * (last + 1))
    return (query_grad, key_grad, value_grad, grad_stream, kernel_grad)


def solution(mesh):
    count, pair = mesh.devices.shape
    far = 8
    split = Mesh(mesh.devices.reshape(far, count // far, pair), CTX + ("tp",))
    frames = P(CTX, "tp")
    return jax.shard_map(
        per_device,
        mesh=split,
        in_specs=(frames,) * 5 + (P(None, "tp"), P("tp", None)),
        out_specs=(frames,) * 4 + (P(None, "tp"),),
        check_vma=False,
    )
```
